32 devices in a mesh: dp: 4 (over x, core), group: 4 (over z), tensor: 2 (over y).
Axes of the slice: x: 2, y: 2, z: 4, core: 2. Of those that a mesh axis runs over, the one named last changes fastest.
Arguments:
- tokens: bfloat16 [4096, 2560], P(('dp', 'group')), may hold values from -6 to 6
- cotangent: float32 [4096, 2560], P(('dp', 'group')), may hold values from -6 to 6
- doc_lengths: int32 [1, 4], replicated, may hold values from 1 to 3072, 4096 in all within a row
- w_query: float32 [2560, 2560], P(('dp', 'group'), 'tensor'), may hold values from -0.125 to 0.125
- w_keyvalue: float32 [2560, 512], P(('dp', 'group')), may hold values from -0.125 to 0.125
- w_out: float32 [2560, 2560], P(('dp', 'group'), 'tensor'), may hold values from -1 to 1
- w_gate: float32 [2560, 7680], P(('dp', 'group'), 'tensor'), may hold values from -0.125 to 0.125
- w_up: float32 [2560, 7680], P(('dp', 'group'), 'tensor'), may hold values from -0.125 to 0.125
- w_down: float32 [2560, 7680], P(('dp', 'group'), 'tensor'), may hold values from -0.125 to 0.125
- norm_gains: float32 [2, 2560], P(None, ('dp', 'group')), may hold values from 0.5 to 1.5
- first_query: float32 [2560, 2560], P(('dp', 'group'), 'tensor'), may hold values from -40 to 40
- first_keyvalue: float32 [2560, 512], P(('dp', 'group')), may hold values from -128 to 128
- first_out: float32 [2560, 2560], P(('dp', 'group'), 'tensor'), may hold values from -4 to 4
- first_gate: float32 [2560, 7680], P(('dp', 'group'), 'tensor'), may hold values from -20 to 20
- first_up: float32 [2560, 7680], P(('dp', 'group'), 'tensor'), may hold values from -20 to 20
- first_down: float32 [2560, 7680], P(('dp', 'group'), 'tensor'), may hold values from -24 to 24
- first_gains: float32 [2, 2560], P(None, ('dp', 'group')), may hold values from -80 to 80
- second_query: float32 [2560, 2560], P(('dp', 'group'), 'tensor'), may hold values from 204.8 to 819.2
- second_keyvalue: float32 [2560, 512], P(('dp', 'group')), may hold values from 1843.2 to 7372.8
- second_out: float32 [2560, 2560], P(('dp', 'group'), 'tensor'), may hold values from 2.048 to 8.192
- second_gate: float32 [2560, 7680], P(('dp', 'group'), 'tensor'), may hold values from 51.2 to 204.8
- second_up: float32 [2560, 7680], P(('dp', 'group'), 'tensor'), may hold values from 51.2 to 204.8
- second_down: float32 [2560, 7680], P(('dp', 'group'), 'tensor'), may hold values from 73.728 to 294.912
- second_gains: float32 [2, 2560], P(None, ('dp', 'group')), may hold values from 819.2 to 3276.8
Outputs:
- mixed: float32 [4096, 2560], P(('dp', 'group'))
- token_grad: float32 [4096, 2560], P(('dp', 'group'))
- next_first_query: float32 [2560, 2560], P(('dp', 'group'), 'tensor')
- next_first_keyvalue: float32 [2560, 512], P(('dp', 'group'))
- next_first_out: float32 [2560, 2560], P(('dp', 'group'), 'tensor')
- next_first_gate: float32 [2560, 7680], P(('dp', 'group'), 'tensor')
- next_first_up: float32 [2560, 7680], P(('dp', 'group'), 'tensor')
- next_first_down: float32 [2560, 7680], P(('dp', 'group'), 'tensor')
- next_first_gains: float32 [2, 2560], P(None, ('dp', 'group'))
- next_second_query: float32 [2560, 2560], P(('dp', 'group'), 'tensor')
- next_second_keyvalue: float32 [2560, 512], P(('dp', 'group'))
- next_second_out: float32 [2560, 2560], P(('dp', 'group'), 'tensor')
- next_second_gate: float32 [2560, 7680], P(('dp', 'group'), 'tensor')
- next_second_up: float32 [2560, 7680], P(('dp', 'group'), 'tensor')
- next_second_down: float32 [2560, 7680], P(('dp', 'group'), 'tensor')
- next_second_gains: float32 [2, 2560], P(None, ('dp', 'group'))
- updated_query: float32 [2560, 2560], P(('dp', 'group'), 'tensor')
- updated_keyvalue: float32 [2560, 512], P(('dp', 'group'))
- updated_out: float32 [2560, 2560], P(('dp', 'group'), 'tensor')
- updated_gate: float32 [2560, 7680], P(('dp', 'group'), 'tensor')
- updated_up: float32 [2560, 7680], P(('dp', 'group'), 'tensor')
- updated_down: float32 [2560, 7680], P(('dp', 'group'), 'tensor')
- updated_gains: float32 [2, 2560], P(None, ('dp', 'group'))
The draws below stay inside these ranges and needn't reach their ends.
Inputs may be any that keep to these rules, and one draw needn't show every extreme that they name: `doc_lengths`: row s lists the lengths of the 4 documents of sequence s in order; each row sums to 4096, and its largest entry is exactly 3072, longer than the window.
All inputs are finite; a program needn't handle non-finite values.
Results may differ from the reference program's by a relative error of at most 0.017.
Values may be sent and summed in bfloat16 or wider, within the bound.
A program may use at most 384 MiB of HBM per device.

```python
import math
import jax
import jax.numpy as jnp
import numpy as np
from jax import lax

D = 2560
H = 10
HD = 256
FF = 7680
WINDOW = 2048
SEQ_LEN = 4096
DOCS = 4
LONGEST = 3072
STEP = 10
TOKENS = 4096
SEQS = 1


def spiked(entries, key, source, target, parts, factor):
    def block_of(axis_at):
        return (jnp.arange(entries.shape[axis_at]) // (entries.shape[axis_at] // parts)).reshape((-1,) + (1,) * (entries.ndim - 1 - axis_at))

    one_side = jax.random.permutation(key, parts)[block_of(target)]
    far = (block_of(target) + parts // 2) % parts
    return jnp.where((block_of(source) == one_side) | (block_of(source) == far), factor * entries, entries)


def level_of(stream_key, shape, shards, low, top_value):
    loudness, own = 1.0, jax.random.fold_in(stream_key, 6)
    for axis_at, blocks in shards:
        heights = jnp.exp(jax.random.uniform(jax.random.fold_in(own, axis_at), (blocks,), jnp.float32, low / len(shards), top_value / len(shards)))
        loudness = loudness * jnp.repeat(heights, shape[axis_at] // blocks).reshape([-1 if axis == axis_at else 1 for axis in range(len(shape))])
    return loudness


def split_up(amount, total, limit, skew):
    loads = [(1 << 20) // math.isqrt(rank ** skew) + 1 for rank in range(2, amount + 1)]
    surplus, given = total - limit - (amount - 1), [1] * (amount - 1)
    while surplus > 0:
        free = [i for i in range(amount - 1) if given[i] < limit]
        pool, budget = sum([loads[i] for i in free]), surplus
        for i in free:
            extra = min(limit - given[i], max(1, budget * loads[i] // pool), surplus)
            given[i] = given[i] + extra
            surplus = surplus - extra
    return np.array([limit] + given)


def ragged(stream_key, number_of, total, most, slope):
    if number_of == 2:
        one = jax.random.randint(stream_key, (), max(1, total - most), min(most, total - 1) + 1)
        return jnp.stack([one, total - one])
    sizes = jnp.asarray(split_up(number_of, total, most, slope), jnp.int32)
    twos = (number_of - 1) // 2
    giver, taker = sizes[1:1 + 2 * twos:2], sizes[2:2 + 2 * twos:2]
    slack = jnp.minimum(giver - 1, most - taker)
    shifted = jax.random.randint(jax.random.fold_in(stream_key, 1), (twos,), 0, 1 << 20) % (slack + 1)
    sizes = sizes.at[1:1 + 2 * twos:2].set(giver - shifted).at[2:2 + 2 * twos:2].set(taker + shifted)
    return sizes[jax.random.permutation(jax.random.fold_in(stream_key, 2), number_of)]


def bell_draw(own_key, dims, spread, limit, shards=(), kind=jnp.bfloat16):
    drawn = jax.random.normal(own_key, dims, jnp.float32) * spread
    if len(shards) > 0:
        drawn = level_of(own_key, dims, shards, -0.22, 0.18) * drawn
    return jnp.clip(drawn, min=-limit, max=limit).astype(kind)


def bell_draw_with(own_key, shape, scale, bound, split, heavy, kind=jnp.bfloat16):
    entries = scale * jax.random.normal(own_key, shape, jnp.float32)
    if split:
        entries = entries * level_of(own_key, shape, split, -0.22, 0.18)
    return jnp.clip(spiked(entries, jax.random.fold_in(own_key, 3), *heavy), -bound, bound).astype(kind)


def setup_inputs(seed: int = 0) -> dict:
    splits = jax.random.split(jax.random.key(seed), 25)
    return {
        "tokens": bell_draw(splits[0], (TOKENS, D), 1.0, 6.0, ((0, 16),)),
        "cotangent": bell_draw_with(splits[1], (TOKENS, D), 1.0, 6.0, ((0, 16),), (0, 1, 16, 2.0), jnp.float32),
        "doc_lengths": jax.vmap(lambda own: ragged(own, DOCS, SEQ_LEN, LONGEST, 1))(jax.random.split(splits[2], SEQS)).reshape((SEQS, DOCS)).astype(jnp.int32),
        "w_query": bell_draw(splits[3], (D, H * HD), D ** -0.5, 0.125, ((0, 16), (1, 2)), jnp.float32),
        "w_keyvalue": bell_draw(splits[4], (D, 2 * HD), D ** -0.5, 0.125, ((0, 16),), jnp.float32),
        "w_out": bell_draw(splits[5], (D, H * HD), (max(1, H * HD // 64)) ** -0.5, 1.0, ((0, 16), (1, 2)), jnp.float32),
        "w_gate": bell_draw(splits[6], (D, FF), D ** -0.5, 0.125, ((0, 16), (1, 2)), jnp.float32),
        "w_up": bell_draw(splits[7], (D, FF), D ** -0.5, 0.125, ((0, 16), (1, 2)), jnp.float32),
        "w_down": bell_draw(splits[8], (D, FF), D ** -0.5, 0.125, ((0, 16), (1, 2)), jnp.float32),
        "norm_gains": jnp.clip(1.0 + 0.1 * jax.random.normal(splits[9], (2, D), jnp.float32), 0.5, 1.5),
        "first_query": bell_draw(splits[10], (D, H * HD), (0.11 * TOKENS ** 0.5), 40.0, ((0, 16), (1, 2)), jnp.float32),
        "first_keyvalue": bell_draw(splits[11], (D, 2 * HD), (0.33 * TOKENS ** 0.5), 128.0, ((0, 16),), jnp.float32),
        "first_out": bell_draw(splits[12], (D, H * HD), (0.011 * TOKENS ** 0.5), 4.0, ((0, 16), (1, 2)), jnp.float32),
        "first_gate": bell_draw(splits[13], (D, FF), (0.055 * TOKENS ** 0.5), 20.0, ((0, 16), (1, 2)), jnp.float32),
        "first_up": bell_draw(splits[14], (D, FF), (0.055 * TOKENS ** 0.5), 20.0, ((0, 16), (1, 2)), jnp.float32),
        "first_down": bell_draw(splits[15], (D, FF), (0.066 * TOKENS ** 0.5), 24.0, ((0, 16), (1, 2)), jnp.float32),
        "first_gains": bell_draw(splits[16], (2, D), (0.22 * TOKENS ** 0.5), 80.0, ((1, 16),), jnp.float32),
        "second_query": jnp.clip(jnp.exp(math.log(819.2) - 1.3862944 * jax.random.uniform(splits[17], (D, H * HD), jnp.float32) ** level_of(splits[17], (D, H * HD), ((0, 16), (1, 2)), -0.2, 0.2)), 204.8, 819.2),
        "second_keyvalue": jnp.clip(jnp.exp(math.log(7372.8) - 1.3862944 * jax.random.uniform(splits[18], (D, 2 * HD), jnp.float32) ** level_of(splits[18], (D, 2 * HD), ((0, 16),), -0.2, 0.2)), 1843.2, 7372.8),
        "second_out": jnp.clip(jnp.exp(math.log(8.192) - 1.3862944 * jax.random.uniform(splits[19], (D, H * HD), jnp.float32) ** level_of(splits[19], (D, H * HD), ((0, 16), (1, 2)), -0.2, 0.2)), 2.048, 8.192),
        "second_gate": jnp.clip(jnp.exp(math.log(204.8) - 1.3862944 * jax.random.uniform(splits[20], (D, FF), jnp.float32) ** level_of(splits[20], (D, FF), ((0, 16), (1, 2)), -0.2, 0.2)), 51.2, 204.8),
        "second_up": jnp.clip(jnp.exp(math.log(204.8) - 1.3862944 * jax.random.uniform(splits[21], (D, FF), jnp.float32) ** level_of(splits[21], (D, FF), ((0, 16), (1, 2)), -0.2, 0.2)), 51.2, 204.8),
        "second_down": jnp.clip(jnp.exp(math.log(294.912) - 1.3862944 * jax.random.uniform(splits[22], (D, FF), jnp.float32) ** level_of(splits[22], (D, FF), ((0, 16), (1, 2)), -0.2, 0.2)), 73.728, 294.912),
        "second_gains": jnp.clip(jnp.exp(math.log(3276.8) - 1.3862944 * jax.random.uniform(splits[23], (2, D), jnp.float32) ** level_of(splits[23], (2, D), ((1, 16),), -0.2, 0.2)), 819.2, 3276.8),
    }


EPSILON = 1e-06
BETA_ONE = 0.9
BETA_TWO = 0.95
ADAM_EPS = 1e-08
DECAY = 0.1

@jax.custom_vjp
def low(v):
    return lax.optimization_barrier(v.astype(jnp.bfloat16)).astype(jnp.float32)

@jax.custom_vjp
def low_back(v):
    return v

def low_keep(v):
    return (low(v), None)

def low_pass(kept, grad):
    return (grad,)

def back_keep(v):
    return (v, None)

def back_low(kept, grad):
    return (low(grad),)
low.defvjp(low_keep, low_pass)
low_back.defvjp(back_keep, back_low)

def rms_norm(values, gain_row):
    inverse = lax.rsqrt(lax.optimization_barrier(jnp.mean(values * values, axis=-1, keepdims=True)) + EPSILON)
    return values * inverse * gain_row

def rope_tables(positions):
    quarter = HD // 4
    freqs = jnp.exp(-math.log(10000.0) * jnp.arange(quarter, dtype=jnp.float32) * 2.0 / (HD // 2))
    angles = positions.astype(jnp.float32)[:, None] * freqs[None, :]
    return (jnp.cos(angles), jnp.sin(angles))

def rotate(values, cosine_table, sine_table):
    quarter = cosine_table.shape[1]
    lead_part = values[..., :quarter]
    pair_part = values[..., quarter:2 * quarter]
    tail_part = values[..., 2 * quarter:]
    cos_wide = cosine_table[:, None, :]
    sin_wide = sine_table[:, None, :]
    return jnp.concatenate([lead_part * cos_wide - pair_part * sin_wide, pair_part * cos_wide + lead_part * sin_wide, tail_part], axis=-1)

def attend(query_rot, keys, values, segments):
    length = query_rot.shape[0]
    block = math.gcd(512, length)
    padded_keys = jnp.pad(keys, ((WINDOW, 0), (0, 0)))
    padded_values = jnp.pad(values, ((WINDOW, 0), (0, 0)))
    padded_segments = jnp.pad(segments, (WINDOW, 0), constant_values=-1)

    def one_block(start):
        queries = lax.dynamic_slice_in_dim(query_rot, start, block, 0)
        key_part = lax.dynamic_slice_in_dim(padded_keys, start, block + WINDOW, 0)
        value_part = lax.dynamic_slice_in_dim(padded_values, start, block + WINDOW, 0)
        query_seg = lax.dynamic_slice_in_dim(segments, start, block, 0)
        key_seg = lax.dynamic_slice_in_dim(padded_segments, start, block + WINDOW, 0)
        query_pos = start + jnp.arange(block, dtype=jnp.int32)
        key_pos = start - WINDOW + jnp.arange(block + WINDOW, dtype=jnp.int32)
        allowed = (query_seg[:, None] == key_seg[None, :]) & (key_pos[None, :] <= query_pos[:, None]) & (query_pos[:, None] - key_pos[None, :] < WINDOW)
        scores = low_back(jnp.einsum('qhd,kd->hqk', queries, key_part, precision=lax.Precision.HIGHEST))
        scores = jnp.where(allowed[None], scores, -jnp.inf)
        row_top = lax.optimization_barrier(jnp.max(scores, axis=-1, keepdims=True))
        exp_scores = jnp.exp(scores - row_top)
        prob_table = exp_scores / lax.optimization_barrier(jnp.sum(exp_scores, axis=-1, keepdims=True))
        return jnp.einsum('hqk,kd->qhd', low(prob_table), value_part, precision=lax.Precision.HIGHEST)
    starts = jnp.arange(0, length, block, dtype=jnp.int32)
    outputs = lax.map(jax.checkpoint(one_block), starts)
    return outputs.reshape(length, query_rot.shape[1], HD)

def block_forward(seq_tokens, query_weight, keyvalue_weight, out_weight, gate_weight, up_weight, down_weight, gain_weights, segments):
    length = seq_tokens.shape[0]
    head_count = query_weight.shape[1] // HD
    highest = lax.Precision.HIGHEST
    gains_low = low(gain_weights)
    normed_first = low(rms_norm(seq_tokens, gains_low[0]))
    query_raw = low_back(jnp.dot(normed_first, low(query_weight), precision=highest))
    keyvalue_raw = low_back(jnp.dot(normed_first, low(keyvalue_weight), precision=highest))
    cosine_table, sine_table = rope_tables(jnp.arange(length, dtype=jnp.int32))
    query_rot = low(rotate(query_raw.reshape(length, head_count, HD), cosine_table, sine_table) * HD ** (-0.5))
    keys = low(rotate(keyvalue_raw[:, None, :HD], cosine_table, sine_table)[:, 0])
    values = low(keyvalue_raw[:, HD:])
    attended = low(low_back(attend(query_rot, keys, values, segments).reshape(length, head_count * HD)))
    attention_out = low_back(jnp.dot(attended, low(out_weight).T, precision=highest))
    middle = seq_tokens + attention_out
    normed_second = low(rms_norm(middle, gains_low[1]))
    gate_pre = low_back(jnp.dot(normed_second, low(gate_weight), precision=highest))
    up_pre = low_back(jnp.dot(normed_second, low(up_weight), precision=highest))
    hidden = low(jax.nn.gelu(gate_pre) * up_pre)
    feed_out = low_back(jnp.dot(hidden, low(down_weight).T, precision=highest))
    return middle + feed_out

def adam_update(weight, moment_old, square_old, gradient, rate_step, decay_rate):
    moment_new = BETA_ONE * moment_old + (1.0 - BETA_ONE) * gradient
    square_new = BETA_TWO * square_old + (1.0 - BETA_TWO) * gradient * gradient
    corrected = moment_new / (1.0 - BETA_ONE ** STEP)
    corrected_square = square_new / (1.0 - BETA_TWO ** STEP)
    weight_new = weight - rate_step * (corrected / (jnp.sqrt(corrected_square) + ADAM_EPS) + decay_rate * weight)
    return (moment_new, square_new, weight_new)

def reference(tokens, cotangent, doc_lengths, w_query, w_keyvalue, w_out, w_gate, w_up, w_down, norm_gains, first_query, first_keyvalue, first_out, first_gate, first_up, first_down, first_gains, second_query, second_keyvalue, second_out, second_gate, second_up, second_down, second_gains):
    weights = (w_query, w_keyvalue, w_out, w_gate, w_up, w_down, norm_gains)
    firsts = (first_query, first_keyvalue, first_out, first_gate, first_up, first_down, first_gains)
    seconds = (second_query, second_keyvalue, second_out, second_gate, second_up, second_down, second_gains)
    tokens_seq = tokens.astype(jnp.float32).reshape(SEQS, SEQ_LEN, D)
    cotangent_seq = cotangent.reshape(SEQS, SEQ_LEN, D)
    positions = jnp.arange(SEQ_LEN, dtype=jnp.int32)
    doc_ends = jnp.cumsum(doc_lengths, axis=1).astype(jnp.int32)
    segments_all = lax.optimization_barrier(jnp.sum((doc_ends[:, None, :] <= positions[None, :, None]).astype(jnp.int32), axis=2)).astype(jnp.int32)

    def one_sequence(totals, inputs):
        seq_tokens, seq_cotangent, seq_segments = inputs

        def run_block(tok_arg, query_weight, keyvalue_weight, out_weight, gate_weight, up_weight, down_weight, gain_weights):
            return block_forward(tok_arg, query_weight, keyvalue_weight, out_weight, gate_weight, up_weight, down_weight, gain_weights, seq_segments)
        output, pullback = jax.vjp(run_block, seq_tokens, w_query, w_keyvalue, w_out, w_gate, w_up, w_down, norm_gains)
        grads = pullback(seq_cotangent)
        totals = tuple((total_now + grad_now for total_now, grad_now in zip(totals, grads[1:])))
        return (totals, (output, grads[0]))
    zeros = tuple((jnp.zeros(weight.shape, jnp.float32) for weight in weights))
    totals, (outputs, token_grads) = lax.scan(one_sequence, zeros, (tokens_seq, cotangent_seq, segments_all))
    dense_rate = 2.0 * D ** (-0.5)
    out_rate = 2.0 * max(1, H * HD // 64) ** (-0.5)
    rates = (dense_rate, dense_rate, out_rate, dense_rate, dense_rate, dense_rate, 0.4)
    decays = (DECAY, DECAY, DECAY, DECAY, DECAY, DECAY, 0.0)
    new_firsts = []
    new_seconds = []
    updated = []
    for weight, moment_old, square_old, gradient, rate_step, decay_rate in zip(weights, firsts, seconds, totals, rates, decays):
        moment_new, square_new, weight_new = adam_update(weight, moment_old, square_old, gradient, rate_step, decay_rate)
        new_firsts.append(moment_new)
        new_seconds.append(square_new)
        updated.append(weight_new)
    mixed = outputs.reshape(TOKENS, D)
    token_grad = token_grads.reshape(TOKENS, D)
    return (mixed, token_grad, new_firsts[0], new_firsts[1], new_firsts[2], new_firsts[3], new_firsts[4], new_firsts[5], new_firsts[6], new_seconds[0], new_seconds[1], new_seconds[2], new_seconds[3], new_seconds[4], new_seconds[5], new_seconds[6], updated[0], updated[1], updated[2], updated[3], updated[4], updated[5], updated[6])
```

```python
import functools
import math

import jax
import jax.numpy as jnp
from jax import lax
from jax.experimental import pallas as pl
from jax.experimental.pallas import tpu as pltpu
from jax.sharding import Mesh
from jax.sharding import PartitionSpec as P

D = 2560
H = 10
HD = 256
WINDOW = 2048
SEQ_LEN = 4096
STEP = 10

EPSILON = 1e-06
BETA_ONE = 0.9
BETA_TWO = 0.95
ADAM_EPS = 1e-08
DECAY = 0.1
CONTRACT_LAST = (((1,), (1,)), ((), ()))
CONTRACT_FIRST = (((0,), (0,)), ((), ()))
BF16 = jnp.bfloat16
F32 = jnp.float32
AXES = ("x", "c", "z", "y")


class Blank:
    @property
    def at(self):
        return self

    def __getitem__(self, _):
        return self

    def landed(self):
        pass


class Copy:
    def __init__(self, copy):
        self.copy, self.arrived = copy, False

    def landed(self):
        if not self.arrived:
            self.copy.wait_recv()
            self.arrived = True


class Net:
    def __init__(self, sizes, me, sems):
        self.sizes, self.me, self.sems = sizes, me, sems
        self.sent, self.kept, self.peers, self.open = 0, 0, [], []

    def device(self, where):
        s, me = self.sizes, self.me
        if len(where) == 4:
            return {a: lax.rem(me[a] + d, s[a]) for a, d in zip(AXES, where)}
        flat = lax.rem((me["x"] * s["c"] + me["c"]) * s["z"] + me["z"] + where[0], s["n"])
        return {
            "x": flat // (s["c"] * s["z"]),
            "c": lax.rem(flat // s["z"], s["c"]),
            "z": lax.rem(flat, s["z"]),
            "y": lax.rem(me["y"] + where[1], s["y"]),
        }

    def opposite(self, where):
        if len(where) == 4:
            return tuple((self.sizes[a] - d) % self.sizes[a] for a, d in zip(AXES, where))
        return ((self.sizes["n"] - where[0]) % self.sizes["n"], (self.sizes["y"] - where[1]) % self.sizes["y"])

    def send(self, src, dst, where):
        k = self.sent
        self.sent += 1
        if self.sems is None:
            for w in (where, self.opposite(where)):
                if w not in self.peers:
                    self.peers.append(w)
            return Blank()
        copy = pltpu.make_async_remote_copy(
            src_ref=src,
            dst_ref=dst,
            send_sem=self.sems[0].at[k],
            recv_sem=self.sems[1].at[k],
            device_id=self.device(where),
            device_id_type=pl.DeviceIdType.MESH,
        )
        copy.start()
        self.open.append(Copy(copy))
        return self.open[-1]

    def keep(self, src, dst):
        k = self.kept
        self.kept += 1
        if self.sems is None:
            return
        copy = pltpu.make_async_copy(src, dst, self.sems[2].at[k])
        copy.start()
        self.open.append(copy)

    def greet(self, peers):
        barrier = pltpu.get_barrier_semaphore()
        for where in peers:
            pl.semaphore_signal(
                barrier, inc=1, device_id=self.device(where), device_id_type=pl.DeviceIdType.MESH
            )
        pl.semaphore_wait(barrier, len(peers))

    def finish(self):
        for item in self.open:
            if isinstance(item, Copy):
                item.landed()
                item.copy.wait_send()
            else:
                item.wait()


def exchange(plan, arrays, outs, sizes, number):
    count = Net(sizes, {a: 0 for a in AXES}, None)
    plan(count, *[Blank()] * (len(arrays) + len(outs)))

    def kernel(*refs):
        data, sems = refs[:-3], refs[-3:]
        net = Net(sizes, {a: lax.axis_index(a) for a in AXES}, sems)
        net.greet(count.peers)
        plan(net, *data)
        net.finish()

    anywhere = pl.BlockSpec(memory_space=pl.ANY)
    return pl.pallas_call(
        kernel,
        out_shape=[jax.ShapeDtypeStruct(shape, dtype) for shape, dtype in outs],
        in_specs=[anywhere] * len(arrays),
        out_specs=[anywhere] * len(outs),
        scratch_shapes=[
            pltpu.SemaphoreType.DMA((count.sent,)),
            pltpu.SemaphoreType.DMA((count.sent,)),
            pltpu.SemaphoreType.DMA((max(1, count.kept),)),
        ],
        compiler_params=pltpu.CompilerParams(collective_id=number, has_side_effects=True),
    )(*arrays)


ZERO = (0, 0, 0, 0)
SIBLING = (0, 1, 0, 0)
OTHER_Y = (0, 0, 0, 1)


def spread_z_x_c(net, pairs):
    x, c, z = (net.me[a] for a in "xcz")
    first = []
    for src, dst in pairs:
        first.append([net.send(src, dst.at[x, c, z], (0, 0, dz, 0)) for dz in range(1, net.sizes["z"])])
    return first


def own_to_x_c(net, pairs):
    x, c, z = (net.me[a] for a in "xcz")
    across = []
    for src, dst in pairs:
        net.keep(src, dst.at[x, c, z])
        net.send(src, dst.at[x, c, z], SIBLING)
        for dx in range(1, net.sizes["x"]):
            across.append((net.send(src, dst.at[x, c, z], (dx, 0, 0, 0)), dst, dx, 0))
    return across


def forward_z(net, pairs, first, across):
    x, c, z = (net.me[a] for a in "xcz")
    for dz in range(1, net.sizes["z"]):
        for (_, dst), copies in zip(pairs, first):
            copies[dz - 1].landed()
            slot = dst.at[x, c, lax.rem(z + net.sizes["z"] - dz, net.sizes["z"])]
            for dx in range(1, net.sizes["x"]):
                across.append((net.send(slot, slot, (dx, 0, 0, 0)), dst, dx, dz))
            net.send(slot, slot, SIBLING)


def forward_x(net, across):
    x, c, z = (net.me[a] for a in "xcz")
    for copy, dst, dx, dz in across:
        copy.landed()
        slot = dst.at[
            lax.rem(x + net.sizes["x"] - dx, net.sizes["x"]),
            c,
            lax.rem(z + net.sizes["z"] - dz, net.sizes["z"]),
        ]
        net.send(slot, slot, SIBLING)


def gather_weights(net, *refs):
    x, c, z, y = (net.me[a] for a in AXES)
    sizes = net.sizes
    attention = list(zip(refs[0:4], refs[7:11]))
    mlp = list(zip(refs[4:7], refs[11:14]))

    def scatter(src, dst):
        got = []
        for dz in range(sizes["z"]):
            for dc in range(sizes["c"]):
                if dz or dc:
                    piece = lax.rem(c + dc, sizes["c"]) * sizes["z"] + lax.rem(z + dz, sizes["z"])
                    got.append((net.send(src.at[piece], dst.at[y, x, c, z], (0, dc, dz, 0)), dc, dz))
        return got

    def spread(src, dst, got):
        own, slot = src.at[c * sizes["z"] + z], dst.at[y, x, c, z]
        net.keep(own, slot)
        across = [[] for _ in range(sizes["x"])]
        for dx in range(1, sizes["x"]):
            across[dx].append(net.send(own, slot, (dx, 0, 0, 0)))
        net.send(own, slot, OTHER_Y)
        for copy, dc, dz in got:
            copy.landed()
            slot = dst.at[
                y, x, lax.rem(c + sizes["c"] - dc, sizes["c"]), lax.rem(z + sizes["z"] - dz, sizes["z"])
            ]
            for dx in range(1, sizes["x"]):
                across[dx].append(net.send(slot, slot, (dx, 0, 0, 0)))
            net.send(slot, slot, OTHER_Y)
        return across

    def relay(dst, across):
        for dx in range(1, sizes["x"]):
            for copy in across[dx]:
                copy.landed()
            block = dst.at[y, lax.rem(x + sizes["x"] - dx, sizes["x"])]
            net.send(block, block, OTHER_Y)

    got_gate = scatter(*mlp[0])
    got_up = scatter(*mlp[1])
    across = own_to_x_c(net, attention)
    over_gate = spread(*mlp[0], got_gate)
    got_down = scatter(*mlp[2])
    over_up = spread(*mlp[1], got_up)
    first = spread_z_x_c(net, attention)
    relay(mlp[0][1], over_gate)
    over_down = spread(*mlp[2], got_down)
    relay(mlp[1][1], over_up)
    forward_z(net, attention, first, across)
    relay(mlp[2][1], over_down)
    forward_x(net, across)


def gather_pairs(net, own, out):
    x, c, z, y = (net.me[a] for a in AXES)
    sizes = net.sizes
    net.keep(own, out.at[y, x, c, z])
    slot = out.at[y, x, c, z]
    first = [net.send(own, slot, (0, 0, dz, 0)) for dz in range(1, sizes["z"])]
    across = [(net.send(own, slot, (dx, 0, 0, 0)), dx, 0) for dx in range(1, sizes["x"])]
    over = [(net.send(own, slot, OTHER_Y), 0, 0)]
    net.send(own, slot, SIBLING)
    for dz in range(1, sizes["z"]):
        first[dz - 1].landed()
        slot = out.at[y, x, c, lax.rem(z + sizes["z"] - dz, sizes["z"])]
        for dx in range(1, sizes["x"]):
            across.append((net.send(slot, slot, (dx, 0, 0, 0)), dx, dz))
        over.append((net.send(slot, slot, OTHER_Y), 0, dz))
        net.send(slot, slot, SIBLING)
    for copy, dx, dz in across:
        copy.landed()
        slot = out.at[
            y, lax.rem(x + sizes["x"] - dx, sizes["x"]), c, lax.rem(z + sizes["z"] - dz, sizes["z"])
        ]
        over.append((net.send(slot, slot, OTHER_Y), dx, dz))
        net.send(slot, slot, SIBLING)
    for copy, dx, dz in over:
        copy.landed()
        slot = out.at[
            lax.rem(y + sizes["y"] - 1, sizes["y"]),
            lax.rem(x + sizes["x"] - dx, sizes["x"]),
            c,
            lax.rem(z + sizes["z"] - dz, sizes["z"]),
        ]
        net.send(slot, slot, SIBLING)


def swap_y(net, *refs):
    count = len(refs) // 2
    for src, dst in zip(refs[:count], refs[count:]):
        net.send(src, dst, OTHER_Y)


def swap_c(net, *refs):
    count = len(refs) // 2
    for src, dst in zip(refs[:count], refs[count:]):
        net.send(src.at[lax.rem(net.me["c"] + 1, net.sizes["c"])], dst, SIBLING)


def scatter_z(net, *refs):
    count, z = len(refs) // 2, net.me["z"]
    for src, dst in zip(refs[:count], refs[count:]):
        net.keep(src.at[z], dst.at[z])
        for dz in range(1, net.sizes["z"]):
            net.send(src.at[lax.rem(z + dz, net.sizes["z"])], dst.at[z], (0, 0, dz, 0))


def gather_rows(net, *refs):
    count, c, z = len(refs) // 2, net.me["c"], net.me["z"]
    waits = []
    for src, dst in zip(refs[:count], refs[count:]):
        net.keep(src, dst.at[c, z])
        waits.append([net.send(src, dst.at[c, z], (0, 0, dz, 0)) for dz in range(1, net.sizes["z"])])
        net.send(src, dst.at[c, z], SIBLING)
    for dst, copies in zip(refs[count:], waits):
        for dz in range(1, net.sizes["z"]):
            copies[dz - 1].landed()
            slot = dst.at[c, lax.rem(z + net.sizes["z"] - dz, net.sizes["z"])]
            net.send(slot, slot, SIBLING)


def return_pairs(reach, net, src, dst):
    y, n = net.me["y"], net.sizes["n"]
    for offset in range(reach + 1):
        for dy in range(net.sizes["y"]):
            piece = src.at[lax.rem(y + dy, net.sizes["y"]), reach - offset]
            slot = dst.at[y, offset]
            if offset == 0 and dy == 0:
                net.keep(piece, slot)
            else:
                net.send(piece, slot, ((n - offset) % n, dy))


def return_first(net, *refs):
    x, c, z, y = (net.me[a] for a in AXES)
    sizes = net.sizes
    attention, mlp, halves, gains = refs[0:3], refs[3:6], refs[6:8], refs[8]
    attention_out, mlp_out, halves_out, gains_out = refs[9:12], refs[12:15], refs[15:17], refs[17]
    for src, dst in zip(attention, attention_out):
        for dx in range(1, sizes["x"]):
            net.send(src.at[lax.rem(x + dx, sizes["x"])], dst.at[dx - 1], (dx, 0, 0, 0))
    for src, dst in zip(mlp, mlp_out):
        net.keep(src.at[c, z], dst.at[c, z])
        for dz in range(sizes["z"]):
            for dc in range(sizes["c"]):
                if dz or dc:
                    piece = src.at[lax.rem(c + dc, sizes["c"]), lax.rem(z + dz, sizes["z"])]
                    net.send(piece, dst.at[c, z], (0, dc, dz, 0))
    for src, dst in zip(halves, halves_out):
        net.send(src, dst, OTHER_Y)
    me = (x * sizes["c"] + c) * sizes["z"] + z
    for offset in range(sizes["n"]):
        for dy in range(sizes["y"]):
            slot, piece = gains_out.at[y, me], gains.at[lax.rem(me + offset, sizes["n"])]
            if offset == 0 and dy == 0:
                net.keep(piece, slot)
            else:
                net.send(piece, slot, (offset, dy))


def rms_forward(values, gain_row):
    inverse = lax.rsqrt(jnp.mean(values * values, axis=-1, keepdims=True) + EPSILON)
    return (values * inverse * gain_row, inverse)


def rms_backward(values, inverse, gain_row, incoming):
    scaled = incoming * gain_row
    gain_grad = jnp.sum(incoming * values * inverse, axis=0)
    value_grad = inverse * scaled - values * inverse * inverse * inverse * jnp.mean(
        scaled * values, axis=-1, keepdims=True
    )
    return (value_grad, gain_grad)


def rope_tables(positions):
    quarter = HD // 4
    freqs = jnp.exp(-math.log(10000.0) * jnp.arange(quarter, dtype=jnp.float32) * 2.0 / (HD // 2))
    angles = positions.astype(jnp.float32)[:, None] * freqs[None, :]
    return (jnp.cos(angles), jnp.sin(angles))


def rotate(values, cosine_table, sine_table):
    quarter = cosine_table.shape[1]
    lead_part = values[..., :quarter]
    pair_part = values[..., quarter : 2 * quarter]
    tail_part = values[..., 2 * quarter :]
    cos_wide = cosine_table[:, None, :]
    sin_wide = sine_table[:, None, :]
    return jnp.concatenate(
        [
            lead_part * cos_wide - pair_part * sin_wide,
            pair_part * cos_wide + lead_part * sin_wide,
            tail_part,
        ],
        axis=-1,
    )


def segment_of(index, doc_ends):
    return jnp.sum((doc_ends[None, :] <= index[:, None]).astype(jnp.int32), axis=1)


def adam_update(weight, moment_old, square_old, gradient, rate_step, decay_rate):
    moment_new = BETA_ONE * moment_old + (1.0 - BETA_ONE) * gradient
    square_new = BETA_TWO * square_old + (1.0 - BETA_TWO) * gradient * gradient
    corrected = moment_new / (1.0 - BETA_ONE**STEP)
    corrected_square = square_new / (1.0 - BETA_TWO**STEP)
    weight_new = weight - rate_step * (
        corrected / (jnp.sqrt(corrected_square) + ADAM_EPS) + decay_rate * weight
    )
    return (moment_new, square_new, weight_new)


def body(
    sizes,
    tokens,
    cotangent,
    doc_lengths,
    w_query,
    w_keyvalue,
    w_out,
    w_gate,
    w_up,
    w_down,
    norm_gains,
    first_query,
    first_keyvalue,
    first_out,
    first_gate,
    first_up,
    first_down,
    first_gains,
    second_query,
    second_keyvalue,
    second_out,
    second_gate,
    second_up,
    second_down,
    second_gains,
):
    masters = (w_query, w_keyvalue, w_out, w_gate, w_up, w_down, norm_gains)
    firsts = (first_query, first_keyvalue, first_out, first_gate, first_up, first_down, first_gains)
    seconds = (
        second_query,
        second_keyvalue,
        second_out,
        second_gate,
        second_up,
        second_down,
        second_gains,
    )
    x, c, z, y = (lax.axis_index(a) for a in AXES)
    X, C, Z, Y, N = (sizes[a] for a in (*AXES, "n"))
    F = C * Z
    rows_w = w_query.shape[0]
    columns = w_query.shape[1]
    rows = tokens.shape[0]
    half = rows // Y
    head_count = columns // HD
    piece = w_gate.shape[1] // F
    device = (x * C + c) * Z + z

    def pick(values, index):
        return lax.dynamic_index_in_dim(values, index, 0, keepdims=False)

    def pieces(weight):
        return weight.astype(BF16).reshape(rows_w, F, piece).transpose(1, 0, 2)

    low_gains = jnp.pad(norm_gains.astype(BF16).astype(F32), ((0, 6), (0, 0)))
    pair_weight = lax.dynamic_slice_in_dim(w_keyvalue, y * HD, HD, 1).astype(BF16)
    g_query, g_out, g_pair, g_gains, g_gate, g_up, g_down = exchange(
        gather_weights,
        [
            w_query.astype(BF16),
            w_out.astype(BF16),
            pair_weight,
            low_gains,
            pieces(w_gate),
            pieces(w_up),
            pieces(w_down),
        ],
        [
            ((X, C, Z, rows_w, columns), BF16),
            ((X, C, Z, rows_w, columns), BF16),
            ((X, C, Z, rows_w, HD), BF16),
            ((X, C, Z, 8, rows_w), F32),
        ]
        + [((Y, X, C, Z, rows_w, piece), BF16)] * 3,
        sizes,
        1,
    )
    g_query, g_out, g_pair = (g.reshape(D, -1) for g in (g_query, g_out, g_pair))
    gain_values = g_gains.reshape(N, 8, rows_w)[:, :2].transpose(1, 0, 2).reshape(2, D)
    g_gate, g_up, g_down = (g.reshape(Y, D, piece) for g in (g_gate, g_up, g_down))

    start_row = device * rows
    query_index = start_row + jnp.arange(rows, dtype=jnp.int32)
    doc_ends = jnp.cumsum(doc_lengths.reshape(-1))
    query_segment = segment_of(query_index, doc_ends)
    cosine_table, sine_table = rope_tables(query_index % SEQ_LEN)
    reach = (WINDOW - 1) // rows + 1
    scale = HD ** (-0.5)
    residual_in = tokens.astype(F32)
    normed_first, inverse_first = rms_forward(residual_in, gain_values[0])
    normed_first = normed_first.astype(BF16)
    query_raw = jnp.dot(normed_first, g_query, preferred_element_type=F32)
    pair_raw = jnp.dot(normed_first, g_pair, preferred_element_type=F32)
    query_rot = (
        rotate(query_raw.reshape(rows, head_count, HD), cosine_table, sine_table) * scale
    ).astype(BF16)
    own_pair = jnp.where(
        y == 0, rotate(pair_raw[:, None], cosine_table, sine_table)[:, 0], pair_raw
    ).astype(BF16)

    (all_pairs,) = exchange(
        gather_pairs, [own_pair], [((Y, X, C, Z, rows, HD), BF16)], sizes, 2
    )
    all_pairs = jnp.pad(all_pairs.reshape(Y, N * rows, HD), ((0, 0), (reach * rows, 0), (0, 0)))
    near = lax.dynamic_slice_in_dim(all_pairs, start_row, (reach + 1) * rows, 1)
    keys_all, values_all = near[0], near[1]
    key_index = start_row - reach * rows + jnp.arange((reach + 1) * rows, dtype=jnp.int32)
    key_segment = segment_of(key_index, doc_ends)
    allowed = (
        (query_segment[:, None] == key_segment[None, :])
        & (key_index[None, :] <= query_index[:, None])
        & (query_index[:, None] - key_index[None, :] < WINDOW)
        & (key_index[None, :] >= 0)
    )
    scores = jnp.einsum("qhd,kd->hqk", query_rot, keys_all, preferred_element_type=F32)
    scores = jnp.where(allowed[None], scores, -jnp.inf)
    row_top = jnp.max(scores, axis=-1, keepdims=True)
    exp_scores = jnp.exp(scores - row_top)
    row_total = jnp.sum(exp_scores, axis=-1, keepdims=True)
    prob_table = exp_scores / row_total
    log_total = row_top + jnp.log(row_total)
    attended = jnp.einsum(
        "hqk,kd->qhd", prob_table.astype(BF16), values_all, preferred_element_type=F32
    )
    attended_low = attended.reshape(rows, head_count * HD).astype(BF16)
    attention_part = lax.dot_general(
        attended_low, g_out, CONTRACT_LAST, preferred_element_type=F32
    ).reshape(Y, half, D)

    (part_in,) = exchange(
        swap_y, [pick(attention_part, 1 - y).astype(BF16)], [((half, D), BF16)], sizes, 3
    )
    middle = (
        pick(residual_in.reshape(Y, half, D), y) + pick(attention_part, y) + part_in.astype(F32)
    )
    normed_second, inverse_second = rms_forward(middle, gain_values[1])
    cotangent_half = pick(cotangent.reshape(Y, half, D), y)
    normed_all, down_grad = exchange(
        gather_rows,
        [normed_second.astype(BF16), cotangent_half.astype(BF16)],
        [((C, Z, half, D), BF16)] * 2,
        sizes,
        4,
    )
    normed_all = normed_all.reshape(F * half, D)
    down_grad = down_grad.reshape(F * half, D)

    feed_part, second_part = 0.0, 0.0
    grads_gate, grads_up, grads_down = [], [], []
    for side in range(Y):
        gate_pre = jnp.dot(normed_all, g_gate[side], preferred_element_type=F32)
        up_pre = jnp.dot(normed_all, g_up[side], preferred_element_type=F32)
        activated, gelu_back = jax.vjp(jax.nn.gelu, gate_pre)
        hidden = (activated * up_pre).astype(BF16)
        feed_part = feed_part + lax.dot_general(
            hidden, g_down[side], CONTRACT_LAST, preferred_element_type=F32
        )
        hidden_grad = jnp.dot(down_grad, g_down[side], preferred_element_type=F32)
        gate_grad = gelu_back(hidden_grad * up_pre)[0].astype(BF16)
        up_grad = (hidden_grad * activated).astype(BF16)
        second_part = (
            second_part
            + lax.dot_general(gate_grad, g_gate[side], CONTRACT_LAST, preferred_element_type=F32)
            + lax.dot_general(up_grad, g_up[side], CONTRACT_LAST, preferred_element_type=F32)
        )
        for grads, left, right in (
            (grads_gate, normed_all, gate_grad),
            (grads_up, normed_all, up_grad),
            (grads_down, down_grad, hidden),
        ):
            grads.append(
                lax.dot_general(left, right, CONTRACT_FIRST, preferred_element_type=F32).astype(BF16)
            )

    second_part = second_part.astype(BF16).reshape(C, Z, half, D)
    (sibling_part,) = exchange(swap_c, [second_part], [((Z, half, D), BF16)], sizes, 5)
    chip_part = (pick(second_part, c).astype(F32) + sibling_part.astype(F32)).astype(BF16)
    (second_pieces,) = exchange(scatter_z, [chip_part], [((Z, half, D), BF16)], sizes, 6)
    second_grad = jnp.sum(second_pieces.astype(F32), axis=0)

    def over_y_x(grads):
        stacked = jnp.stack(grads).reshape(Y * X, C, Z, rows_w, piece)
        return lax.psum_scatter(stacked, ("y", "x"), scatter_dimension=0, tiled=True).reshape(
            C, Z, rows_w, piece
        )

    mlp_grads = [over_y_x(grads) for grads in (grads_gate, grads_up, grads_down)]
    feed_out = lax.psum_scatter(
        feed_part.astype(BF16), ("c", "z"), scatter_dimension=0, tiled=True
    ).astype(F32)
    mixed_half = middle + feed_out

    middle_norm_grad, gain_two = rms_backward(middle, inverse_second, gain_values[1], second_grad)
    middle_grad = cotangent_half + middle_norm_grad
    branch_half = middle_grad.astype(BF16)
    (branch_in,) = exchange(swap_y, [branch_half], [((half, D), BF16)], sizes, 7)
    branch_grad = jnp.where(
        y == 0,
        jnp.concatenate([branch_half, branch_in]),
        jnp.concatenate([branch_in, branch_half]),
    )
    grad_out = lax.dot_general(
        branch_grad, attended_low, CONTRACT_FIRST, preferred_element_type=F32
    ).astype(BF16)
    attended_grad = jnp.dot(branch_grad, g_out, preferred_element_type=F32).astype(BF16)
    attended_grad = attended_grad.reshape(rows, head_count, HD)
    scores_again = jnp.einsum("qhd,kd->hqk", query_rot, keys_all, preferred_element_type=F32)
    scores_again = jnp.where(allowed[None], scores_again, -jnp.inf)
    prob_again = jnp.exp(scores_again - log_total)
    prob_grad = jnp.einsum("qhd,kd->hqk", attended_grad, values_all, preferred_element_type=F32)
    score_grad = (
        prob_again * (prob_grad - jnp.sum(prob_again * prob_grad, axis=-1, keepdims=True))
    ).astype(BF16)
    query_grad_rot = (
        jnp.einsum("hqk,kd->qhd", score_grad, keys_all, preferred_element_type=F32) * scale
    )
    key_grad_all = jnp.einsum("hqk,qhd->kd", score_grad, query_rot, preferred_element_type=F32)
    value_grad_all = jnp.einsum(
        "hqk,qhd->kd", prob_again.astype(BF16), attended_grad, preferred_element_type=F32
    )
    pair_grad = jnp.stack([key_grad_all, value_grad_all]).astype(BF16)
    (pair_parts,) = exchange(
        functools.partial(return_pairs, reach),
        [pair_grad.reshape(2, reach + 1, rows, HD)],
        [((Y, reach + 1, rows, HD), BF16)],
        sizes,
        8,
    )
    pair_total = jnp.sum(pair_parts.astype(F32), axis=(0, 1))
    pair_total = jnp.where(
        y == 0, rotate(pair_total[:, None], cosine_table, -sine_table)[:, 0], pair_total
    ).astype(BF16)
    query_grad = (
        rotate(query_grad_rot, cosine_table, -sine_table)
        .reshape(rows, head_count * HD)
        .astype(BF16)
    )
    first_part = (
        lax.dot_general(query_grad, g_query, CONTRACT_LAST, preferred_element_type=F32)
        + lax.dot_general(pair_total, g_pair, CONTRACT_LAST, preferred_element_type=F32)
    ).reshape(Y, half, D)
    (first_in,) = exchange(
        swap_y, [pick(first_part, 1 - y).astype(BF16)], [((half, D), BF16)], sizes, 9
    )
    first_grad = pick(first_part, y) + first_in.astype(F32)
    grad_query = lax.dot_general(
        normed_first, query_grad, CONTRACT_FIRST, preferred_element_type=F32
    ).astype(BF16)
    grad_pair = lax.dot_general(
        normed_first, pair_total, CONTRACT_FIRST, preferred_element_type=F32
    ).astype(BF16)
    input_norm_grad, gain_one = rms_backward(
        pick(residual_in.reshape(Y, half, D), y),
        pick(inverse_first.reshape(Y, half, 1), y),
        gain_values[0],
        first_grad,
    )
    token_half = middle_grad + input_norm_grad
    grad_gains = jnp.pad(
        jnp.stack([gain_one, gain_two]).reshape(2, N, rows_w).transpose(1, 0, 2),
        ((0, 0), (0, 6), (0, 0)),
    )

    attention_grads = [
        g.reshape(X, C, Z, rows_w, -1) for g in (grad_query, grad_out, grad_pair)
    ]
    widths = (columns, columns, HD)
    results = exchange(
        return_first,
        [*attention_grads, *mlp_grads, mixed_half, token_half, grad_gains],
        [((X - 1, C, Z, rows_w, w), BF16) for w in widths]
        + [((C, Z, rows_w, piece), BF16)] * 3
        + [((half, D), F32)] * 2
        + [((Y, N, 8, rows_w), F32)],
        sizes,
        10,
    )
    mixed_in, token_in, gain_parts = results[6:]

    def whole(own, other):
        return jnp.where(
            y == 0, jnp.concatenate([own, other]), jnp.concatenate([other, own])
        )

    mixed, token_grad = whole(mixed_half, mixed_in), whole(token_half, token_in)
    reduced_gains = jnp.sum(gain_parts, axis=(0, 1))[:2]
    reduced_mlp = [
        g.reshape(F, rows_w, piece).transpose(1, 0, 2).reshape(rows_w, F * piece).astype(F32)
        for g in results[3:6]
    ]
    over_x = [
        (pick(own, x).astype(F32) + jnp.sum(got.astype(F32), axis=0)).astype(BF16)
        for own, got in zip(attention_grads, results[0:3])
    ]
    from_sibling = exchange(
        swap_c, over_x, [((Z, rows_w, w), BF16) for w in widths], sizes, 11
    )
    over_c = [
        (pick(own, c).astype(F32) + got.astype(F32)).astype(BF16)
        for own, got in zip(over_x, from_sibling)
    ]
    over_z = exchange(scatter_z, over_c, [((Z, rows_w, w), BF16) for w in widths], sizes, 12)
    reduced_query, reduced_out, reduced_half = (
        jnp.sum(g.astype(F32), axis=0) for g in over_z
    )
    (half_in,) = exchange(swap_y, [reduced_half], [((rows_w, HD), F32)], sizes, 13)
    reduced_pair = jnp.where(
        y == 0,
        jnp.concatenate([reduced_half, half_in], axis=1),
        jnp.concatenate([half_in, reduced_half], axis=1),
    )
    reduced = (reduced_query, reduced_pair, reduced_out, *reduced_mlp, reduced_gains)
    dense_rate = 2.0 * D ** (-0.5)
    out_rate = 2.0 * max(1, H * HD // 64) ** (-0.5)
    rates = (dense_rate, dense_rate, out_rate, dense_rate, dense_rate, dense_rate, 0.4)
    decays = (DECAY, DECAY, DECAY, DECAY, DECAY, DECAY, 0.0)
    new_firsts = []
    new_seconds = []
    updated = []
    for weight, moment_old, square_old, gradient, rate_step, decay_rate in zip(
        masters, firsts, seconds, reduced, rates, decays
    ):
        moment_new, square_new, weight_new = adam_update(
            weight, moment_old, square_old, gradient, rate_step, decay_rate
        )
        new_firsts.append(moment_new)
        new_seconds.append(square_new)
        updated.append(weight_new)
    return (mixed, token_grad, *new_firsts, *new_seconds, *updated)


def solution(mesh):
    shape = dict(mesh.shape)
    sizes = {"x": shape["dp"] // 2, "c": 2, "z": shape["group"], "y": shape["tensor"]}
    sizes["n"] = sizes["x"] * sizes["c"] * sizes["z"]
    grid = Mesh(mesh.devices.reshape([sizes[a] for a in AXES]), AXES)
    blocks = ("x", "c", "z")
    by_rows, by_both, gains = P(blocks, None), P(blocks, "y"), P(None, blocks)
    weights = (by_both, by_rows, by_both, by_both, by_both, by_both, gains)
    return jax.shard_map(
        functools.partial(body, sizes),
        mesh=grid,
        in_specs=(by_rows, by_rows, P(), *weights * 3),
        out_specs=(by_rows, by_rows, *weights * 3),
        check_vma=False,
    )
```

```python
import functools
import math

import jax
import jax.numpy as jnp
from jax import lax
from jax.experimental import pallas as pl
from jax.experimental.pallas import tpu as pltpu
from jax.sharding import Mesh
from jax.sharding import PartitionSpec as P

D = 2560
H = 10
HD = 256
WINDOW = 2048
SEQ_LEN = 4096
STEP = 10

EPSILON = 1e-06
BETA_ONE = 0.9
BETA_TWO = 0.95
ADAM_EPS = 1e-08
DECAY = 0.1
CONTRACT_LAST = (((1,), (1,)), ((), ()))
CONTRACT_FIRST = (((0,), (0,)), ((), ()))
BF16 = jnp.bfloat16
F32 = jnp.float32
AXES = ("x", "c", "z", "y")


class Blank:
    @property
    def at(self):
        return self

    def __getitem__(self, _):
        return self

    def landed(self):
        pass


def guarded(condition, step):
    if condition is None:
        step()
    else:
        pl.when(condition)(step)


class Copy:
    def __init__(self, copy, sends, comes):
        self.copy, self.sends, self.comes, self.arrived = copy, sends, comes, False

    def landed(self):
        if not self.arrived:
            guarded(self.comes, self.copy.wait_recv)
            self.arrived = True

    def done(self):
        self.landed()
        guarded(self.sends, self.copy.wait_send)


class Local:
    def __init__(self, copy):
        self.copy, self.arrived = copy, False

    def landed(self):
        if not self.arrived:
            self.copy.wait()
            self.arrived = True

    def done(self):
        self.landed()


class Net:
    def __init__(self, sizes, me, sems):
        self.sizes, self.me, self.sems = sizes, me, sems
        self.sent, self.kept, self.peers, self.open = 0, 0, [], []

    def device(self, where):
        s, me = self.sizes, self.me
        if len(where) == 4:
            return {a: lax.rem(me[a] + d, s[a]) for a, d in zip(AXES, where)}
        flat = lax.rem((me["x"] * s["c"] + me["c"]) * s["z"] + me["z"] + where[0], s["n"])
        return {
            "x": flat // (s["c"] * s["z"]),
            "c": lax.rem(flat // s["z"], s["c"]),
            "z": lax.rem(flat, s["z"]),
            "y": lax.rem(me["y"] + where[1], s["y"]),
        }

    def opposite(self, where):
        if len(where) == 4:
            return tuple((self.sizes[a] - d) % self.sizes[a] for a, d in zip(AXES, where))
        return ((self.sizes["n"] - where[0]) % self.sizes["n"], (self.sizes["y"] - where[1]) % self.sizes["y"])

    def send(self, src, dst, where, sends=None, comes=None):
        k = self.sent
        self.sent += 1
        if self.sems is None:
            for w in (where, self.opposite(where)):
                if w not in self.peers:
                    self.peers.append(w)
            return Blank()
        copy = pltpu.make_async_remote_copy(
            src_ref=src,
            dst_ref=dst,
            send_sem=self.sems[0].at[k],
            recv_sem=self.sems[1].at[k],
            device_id=self.device(where),
            device_id_type=pl.DeviceIdType.MESH,
        )
        guarded(sends, copy.start)
        self.open.append(Copy(copy, sends, comes))
        return self.open[-1]

    def keep(self, src, dst):
        k = self.kept
        self.kept += 1
        if self.sems is None:
            return Blank()
        copy = pltpu.make_async_copy(src, dst, self.sems[2].at[k])
        copy.start()
        self.open.append(Local(copy))
        return self.open[-1]

    def add(self, rows, step):
        if self.sems is not None:
            some = 16 if rows % 16 == 0 else rows

            def one(i, carry):
                step(pl.ds(pl.multiple_of(i * some, some), some))
                return carry

            lax.fori_loop(0, rows // some, one, 0)

    def greet(self, peers):
        barrier = pltpu.get_barrier_semaphore()
        for where in peers:
            pl.semaphore_signal(
                barrier, inc=1, device_id=self.device(where), device_id_type=pl.DeviceIdType.MESH
            )
        pl.semaphore_wait(barrier, len(peers))

    def finish(self):
        for item in self.open:
            item.done()


def exchange(plan, arrays, outs, sizes, number, scratch=(), in_vmem=()):
    count = Net(sizes, {a: 0 for a in AXES}, None)
    plan(count, *[Blank()] * (len(arrays) + len(outs) + len(scratch)))

    def kernel(*refs):
        data, sems = refs[:-3], refs[-3:]
        net = Net(sizes, {a: lax.axis_index(a) for a in AXES}, sems)
        net.greet(count.peers)
        plan(net, *data)
        net.finish()

    anywhere = pl.BlockSpec(memory_space=pl.ANY)
    inside = pl.BlockSpec(memory_space=pltpu.VMEM)
    return pl.pallas_call(
        kernel,
        out_shape=[jax.ShapeDtypeStruct(shape, dtype) for shape, dtype in outs],
        in_specs=[anywhere] * len(arrays),
        out_specs=[inside if i in in_vmem else anywhere for i in range(len(outs))],
        scratch_shapes=[
            *(pltpu.VMEM(shape, dtype) for shape, dtype in scratch),
            pltpu.SemaphoreType.DMA((count.sent,)),
            pltpu.SemaphoreType.DMA((count.sent,)),
            pltpu.SemaphoreType.DMA((max(1, count.kept),)),
        ],
        compiler_params=pltpu.CompilerParams(
            collective_id=number, has_side_effects=True, vmem_limit_bytes=48 * 2**20
        ),
    )(*arrays)


SIBLING = (0, 1, 0, 0)
OTHER_Y = (0, 0, 0, 1)


def back(value, step, size):
    return lax.rem(value + size - step, size)


def along_line(net, pairs):
    z, size = net.me["z"], net.sizes["z"]

    def up(pair, step):
        slot = pair[1](back(z, step, size))
        return net.send(
            slot if step else pair[0],
            slot,
            (0, 0, 1, 0),
            sends=(z + 1 < size) & (z - step >= 0),
            comes=z - 1 - step >= 0,
        )

    def down(pair, step):
        slot = pair[1](lax.rem(z + step, size))
        return net.send(
            slot if step else pair[0],
            slot,
            (0, 0, size - 1, 0),
            sends=(z >= 1) & (z + step < size),
            comes=z + 1 + step < size,
        )

    moves = [(up(pair, 0), down(pair, 0)) for pair in pairs]

    def steps():
        for step in range(size - 1):
            for i, pair in enumerate(pairs):
                rising, falling = moves[i]
                rising.landed()
                if step + 1 < size - 1:
                    rising = up(pair, step + 1)
                yield i, (back(z, step + 1, size), z - 1 - step >= 0)
                falling.landed()
                if step + 1 < size - 1:
                    falling = down(pair, step + 1)
                yield i, (lax.rem(z + step + 1, size), z + 1 + step < size)
                moves[i] = (rising, falling)

    return steps()


def gather_weights(width, net, *refs):
    x, c, z, y = (net.me[a] for a in AXES)
    xs, cs, zs = (net.sizes[a] for a in "xcz")
    pairs = list(zip(refs[0:4], refs[7:11]))
    gate, up, down = refs[4:7]
    gate_out, up_out, down_out = refs[11:14]
    mine = pl.ds(y * width, width)

    def part(src, f):
        return src.at[:, pl.ds(f * width, width)]

    def scatter(src, slot):
        got = []
        for dz in range(zs):
            for dc in range(cs):
                if dz or dc:
                    f = lax.rem(c + dc, cs) * zs + lax.rem(z + dz, zs)
                    copy = net.send(part(src, f), slot(c, z), (0, dc, dz, 0))
                    got.append((copy, slot(back(c, dc, cs), back(z, dz, zs))))
        return got

    def spread(src, slot, got):
        own = part(src, c * zs + z)
        net.keep(own, slot(c, z))
        across = [[net.send(own, slot(c, z), (dx, 0, 0, 0))] for dx in range(1, xs)]
        net.send(own, slot(c, z), OTHER_Y)
        for copy, ref in got:
            copy.landed()
            for dx in range(1, xs):
                across[dx - 1].append(net.send(ref, ref, (dx, 0, 0, 0)))
            net.send(ref, ref, OTHER_Y)
        return across

    def relay(dst, across):
        for dx in range(1, xs):
            for copy in across[dx - 1]:
                copy.landed()
            for i in range(cs):
                block = dst.at[back(x, dx, xs), i, :, :, mine]
                net.send(block, block, OTHER_Y)

    def gate_slot(i, j):
        return gate_out.at[x, i, j, :, mine]

    def up_slot(i, j):
        return up_out.at[x, i, j, :, mine]

    def down_slot(i, j):
        return down_out.at[i, j]

    got_gate = scatter(gate, gate_slot)
    line = along_line(
        net, [(src, lambda j, dst=dst: dst.at[x, c, j]) for src, dst in pairs]
    )
    across = []

    def onward(i, src, slot, condition):
        for dx in range(1, xs):
            copy = net.send(src, slot(x), (dx, 0, 0, 0), sends=condition, comes=condition)
            across.append((copy, slot(back(x, dx, xs)), condition))
        net.send(src, slot(x), SIBLING, sends=condition, comes=condition)

    for i, (src, dst) in enumerate(pairs):
        net.keep(src, dst.at[x, c, z])
        onward(i, src, lambda px, dst=dst: dst.at[px, c, z], None)

    def advance():
        for _ in range(2 * len(pairs)):
            i, (j, condition) = next(line)
            dst = pairs[i][1]
            onward(i, dst.at[x, c, j], lambda px, dst=dst: dst.at[px, c, j], condition)

    over_gate = spread(gate, gate_slot, got_gate)
    got_up = scatter(up, up_slot)
    advance()
    over_up = spread(up, up_slot, got_up)
    got_down = scatter(down, down_slot)
    net.keep(part(down, c * zs + z), down_slot(c, z))
    relay(gate_out, over_gate)
    for _ in range(zs - 2):
        advance()
    relay(up_out, over_up)
    for copy, slot, condition in across:
        copy.landed()
        net.send(slot, slot, SIBLING, sends=condition, comes=condition)


def gather_rows(width, net, rows, block, all_rows, all_blocks):
    x, c, z, y = (net.me[a] for a in AXES)
    xs, cs = net.sizes["x"], net.sizes["c"]
    mine = pl.ds(y * width, width)
    line = along_line(net, [(rows, lambda j: all_rows.at[c, j])])
    across = []
    for i in range(cs):
        slot = all_blocks.at[x, i, :, :, mine]
        net.keep(block.at[i], slot)
        for dx in range(1, xs):
            copy = net.send(block.at[i], slot, (dx, 0, 0, 0))
            across.append((copy, all_blocks.at[back(x, dx, xs), i, :, :, mine]))
        net.send(block.at[i], slot, OTHER_Y)
    net.keep(rows, all_rows.at[c, z])
    net.send(rows, all_rows.at[c, z], SIBLING)
    for step, (_, (j, condition)) in enumerate(line):
        slot = all_rows.at[c, j]
        net.send(slot, slot, SIBLING, sends=condition, comes=condition)
    for copy, slot in across:
        copy.landed()
        net.send(slot, slot, OTHER_Y)


def far_first(size):
    return sorted(range(size), key=lambda d: -min(d, size - d))


def sum_rows(net, part, out, own, got, landed):
    c, z = net.me["c"], net.me["z"]
    zs = net.sizes["z"]
    rows = 0 if net.sems is None else out.shape[0]
    ready = {}
    for dz in far_first(zs):
        j = lax.rem(z + dz, zs)
        ready[dz] = (
            net.send(part.at[lax.rem(c + 1, net.sizes["c"]), j], got.at[j], SIBLING),
            net.keep(part.at[c, j], own.at[j]),
        )
    sent = {}
    for dz in far_first(zs):
        j = lax.rem(z + dz, zs)
        for copy in ready[dz]:
            copy.landed()

        def both(at, j=j):
            return own[j, at].astype(F32) + got[j, at].astype(F32)

        if dz:

            def keep_low(at, j=j, both=both):
                own[j, at] = both(at).astype(BF16)

            net.add(rows, keep_low)
            sent[dz] = net.send(own.at[j], landed.at[dz - 1], (0, 0, dz, 0))
        else:

            def keep_wide(at, both=both):
                out[at] = both(at)

            net.add(rows, keep_wide)
    for dz in range(1, zs):
        sent[dz].landed()

        def more(at, dz=dz):
            out[at] += landed[dz - 1, at].astype(F32)

        net.add(rows, more)


def sum_weights(net, *refs):
    x, c, z, y = (net.me[a] for a in AXES)
    xs, cs, zs = (net.sizes[a] for a in "xcz")
    sources, swapped, gains = refs[0:3], refs[3:5], refs[5]
    outs, swapped_out, gains_out = refs[6:9], refs[9:11], refs[11]
    own, got, from_x, from_z = (refs[12 + 3 * i : 15 + 3 * i] for i in range(4))
    rows = 0 if net.sems is None else outs[0].shape[0]
    order = far_first(zs)
    ready = {}
    for dx in [*range(1, xs), 0]:
        i = lax.rem(x + dx, xs)
        for dz in order:
            j = lax.rem(z + dz, zs)
            for k in range(3):
                ready[dx, dz, k] = (
                    net.send(
                        sources[k].at[i, lax.rem(c + 1, cs), j], got[k].at[i, j], SIBLING
                    ),
                    net.keep(sources[k].at[i, c, j], own[k].at[i, j]),
                )
    for src, dst in zip(swapped, swapped_out):
        net.send(src, dst, OTHER_Y)
    gains_to_owners(net, gains, gains_out)
    over = {}
    for dx in range(1, xs):
        i = lax.rem(x + dx, xs)
        for dz in order:
            j = lax.rem(z + dz, zs)
            for k in range(3):
                for copy in ready[dx, dz, k]:
                    copy.landed()

                def pair(at, mine=own[k], other=got[k], i=i, j=j):
                    mine[i, j, at] = (
                        mine[i, j, at].astype(F32) + other[i, j, at].astype(F32)
                    ).astype(BF16)

                net.add(rows, pair)
                over[dx, dz, k] = net.send(
                    own[k].at[i, j], from_x[k].at[dx - 1, j], (dx, 0, 0, 0)
                )
    sent = {}
    for dz in order:
        j = lax.rem(z + dz, zs)
        for k in range(3):
            for copy in ready[0, dz, k]:
                copy.landed()
            for dx in range(1, xs):
                over[dx, dz, k].landed()

            def chips(at, mine=own[k], other=got[k], far=from_x[k], j=j):
                total = mine[x, j, at].astype(F32) + other[x, j, at].astype(F32)
                for dx in range(1, xs):
                    total = total + far[dx - 1, j, at].astype(F32)
                return total

            if dz:

                def keep_low(at, mine=own[k], chips=chips, j=j):
                    mine[x, j, at] = chips(at).astype(BF16)

                net.add(rows, keep_low)
                sent[dz, k] = net.send(own[k].at[x, j], from_z[k].at[dz - 1], (0, 0, dz, 0))
            else:

                def keep_wide(at, out=outs[k], chips=chips):
                    out[at] = chips(at)

                net.add(rows, keep_wide)
    for dz in order[:-1]:
        for k in range(3):
            sent[dz, k].landed()

            def more(at, out=outs[k], far=from_z[k], dz=dz):
                out[at] += far[dz - 1, at].astype(F32)

            net.add(rows, more)


def gather_pairs(net, own, out):
    x, c, z, y = (net.me[a] for a in AXES)
    sizes = net.sizes
    net.keep(own, out.at[y, x, c, z])
    slot = out.at[y, x, c, z]
    first = [net.send(own, slot, (0, 0, dz, 0)) for dz in range(1, sizes["z"])]
    across = [(net.send(own, slot, (dx, 0, 0, 0)), dx, 0) for dx in range(1, sizes["x"])]
    over = [(net.send(own, slot, OTHER_Y), 0, 0)]
    net.send(own, slot, SIBLING)
    for dz in range(1, sizes["z"]):
        first[dz - 1].landed()
        slot = out.at[y, x, c, lax.rem(z + sizes["z"] - dz, sizes["z"])]
        for dx in range(1, sizes["x"]):
            across.append((net.send(slot, slot, (dx, 0, 0, 0)), dx, dz))
        over.append((net.send(slot, slot, OTHER_Y), 0, dz))
        net.send(slot, slot, SIBLING)
    for copy, dx, dz in across:
        copy.landed()
        slot = out.at[
            y, lax.rem(x + sizes["x"] - dx, sizes["x"]), c, lax.rem(z + sizes["z"] - dz, sizes["z"])
        ]
        over.append((net.send(slot, slot, OTHER_Y), dx, dz))
        net.send(slot, slot, SIBLING)
    for copy, dx, dz in over:
        copy.landed()
        slot = out.at[
            lax.rem(y + sizes["y"] - 1, sizes["y"]),
            lax.rem(x + sizes["x"] - dx, sizes["x"]),
            c,
            lax.rem(z + sizes["z"] - dz, sizes["z"]),
        ]
        net.send(slot, slot, SIBLING)


def swap_y(net, *refs):
    count = len(refs) // 2
    for src, dst in zip(refs[:count], refs[count:]):
        net.send(src, dst, OTHER_Y)


def return_pairs(reach, net, src, dst):
    y, n = net.me["y"], net.sizes["n"]
    for offset in range(reach + 1):
        for dy in range(net.sizes["y"]):
            piece = src.at[lax.rem(y + dy, net.sizes["y"]), reach - offset]
            slot = dst.at[y, offset]
            if offset == 0 and dy == 0:
                net.keep(piece, slot)
            else:
                net.send(piece, slot, ((n - offset) % n, dy))


def gains_to_owners(net, gains, gains_out):
    x, c, z, y = (net.me[a] for a in AXES)
    n = net.sizes["n"]
    me = (x * net.sizes["c"] + c) * net.sizes["z"] + z
    for offset in range(n):
        for dy in range(net.sizes["y"]):
            slot, piece = gains_out.at[y, me], gains.at[lax.rem(me + offset, n)]
            if offset == 0 and dy == 0:
                net.keep(piece, slot)
            else:
                net.send(piece, slot, (offset, dy))


def finish_small(net, pair, gains, pair_out, gains_out):
    net.send(pair, pair_out, OTHER_Y)
    gains_to_owners(net, gains, gains_out)


def rms_forward(values, gain_row):
    inverse = lax.rsqrt(jnp.mean(values * values, axis=-1, keepdims=True) + EPSILON)
    return (values * inverse * gain_row, inverse)


def rms_backward(values, inverse, gain_row, incoming):
    scaled = incoming * gain_row
    gain_grad = jnp.sum(incoming * values * inverse, axis=0)
    value_grad = inverse * scaled - values * inverse * inverse * inverse * jnp.mean(
        scaled * values, axis=-1, keepdims=True
    )
    return (value_grad, gain_grad)


def rope_tables(positions):
    quarter = HD // 4
    freqs = jnp.exp(-math.log(10000.0) * jnp.arange(quarter, dtype=jnp.float32) * 2.0 / (HD // 2))
    angles = positions.astype(jnp.float32)[:, None] * freqs[None, :]
    return (jnp.cos(angles), jnp.sin(angles))


def rotate(values, cosine_table, sine_table):
    quarter = cosine_table.shape[1]
    lead_part = values[..., :quarter]
    pair_part = values[..., quarter : 2 * quarter]
    tail_part = values[..., 2 * quarter :]
    cos_wide = cosine_table[:, None, :]
    sin_wide = sine_table[:, None, :]
    return jnp.concatenate(
        [
            lead_part * cos_wide - pair_part * sin_wide,
            pair_part * cos_wide + lead_part * sin_wide,
            tail_part,
        ],
        axis=-1,
    )


def segment_of(index, doc_ends):
    return jnp.sum((doc_ends[None, :] <= index[:, None]).astype(jnp.int32), axis=1)


def adam_update(weight, moment_old, square_old, gradient, rate_step, decay_rate):
    moment_new = BETA_ONE * moment_old + (1.0 - BETA_ONE) * gradient
    square_new = BETA_TWO * square_old + (1.0 - BETA_TWO) * gradient * gradient
    corrected = moment_new / (1.0 - BETA_ONE**STEP)
    corrected_square = square_new / (1.0 - BETA_TWO**STEP)
    weight_new = weight - rate_step * (
        corrected / (jnp.sqrt(corrected_square) + ADAM_EPS) + decay_rate * weight
    )
    return (moment_new, square_new, weight_new)


def body(
    sizes,
    tokens,
    cotangent,
    doc_lengths,
    w_query,
    w_keyvalue,
    w_out,
    w_gate,
    w_up,
    w_down,
    norm_gains,
    first_query,
    first_keyvalue,
    first_out,
    first_gate,
    first_up,
    first_down,
    first_gains,
    second_query,
    second_keyvalue,
    second_out,
    second_gate,
    second_up,
    second_down,
    second_gains,
):
    masters = (w_query, w_keyvalue, w_out, w_gate, w_up, w_down, norm_gains)
    firsts = (first_query, first_keyvalue, first_out, first_gate, first_up, first_down, first_gains)
    seconds = (
        second_query,
        second_keyvalue,
        second_out,
        second_gate,
        second_up,
        second_down,
        second_gains,
    )
    x, c, z, y = (lax.axis_index(a) for a in AXES)
    X, C, Z, Y, N = (sizes[a] for a in (*AXES, "n"))
    F = C * Z
    rows_w = w_query.shape[0]
    columns = w_query.shape[1]
    rows = tokens.shape[0]
    half = rows // Y
    head_count = columns // HD
    mlp_columns = w_gate.shape[1]
    width = -(-mlp_columns // (F * 128)) * 128
    device = (x * C + c) * Z + z

    def pick(values, index):
        return lax.dynamic_index_in_dim(values, index, 0, keepdims=False)

    def pieces(weight):
        return jnp.pad(weight.astype(BF16), ((0, 0), (0, F * width - mlp_columns)))

    low_gains = jnp.pad(norm_gains.astype(BF16).astype(F32), ((0, 6), (0, 0)))
    pair_weight = lax.dynamic_slice_in_dim(w_keyvalue, y * HD, HD, 1).astype(BF16)
    g_query, g_out, g_pair, g_gains, g_gate, g_up, down_block = exchange(
        functools.partial(gather_weights, width),
        [
            w_query.astype(BF16),
            w_out.astype(BF16),
            pair_weight,
            low_gains,
            pieces(w_gate),
            pieces(w_up),
            pieces(w_down),
        ],
        [
            ((X, C, Z, rows_w, columns), BF16),
            ((X, C, Z, rows_w, columns), BF16),
            ((X, C, Z, rows_w, HD), BF16),
            ((X, C, Z, 8, rows_w), F32),
        ]
        + [((X, C, Z, rows_w, Y * width), BF16)] * 2
        + [((C, Z, rows_w, width), BF16)],
        sizes,
        1,
    )
    g_query, g_out, g_pair = (g.reshape(D, -1) for g in (g_query, g_out, g_pair))
    gain_values = g_gains.reshape(N, 8, rows_w)[:, :2].transpose(1, 0, 2).reshape(2, D)
    g_gate, g_up = g_gate.reshape(D, Y * width), g_up.reshape(D, Y * width)
    cotangent_half = pick(cotangent.reshape(Y, half, D), y)
    down_grad, _ = lax.optimization_barrier((cotangent_half.astype(BF16), down_block))
    down_grad = lax.all_gather(down_grad, ("c", "z"), axis=0, tiled=True)

    start_row = device * rows
    query_index = start_row + jnp.arange(rows, dtype=jnp.int32)
    doc_ends = jnp.cumsum(doc_lengths.reshape(-1))
    query_segment = segment_of(query_index, doc_ends)
    cosine_table, sine_table = rope_tables(query_index % SEQ_LEN)
    reach = (WINDOW - 1) // rows + 1
    scale = HD ** (-0.5)
    residual_in = tokens.astype(F32)
    normed_first, inverse_first = rms_forward(residual_in, gain_values[0])
    normed_first = normed_first.astype(BF16)
    query_raw = jnp.dot(normed_first, g_query, preferred_element_type=F32)
    pair_raw = jnp.dot(normed_first, g_pair, preferred_element_type=F32)
    query_rot = (
        rotate(query_raw.reshape(rows, head_count, HD), cosine_table, sine_table) * scale
    ).astype(BF16)
    own_pair = jnp.where(
        y == 0, rotate(pair_raw[:, None], cosine_table, sine_table)[:, 0], pair_raw
    ).astype(BF16)

    (all_pairs,) = exchange(
        gather_pairs, [own_pair], [((Y, X, C, Z, rows, HD), BF16)], sizes, 2
    )
    all_pairs = jnp.pad(all_pairs.reshape(Y, N * rows, HD), ((0, 0), (reach * rows, 0), (0, 0)))
    near = lax.dynamic_slice_in_dim(all_pairs, start_row, (reach + 1) * rows, 1)
    keys_all, values_all = near[0], near[1]
    key_index = start_row - reach * rows + jnp.arange((reach + 1) * rows, dtype=jnp.int32)
    key_segment = segment_of(key_index, doc_ends)
    allowed = (
        (query_segment[:, None] == key_segment[None, :])
        & (key_index[None, :] <= query_index[:, None])
        & (query_index[:, None] - key_index[None, :] < WINDOW)
        & (key_index[None, :] >= 0)
    )
    scores = jnp.einsum("qhd,kd->hqk", query_rot, keys_all, preferred_element_type=F32)
    scores = jnp.where(allowed[None], scores, -jnp.inf)
    row_top = jnp.max(scores, axis=-1, keepdims=True)
    exp_scores = jnp.exp(scores - row_top)
    row_total = jnp.sum(exp_scores, axis=-1, keepdims=True)
    prob_table = exp_scores / row_total
    log_total = row_top + jnp.log(row_total)
    attended = jnp.einsum(
        "hqk,kd->qhd", prob_table.astype(BF16), values_all, preferred_element_type=F32
    )
    attended_low = attended.reshape(rows, head_count * HD).astype(BF16)
    attention_part = lax.dot_general(
        attended_low, g_out, CONTRACT_LAST, preferred_element_type=F32
    ).reshape(Y, half, D)

    (part_in,) = exchange(
        swap_y, [pick(attention_part, 1 - y).astype(BF16)], [((half, D), BF16)], sizes, 3
    )
    middle = (
        pick(residual_in.reshape(Y, half, D), y) + pick(attention_part, y) + part_in.astype(F32)
    )
    normed_second, inverse_second = rms_forward(middle, gain_values[1])
    normed_all, g_down = exchange(
        functools.partial(gather_rows, width),
        [normed_second.astype(BF16), down_block],
        [((C, Z, half, D), BF16), ((X, C, Z, rows_w, Y * width), BF16)],
        sizes,
        4,
    )
    normed_all = normed_all.reshape(F * half, D)
    g_down = g_down.reshape(D, Y * width)

    gate_pre = jnp.dot(normed_all, g_gate, preferred_element_type=F32)
    up_pre = jnp.dot(normed_all, g_up, preferred_element_type=F32)
    activated, gelu_back = jax.vjp(jax.nn.gelu, gate_pre)
    hidden = (activated * up_pre).astype(BF16)
    feed_part = lax.dot_general(hidden, g_down, CONTRACT_LAST, preferred_element_type=F32)
    hidden_grad = jnp.dot(down_grad, g_down, preferred_element_type=F32)
    gate_grad = gelu_back(hidden_grad * up_pre)[0].astype(BF16)
    up_grad = (hidden_grad * activated).astype(BF16)
    second_part = lax.dot_general(
        gate_grad, g_gate, CONTRACT_LAST, preferred_element_type=F32
    ) + lax.dot_general(up_grad, g_up, CONTRACT_LAST, preferred_element_type=F32)

    def weight_grad(left, right):
        sides = [
            lax.dot_general(
                left,
                right[:, i * width : (i + 1) * width],
                CONTRACT_FIRST,
                preferred_element_type=F32,
            ).astype(BF16)
            for i in range(Y)
        ]
        stacked = jnp.stack(sides).reshape(Y * X, C, Z, rows_w, width)
        mine = lax.psum_scatter(stacked, ("y", "x"), scatter_dimension=0, tiled=True)
        return lax.all_to_all(mine.reshape(F, rows_w, width), ("c", "z"), 0, 0, tiled=True)

    second_part = second_part.astype(BF16).reshape(C, Z, half, D)
    (second_grad,) = exchange(
        sum_rows,
        [second_part],
        [((half, D), F32)],
        sizes,
        5,
        scratch=[((Z, half, D), BF16)] * 2 + [((Z - 1, half, D), BF16)],
        in_vmem=(0,),
    )
    mlp_grads = [
        weight_grad(left, right)
        for left, right in ((normed_all, gate_grad), (normed_all, up_grad), (down_grad, hidden))
    ]
    feed_out = lax.psum_scatter(
        feed_part.astype(BF16), ("c", "z"), scatter_dimension=0, tiled=True
    ).astype(F32)
    mixed_half = middle + feed_out
    mixed_in = lax.ppermute(mixed_half, "y", [(i, (i + 1) % Y) for i in range(Y)])

    def whole(own, other):
        return jnp.where(
            y == 0, jnp.concatenate([own, other]), jnp.concatenate([other, own])
        )

    mixed = whole(mixed_half, mixed_in)

    middle_norm_grad, gain_two = rms_backward(middle, inverse_second, gain_values[1], second_grad)
    middle_grad = cotangent_half + middle_norm_grad
    branch_half = middle_grad.astype(BF16)
    (branch_in,) = exchange(swap_y, [branch_half], [((half, D), BF16)], sizes, 7)
    branch_grad = whole(branch_half, branch_in)
    grad_out = lax.dot_general(
        branch_grad, attended_low, CONTRACT_FIRST, preferred_element_type=F32
    ).astype(BF16)
    attended_grad = jnp.dot(branch_grad, g_out, preferred_element_type=F32).astype(BF16)
    attended_grad = attended_grad.reshape(rows, head_count, HD)
    scores_again = jnp.einsum("qhd,kd->hqk", query_rot, keys_all, preferred_element_type=F32)
    scores_again = jnp.where(allowed[None], scores_again, -jnp.inf)
    prob_again = jnp.exp(scores_again - log_total)
    prob_grad = jnp.einsum("qhd,kd->hqk", attended_grad, values_all, preferred_element_type=F32)
    score_grad = (
        prob_again * (prob_grad - jnp.sum(prob_again * prob_grad, axis=-1, keepdims=True))
    ).astype(BF16)
    query_grad_rot = (
        jnp.einsum("hqk,kd->qhd", score_grad, keys_all, preferred_element_type=F32) * scale
    )
    key_grad_all = jnp.einsum("hqk,qhd->kd", score_grad, query_rot, preferred_element_type=F32)
    value_grad_all = jnp.einsum(
        "hqk,qhd->kd", prob_again.astype(BF16), attended_grad, preferred_element_type=F32
    )
    pair_grad = jnp.stack([key_grad_all, value_grad_all]).astype(BF16)
    (pair_parts,) = exchange(
        functools.partial(return_pairs, reach),
        [pair_grad.reshape(2, reach + 1, rows, HD)],
        [((Y, reach + 1, rows, HD), BF16)],
        sizes,
        8,
    )
    pair_total = jnp.sum(pair_parts.astype(F32), axis=(0, 1))
    pair_total = jnp.where(
        y == 0, rotate(pair_total[:, None], cosine_table, -sine_table)[:, 0], pair_total
    ).astype(BF16)
    query_grad = (
        rotate(query_grad_rot, cosine_table, -sine_table)
        .reshape(rows, head_count * HD)
        .astype(BF16)
    )
    first_part = (
        lax.dot_general(query_grad, g_query, CONTRACT_LAST, preferred_element_type=F32)
        + lax.dot_general(pair_total, g_pair, CONTRACT_LAST, preferred_element_type=F32)
    ).astype(BF16)
    grad_query = lax.dot_general(
        normed_first, query_grad, CONTRACT_FIRST, preferred_element_type=F32
    ).astype(BF16)
    grad_pair = lax.dot_general(
        normed_first, pair_total, CONTRACT_FIRST, preferred_element_type=F32
    ).astype(BF16)
    attention_grads = [
        g.reshape(X, C, Z, rows_w, -1) for g in (grad_query, grad_out, grad_pair)
    ]
    widths = (columns, columns, HD)
    reduced_query, reduced_out, reduced_half, first_in, middle_in, gain_two_parts = exchange(
        sum_weights,
        [
            *attention_grads,
            first_part,
            middle_grad,
            jnp.pad(gain_two.reshape(N, 1, rows_w), ((0, 0), (0, 7), (0, 0))),
        ],
        [((rows_w, w), F32) for w in widths]
        + [((rows, D), BF16), ((half, D), F32), ((Y, N, 8, rows_w), F32)],
        sizes,
        9,
        scratch=[((X, Z, rows_w, w), BF16) for w in widths] * 2
        + [((X - 1, Z, rows_w, w), BF16) for w in widths]
        + [((Z - 1, rows_w, w), BF16) for w in widths],
        in_vmem=(0, 1, 2),
    )
    first_grad = first_part.astype(F32) + first_in.astype(F32)
    input_norm_grad, _ = rms_backward(residual_in, inverse_first, gain_values[0], first_grad)
    token_grad = whole(middle_grad, middle_in) + input_norm_grad
    gain_one = jnp.sum(
        pick((first_grad * residual_in * inverse_first).reshape(Y, half, D), y), axis=0
    )
    half_in, gain_one_parts = exchange(
        finish_small,
        [reduced_half, jnp.pad(gain_one.reshape(N, 1, rows_w), ((0, 0), (0, 7), (0, 0)))],
        [((rows_w, HD), F32), ((Y, N, 8, rows_w), F32)],
        sizes,
        10,
    )
    reduced_gains = jnp.stack(
        [jnp.sum(g, axis=(0, 1))[0] for g in (gain_one_parts, gain_two_parts)]
    )
    reduced_mlp = [
        g.transpose(1, 0, 2).reshape(rows_w, F * width)[:, :mlp_columns].astype(F32)
        for g in mlp_grads
    ]
    reduced_pair = jnp.where(
        y == 0,
        jnp.concatenate([reduced_half, half_in], axis=1),
        jnp.concatenate([half_in, reduced_half], axis=1),
    )
    reduced = (reduced_query, reduced_pair, reduced_out, *reduced_mlp, reduced_gains)
    dense_rate = 2.0 * D ** (-0.5)
    out_rate = 2.0 * max(1, H * HD // 64) ** (-0.5)
    rates = (dense_rate, dense_rate, out_rate, dense_rate, dense_rate, dense_rate, 0.4)
    decays = (DECAY, DECAY, DECAY, DECAY, DECAY, DECAY, 0.0)
    new_firsts = []
    new_seconds = []
    updated = []
    for weight, moment_old, square_old, gradient, rate_step, decay_rate in zip(
        masters, firsts, seconds, reduced, rates, decays
    ):
        moment_new, square_new, weight_new = adam_update(
            weight, moment_old, square_old, gradient, rate_step, decay_rate
        )
        new_firsts.append(moment_new)
        new_seconds.append(square_new)
        updated.append(weight_new)
    return (mixed, token_grad, *new_firsts, *new_seconds, *updated)


def solution(mesh):
    shape = dict(mesh.shape)
    sizes = {"x": shape["dp"] // 2, "c": 2, "z": shape["group"], "y": shape["tensor"]}
    sizes["n"] = sizes["x"] * sizes["c"] * sizes["z"]
    grid = Mesh(mesh.devices.reshape([sizes[a] for a in AXES]), AXES)
    blocks = ("x", "c", "z")
    by_rows, by_both, gains = P(blocks, None), P(blocks, "y"), P(None, blocks)
    weights = (by_both, by_rows, by_both, by_both, by_both, by_both, gains)
    return jax.shard_map(
        functools.partial(body, sizes),
        mesh=grid,
        in_specs=(by_rows, by_rows, P(), *weights * 3),
        out_specs=(by_rows, by_rows, *weights * 3),
        check_vma=False,
    )
```

```python
import functools
import math

import jax
import jax.numpy as jnp
from jax import lax
from jax.experimental import pallas as pl
from jax.experimental.pallas import tpu as pltpu
from jax.sharding import Mesh
from jax.sharding import PartitionSpec as P

D = 2560
H = 10
HD = 256
WINDOW = 2048
SEQ_LEN = 4096
STEP = 10

EPSILON = 1e-06
BETA_ONE = 0.9
BETA_TWO = 0.95
ADAM_EPS = 1e-08
DECAY = 0.1
CONTRACT_LAST = (((1,), (1,)), ((), ()))
CONTRACT_FIRST = (((0,), (0,)), ((), ()))
BF16 = jnp.bfloat16
F32 = jnp.float32
AXES = ("x", "c", "z", "y")


class Blank:
    @property
    def at(self):
        return self

    def __getitem__(self, _):
        return self

    def landed(self):
        pass


def guarded(condition, step):
    if condition is None:
        step()
    else:
        pl.when(condition)(step)


class Copy:
    def __init__(self, copy, sends, comes):
        self.copy, self.sends, self.comes, self.arrived = copy, sends, comes, False

    def landed(self):
        if not self.arrived:
            guarded(self.comes, self.copy.wait_recv)
            self.arrived = True

    def done(self):
        self.landed()
        guarded(self.sends, self.copy.wait_send)


class Local:
    def __init__(self, copy):
        self.copy, self.arrived = copy, False

    def landed(self):
        if not self.arrived:
            self.copy.wait()
            self.arrived = True

    def done(self):
        self.landed()


class Net:
    def __init__(self, sizes, me, sems):
        self.sizes, self.me, self.sems = sizes, me, sems
        self.sent, self.kept, self.peers, self.open = 0, 0, [], []

    def device(self, where):
        s, me = self.sizes, self.me
        if len(where) == 4:
            return {a: lax.rem(me[a] + d, s[a]) for a, d in zip(AXES, where)}
        flat = lax.rem((me["x"] * s["c"] + me["c"]) * s["z"] + me["z"] + where[0], s["n"])
        return {
            "x": flat // (s["c"] * s["z"]),
            "c": lax.rem(flat // s["z"], s["c"]),
            "z": lax.rem(flat, s["z"]),
            "y": lax.rem(me["y"] + where[1], s["y"]),
        }

    def opposite(self, where):
        if len(where) == 4:
            return tuple((self.sizes[a] - d) % self.sizes[a] for a, d in zip(AXES, where))
        return ((self.sizes["n"] - where[0]) % self.sizes["n"], (self.sizes["y"] - where[1]) % self.sizes["y"])

    def send(self, src, dst, where, sends=None, comes=None, now=True):
        k = self.sent
        self.sent += 1
        if self.sems is None:
            for w in (where, self.opposite(where)):
                if w not in self.peers:
                    self.peers.append(w)
            return Blank()
        copy = pltpu.make_async_remote_copy(
            src_ref=src,
            dst_ref=dst,
            send_sem=self.sems[0].at[k],
            recv_sem=self.sems[1].at[k],
            device_id=self.device(where),
            device_id_type=pl.DeviceIdType.MESH,
        )
        self.open.append(Copy(copy, sends, comes))
        if now:
            guarded(sends, copy.start)
        return self.open[-1]

    def keep(self, src, dst):
        k = self.kept
        self.kept += 1
        if self.sems is None:
            return Blank()
        copy = pltpu.make_async_copy(src, dst, self.sems[2].at[k])
        copy.start()
        self.open.append(Local(copy))
        return self.open[-1]

    def add(self, rows, step):
        if self.sems is not None:
            some = 16 if rows % 16 == 0 else rows

            def one(i, carry):
                step(pl.ds(pl.multiple_of(i * some, some), some))
                return carry

            lax.fori_loop(0, rows // some, one, 0)

    def greet(self, peers):
        barrier = pltpu.get_barrier_semaphore()
        for where in peers:
            pl.semaphore_signal(
                barrier, inc=1, device_id=self.device(where), device_id_type=pl.DeviceIdType.MESH
            )
        pl.semaphore_wait(barrier, len(peers))

    def finish(self):
        for item in self.open:
            item.done()


def exchange(plan, arrays, outs, sizes, number, micros, scratch=(), in_vmem=()):
    count = Net(sizes, {a: 0 for a in AXES}, None)
    plan(count, *[Blank()] * (len(arrays) + len(outs) + len(scratch)))

    def kernel(*refs):
        data, sems = refs[:-3], refs[-3:]
        net = Net(sizes, {a: lax.axis_index(a) for a in AXES}, sems)
        net.greet(count.peers)
        plan(net, *data)
        net.finish()

    anywhere = pl.BlockSpec(memory_space=pl.ANY)
    inside = pl.BlockSpec(memory_space=pltpu.VMEM)
    return pl.pallas_call(
        kernel,
        out_shape=[jax.ShapeDtypeStruct(shape, dtype) for shape, dtype in outs],
        in_specs=[anywhere] * len(arrays),
        out_specs=[inside if i in in_vmem else anywhere for i in range(len(outs))],
        scratch_shapes=[
            *(pltpu.VMEM(shape, dtype) for shape, dtype in scratch),
            pltpu.SemaphoreType.DMA((count.sent,)),
            pltpu.SemaphoreType.DMA((count.sent,)),
            pltpu.SemaphoreType.DMA((max(1, count.kept),)),
        ],
        compiler_params=pltpu.CompilerParams(
            collective_id=number, has_side_effects=True, vmem_limit_bytes=48 * 2**20
        ),
        cost_estimate=pl.CostEstimate(
            flops=0, bytes_accessed=micros * 3_600_000, transcendentals=0
        ),
    )(*arrays)


SIBLING = (0, 1, 0, 0)
OTHER_Y = (0, 0, 0, 1)


def back(value, step, size):
    return lax.rem(value + size - step, size)


def along_line(net, pairs):
    z, size = net.me["z"], net.sizes["z"]

    def up(pair, step):
        slot = pair[1](back(z, step, size))
        return net.send(
            slot if step else pair[0],
            slot,
            (0, 0, 1, 0),
            sends=(z + 1 < size) & (z - step >= 0),
            comes=z - 1 - step >= 0,
        )

    def down(pair, step):
        slot = pair[1](lax.rem(z + step, size))
        return net.send(
            slot if step else pair[0],
            slot,
            (0, 0, size - 1, 0),
            sends=(z >= 1) & (z + step < size),
            comes=z + 1 + step < size,
        )

    moves = [(up(pair, 0), down(pair, 0)) for pair in pairs]

    def steps():
        for step in range(size - 1):
            for i, pair in enumerate(pairs):
                rising, falling = moves[i]
                rising.landed()
                if step + 1 < size - 1:
                    rising = up(pair, step + 1)
                yield i, (back(z, step + 1, size), z - 1 - step >= 0)
                falling.landed()
                if step + 1 < size - 1:
                    falling = down(pair, step + 1)
                yield i, (lax.rem(z + step + 1, size), z + 1 + step < size)
                moves[i] = (rising, falling)

    return steps()


def gather_x_c_z(net, pairs):
    x, c, z = (net.me[a] for a in "xcz")
    xs = net.sizes["x"]
    line = along_line(net, [(src, lambda j, dst=dst: dst.at[x, c, j]) for src, dst in pairs])
    across = []

    def onward(src, slot, condition):
        for dx in range(1, xs):
            copy = net.send(src, slot(x), (dx, 0, 0, 0), sends=condition, comes=condition)
            across.append((copy, slot(back(x, dx, xs)), condition))
        net.send(src, slot(x), SIBLING, sends=condition, comes=condition)

    for src, dst in pairs:
        net.keep(src, dst.at[x, c, z])
        onward(src, lambda px, dst=dst: dst.at[px, c, z], None)
    yield
    for count, (i, (j, condition)) in enumerate(line):
        dst = pairs[i][1]
        onward(dst.at[x, c, j], lambda px, dst=dst, j=j: dst.at[px, c, j], condition)
        if count % (2 * len(pairs)) == 2 * len(pairs) - 1:
            yield
    for copy, slot, condition in across:
        copy.landed()
        net.send(slot, slot, SIBLING, sends=condition, comes=condition)


def gather_small(net, *refs):
    for _ in gather_x_c_z(net, list(zip(refs[:2], refs[2:]))):
        pass


def gather_weights(width, net, *refs):
    x, c, z, y = (net.me[a] for a in AXES)
    xs, cs, zs = (net.sizes[a] for a in "xcz")
    gate, up, gate_out, up_out = *refs[2:4], *refs[6:8]
    mine = pl.ds(y * width, width)

    def part(src, f):
        return src.at[:, pl.ds(f * width, width)]

    def scatter(src, slot):
        got = []
        for dz in range(zs):
            for dc in range(cs):
                if dz or dc:
                    f = lax.rem(c + dc, cs) * zs + lax.rem(z + dz, zs)
                    copy = net.send(part(src, f), slot(c, z), (0, dc, dz, 0))
                    got.append((copy, slot(back(c, dc, cs), back(z, dz, zs))))
        return got

    def spread(src, slot, got):
        own = part(src, c * zs + z)
        net.keep(own, slot(c, z))
        across = [[net.send(own, slot(c, z), (dx, 0, 0, 0))] for dx in range(1, xs)]
        net.send(own, slot(c, z), OTHER_Y)
        for copy, ref in got:
            copy.landed()
            for dx in range(1, xs):
                across[dx - 1].append(net.send(ref, ref, (dx, 0, 0, 0)))
            net.send(ref, ref, OTHER_Y)
        return across

    def relay(dst, across):
        for dx in range(1, xs):
            for copy in across[dx - 1]:
                copy.landed()
            for i in range(cs):
                block = dst.at[back(x, dx, xs), i, :, :, mine]
                net.send(block, block, OTHER_Y)

    def gate_slot(i, j):
        return gate_out.at[x, i, j, :, mine]

    def up_slot(i, j):
        return up_out.at[x, i, j, :, mine]

    got_gate = scatter(gate, gate_slot)
    weights = gather_x_c_z(net, [(refs[0], refs[4]), (refs[1], refs[5])])
    next(weights)
    over_gate = spread(gate, gate_slot, got_gate)
    got_up = scatter(up, up_slot)
    next(weights)
    over_up = spread(up, up_slot, got_up)
    relay(gate_out, over_gate)
    for _ in weights:
        pass
    relay(up_out, over_up)


def gather_rows(width, net, rows, block, all_rows, all_blocks):
    x, c, z, y = (net.me[a] for a in AXES)
    xs, cs, ys = (net.sizes[a] for a in "xcy")
    line = along_line(net, [(rows, lambda j: all_rows.at[c, j])])
    next_x, next_y = [], []
    for i in range(cs):

        def slot(px, py, i=i):
            return all_blocks.at[px, i, :, :, pl.ds(py * width, width)]

        net.keep(block.at[i], slot(x, y))
        for dx in range(1, xs):
            copy = net.send(block.at[i], slot(x, y), (dx, 0, 0, 0))
            if i % 2 == 0:
                next_y.append((copy, slot(back(x, dx, xs), y)))
        copy = net.send(block.at[i], slot(x, y), OTHER_Y)
        if i % 2 == 1:
            next_x.append((copy, slot(x, back(y, 1, ys))))
    net.keep(rows, all_rows.at[c, z])
    net.send(rows, all_rows.at[c, z], SIBLING)
    for step, (_, (j, condition)) in enumerate(line):
        slot = all_rows.at[c, j]
        net.send(slot, slot, SIBLING, sends=condition, comes=condition)
        if step == 1:
            for copy, slot in next_y:
                copy.landed()
                net.send(slot, slot, OTHER_Y)
            for copy, slot in next_x:
                copy.landed()
                for dx in range(1, xs):
                    net.send(slot, slot, (dx, 0, 0, 0))


def together(net, *plans):
    plans = list(plans)
    while plans:
        for plan in list(plans):
            if next(plan, plans) is plans:
                plans.remove(plan)


def far_first(size):
    return sorted(range(size), key=lambda d: -min(d, size - d))


def ends_first(size):
    return sorted(range(size), key=lambda t: min(t, size - 1 - t))


def add_low(net, target, other, rows):
    def step(at):
        target[at] = (target[at].astype(F32) + other[at].astype(F32)).astype(BF16)

    net.add(rows, step)


def sum_along_line(net, own, rising, falling, rows):
    z, size = net.me["z"], net.sizes["z"]
    ups = [(t, True) for t in range(size - 1, 0, -1)]
    downs = [(t, False) for t in range(size - 1)]
    copies = {}
    for t, up in ups + downs:
        copies[t, up] = net.send(
            own.at[t],
            (rising if up else falling).at[t],
            (0, 0, 1 if up else size - 1, 0),
            sends=(z < t) if up else (z > t),
            comes=((z > 0) & (z <= t)) if up else ((z < size - 1) & (z >= t)),
            now=False,
        )

    def take(t, up):
        copies[t, up].copy.wait_recv()
        add_low(net, own.at[t], (rising if up else falling).at[t], rows)

    def move(t, up):
        inner = ((z > 0) & (z < t)) if up else ((z < size - 1) & (z > t))
        pl.when(inner)(lambda: take(t, up))
        pl.when((z < t) if up else (z > t))(copies[t, up].copy.start)

    for first, second in zip(ups + downs, downs + ups):
        if net.sems is not None:
            pl.when(z < size // 2)(lambda: move(*first))
            pl.when(z >= size // 2)(lambda: move(*second))
        yield
    for t, up in ups + downs:
        if net.sems is not None:
            last = (z == t) & ((z > 0) if up else (z < size - 1))
            pl.when(last)(lambda: take(t, up))
            copies[t, up].arrived = True
        yield


def sum_rows(net, part, out, own, got, rising, falling):
    c, z = net.me["c"], net.me["z"]
    zs = net.sizes["z"]
    rows = 0 if net.sems is None else out.shape[0]
    ready = {}
    for t in ends_first(zs):
        ready[t] = (
            net.send(part.at[lax.rem(c + 1, net.sizes["c"]), t], got.at[t], SIBLING),
            net.keep(part.at[c, t], own.at[t]),
        )
    yield
    for t in ends_first(zs):
        for copy in ready[t]:
            copy.landed()
        add_low(net, own.at[t], got.at[t], rows)
    yield from sum_along_line(net, own, rising, falling, rows)

    def result(at):
        out[at] = own[z, at].astype(F32)

    net.add(rows, result)


def sum_weights(net, *refs):
    x, c, z, y = (net.me[a] for a in AXES)
    xs, cs, zs = (net.sizes[a] for a in "xcz")
    sources, swapped, gains = refs[0:3], refs[3:6], refs[6]
    outs, swapped_out, gains_out, other_pair = refs[7:10], refs[10:13], refs[13], refs[14]
    own, got, from_x, from_z = (refs[15 + 3 * i : 18 + 3 * i] for i in range(4))
    rows = 0 if net.sems is None else outs[0].shape[0]
    order = far_first(zs)
    ready = {}
    for dx in [*range(1, xs), 0]:
        i = lax.rem(x + dx, xs)
        for dz in order:
            j = lax.rem(z + dz, zs)
            for k in range(3):
                ready[dx, dz, k] = (
                    net.send(
                        sources[k].at[i, lax.rem(c + 1, cs), j], got[k].at[i, j], SIBLING
                    ),
                    net.keep(sources[k].at[i, c, j], own[k].at[i, j]),
                )
    for src, dst in zip(swapped, swapped_out):
        net.send(src, dst, OTHER_Y)
    gains_to_owners(net, gains, gains_out)
    over = {}
    for dx in range(1, xs):
        i = lax.rem(x + dx, xs)
        for dz in order:
            j = lax.rem(z + dz, zs)
            for k in range(3):
                for copy in ready[dx, dz, k]:
                    copy.landed()

                def pair(at, mine=own[k], other=got[k], i=i, j=j):
                    mine[i, j, at] = (
                        mine[i, j, at].astype(F32) + other[i, j, at].astype(F32)
                    ).astype(BF16)

                net.add(rows, pair)
                over[dx, dz, k] = net.send(
                    own[k].at[i, j], from_x[k].at[dx - 1, j], (dx, 0, 0, 0)
                )
    sent = {}
    for dz in order:
        j = lax.rem(z + dz, zs)
        for k in range(3):
            for copy in ready[0, dz, k]:
                copy.landed()
            for dx in range(1, xs):
                over[dx, dz, k].landed()

            def chips(at, mine=own[k], other=got[k], far=from_x[k], j=j):
                total = mine[x, j, at].astype(F32) + other[x, j, at].astype(F32)
                for dx in range(1, xs):
                    total = total + far[dx - 1, j, at].astype(F32)
                return total

            if dz:

                def keep_low(at, mine=own[k], chips=chips, j=j):
                    mine[x, j, at] = chips(at).astype(BF16)

                net.add(rows, keep_low)
                sent[dz, k] = net.send(own[k].at[x, j], from_z[k].at[dz - 1], (0, 0, dz, 0))
            else:

                def keep_wide(at, out=outs[k], chips=chips):
                    out[at] = chips(at)

                net.add(rows, keep_wide)
    for k in (2, 0, 1):
        for dz in order[:-1]:
            sent[dz, k].landed()

            def more(at, out=outs[k], far=from_z[k], dz=dz):
                out[at] += far[dz - 1, at].astype(F32)

            net.add(rows, more)
        if k == 2:
            net.send(outs[2], other_pair, OTHER_Y)


def swap_y(net, *refs):
    count = len(refs) // 2
    for src, dst in zip(refs[:count], refs[count:]):
        net.send(src, dst, OTHER_Y)


def return_pairs(reach, net, src, out, own, got):
    y, n = net.me["y"], net.sizes["n"]
    rows = 0 if net.sems is None else out.shape[1]
    ready = {}
    for offset in range(reach, -1, -1):
        j = reach - offset
        ready[j] = (
            net.send(src.at[back(y, 1, net.sizes["y"]), j], got.at[j], OTHER_Y),
            net.keep(src.at[y, j], own.at[j]),
        )
    yield
    for offset in range(reach, -1, -1):
        j = reach - offset
        for copy in ready[j]:
            copy.landed()

        def both(at, j=j):
            own[j, at] = (own[j, at].astype(F32) + got[j, at].astype(F32)).astype(BF16)

        net.add(rows, both)
        if offset:
            net.send(own.at[j], out.at[offset], ((n - offset) % n, 0))
            yield
        else:
            net.keep(own.at[j], out.at[0])


def sum_second(net, *refs):
    together(net, sum_rows(net, *refs))


def return_pairs_sum_feed(reach, net, pairs, feed, pairs_out, feed_out, *scratch):
    together(
        net,
        return_pairs(reach, net, pairs, pairs_out, *scratch[:2]),
        sum_rows(net, feed, feed_out, *scratch[2:]),
    )


def gains_to_owners(net, gains, gains_out):
    x, c, z, y = (net.me[a] for a in AXES)
    n = net.sizes["n"]
    me = (x * net.sizes["c"] + c) * net.sizes["z"] + z
    for offset in range(n):
        for dy in range(net.sizes["y"]):
            slot, piece = gains_out.at[y, me], gains.at[lax.rem(me + offset, n)]
            if offset == 0 and dy == 0:
                net.keep(piece, slot)
            else:
                net.send(piece, slot, (offset, dy))


def rms_forward(values, gain_row):
    inverse = lax.rsqrt(jnp.mean(values * values, axis=-1, keepdims=True) + EPSILON)
    return (values * inverse * gain_row, inverse)


def rms_backward(values, inverse, gain_row, incoming):
    scaled = incoming * gain_row
    gain_grad = jnp.sum(incoming * values * inverse, axis=0)
    value_grad = inverse * scaled - values * inverse * inverse * inverse * jnp.mean(
        scaled * values, axis=-1, keepdims=True
    )
    return (value_grad, gain_grad)


def rope_tables(positions):
    quarter = HD // 4
    freqs = jnp.exp(-math.log(10000.0) * jnp.arange(quarter, dtype=jnp.float32) * 2.0 / (HD // 2))
    angles = positions.astype(jnp.float32)[:, None] * freqs[None, :]
    return (jnp.cos(angles), jnp.sin(angles))


def rotate(values, cosine_table, sine_table):
    quarter = cosine_table.shape[1]
    lead_part = values[..., :quarter]
    pair_part = values[..., quarter : 2 * quarter]
    tail_part = values[..., 2 * quarter :]
    cos_wide = cosine_table[:, None, :]
    sin_wide = sine_table[:, None, :]
    return jnp.concatenate(
        [
            lead_part * cos_wide - pair_part * sin_wide,
            pair_part * cos_wide + lead_part * sin_wide,
            tail_part,
        ],
        axis=-1,
    )


def segment_of(index, doc_ends):
    return jnp.sum((doc_ends[None, :] <= index[:, None]).astype(jnp.int32), axis=1)


def adam_update(weight, moment_old, square_old, gradient, rate_step, decay_rate):
    moment_new = BETA_ONE * moment_old + (1.0 - BETA_ONE) * gradient
    square_new = BETA_TWO * square_old + (1.0 - BETA_TWO) * gradient * gradient
    corrected = moment_new / (1.0 - BETA_ONE**STEP)
    corrected_square = square_new / (1.0 - BETA_TWO**STEP)
    weight_new = weight - rate_step * (
        corrected / (jnp.sqrt(corrected_square) + ADAM_EPS) + decay_rate * weight
    )
    return (moment_new, square_new, weight_new)


def body(
    sizes,
    tokens,
    cotangent,
    doc_lengths,
    w_query,
    w_keyvalue,
    w_out,
    w_gate,
    w_up,
    w_down,
    norm_gains,
    first_query,
    first_keyvalue,
    first_out,
    first_gate,
    first_up,
    first_down,
    first_gains,
    second_query,
    second_keyvalue,
    second_out,
    second_gate,
    second_up,
    second_down,
    second_gains,
):
    masters = (w_query, w_keyvalue, w_out, w_gate, w_up, w_down, norm_gains)
    firsts = (first_query, first_keyvalue, first_out, first_gate, first_up, first_down, first_gains)
    seconds = (
        second_query,
        second_keyvalue,
        second_out,
        second_gate,
        second_up,
        second_down,
        second_gains,
    )
    x, c, z, y = (lax.axis_index(a) for a in AXES)
    X, C, Z, Y, N = (sizes[a] for a in (*AXES, "n"))
    F = C * Z
    rows_w = w_query.shape[0]
    columns = w_query.shape[1]
    rows = tokens.shape[0]
    half = rows // Y
    head_count = columns // HD
    mlp_columns = w_gate.shape[1]
    width = -(-mlp_columns // (F * 128)) * 128
    device = (x * C + c) * Z + z

    def pick(values, index):
        return lax.dynamic_index_in_dim(values, index, 0, keepdims=False)

    def after(value, *others):
        return lax.optimization_barrier((value, *others))[0]

    def pieces(weight):
        return jnp.pad(weight.astype(BF16), ((0, 0), (0, F * width - mlp_columns)))

    low_gains = jnp.pad(norm_gains.astype(BF16).astype(F32), ((0, 6), (0, 0)))
    pair_weight = lax.dynamic_slice_in_dim(w_keyvalue, y * HD, HD, 1).astype(BF16)
    g_pair, g_gains = exchange(
        gather_small,
        [pair_weight, low_gains],
        [((X, C, Z, rows_w, HD), BF16), ((X, C, Z, 8, rows_w), F32)],
        sizes,
        2,
        18,
    )
    g_pair = g_pair.reshape(D, HD)
    gain_values = g_gains.reshape(N, 8, rows_w)[:, :2].transpose(1, 0, 2).reshape(2, D)
    start_row = device * rows
    query_index = start_row + jnp.arange(rows, dtype=jnp.int32)
    doc_ends = jnp.cumsum(doc_lengths.reshape(-1))
    query_segment = segment_of(query_index, doc_ends)
    cosine_table, sine_table = rope_tables(query_index % SEQ_LEN)
    reach = (WINDOW - 1) // rows + 1
    scale = HD ** (-0.5)
    residual_in = tokens.astype(F32)
    normed_first, inverse_first = rms_forward(residual_in, gain_values[0])
    normed_first = normed_first.astype(BF16)
    pair_raw = jnp.dot(normed_first, g_pair, preferred_element_type=F32)
    own_pair = jnp.where(
        y == 0, rotate(pair_raw[:, None], cosine_table, sine_table)[:, 0], pair_raw
    ).astype(BF16)

    all_pairs = lax.all_gather(own_pair, ("y", "x", "c", "z"), axis=0)
    g_query, g_out, g_gate, g_up = exchange(
        functools.partial(gather_weights, width),
        [after(w_query.astype(BF16), own_pair), w_out.astype(BF16), pieces(w_gate), pieces(w_up)],
        [((X, C, Z, rows_w, columns), BF16)] * 2
        + [((X, C, Z, rows_w, Y * width), BF16)] * 2,
        sizes,
        1,
        150,
    )
    g_query, g_out = g_query.reshape(D, columns), g_out.reshape(D, columns)
    g_gate, g_up = g_gate.reshape(D, Y * width), g_up.reshape(D, Y * width)
    cotangent_half = pick(cotangent.reshape(Y, half, D), y)
    down_block = pieces(w_down).reshape(rows_w, F, width).transpose(1, 0, 2)
    down_block, down_grad = lax.optimization_barrier(
        (down_block, cotangent_half.astype(BF16), g_out)
    )[:2]
    down_block = lax.all_to_all(down_block, ("c", "z"), 0, 0, tiled=True)
    down_grad = lax.all_gather(down_grad, ("c", "z"), axis=0, tiled=True)

    query_raw = lax.optimization_barrier(
        jnp.dot(normed_first, g_query, preferred_element_type=F32)
    )
    query_rot = (
        rotate(query_raw.reshape(rows, head_count, HD), cosine_table, sine_table) * scale
    ).astype(BF16)
    all_pairs = jnp.pad(all_pairs.reshape(Y, N * rows, HD), ((0, 0), (reach * rows, 0), (0, 0)))
    near = lax.dynamic_slice_in_dim(all_pairs, start_row, (reach + 1) * rows, 1)
    keys_all, values_all = near[0], near[1]
    key_index = start_row - reach * rows + jnp.arange((reach + 1) * rows, dtype=jnp.int32)
    key_segment = segment_of(key_index, doc_ends)
    allowed = (
        (query_segment[:, None] == key_segment[None, :])
        & (key_index[None, :] <= query_index[:, None])
        & (query_index[:, None] - key_index[None, :] < WINDOW)
        & (key_index[None, :] >= 0)
    )
    scores = jnp.einsum("qhd,kd->hqk", query_rot, keys_all, preferred_element_type=F32)
    scores = jnp.where(allowed[None], scores, -jnp.inf)
    row_top = jnp.max(scores, axis=-1, keepdims=True)
    exp_scores = jnp.exp(scores - row_top)
    row_total = jnp.sum(exp_scores, axis=-1, keepdims=True)
    prob_table = exp_scores / row_total
    log_total = row_top + jnp.log(row_total)
    attended = jnp.einsum(
        "hqk,kd->qhd", prob_table.astype(BF16), values_all, preferred_element_type=F32
    )
    attended_low = attended.reshape(rows, head_count * HD).astype(BF16)
    attention_part = lax.dot_general(
        attended_low, g_out, CONTRACT_LAST, preferred_element_type=F32
    ).reshape(Y, half, D)

    (part_in,) = exchange(
        swap_y, [pick(attention_part, 1 - y).astype(BF16)], [((half, D), BF16)], sizes, 3, 17
    )
    middle = (
        pick(residual_in.reshape(Y, half, D), y) + pick(attention_part, y) + part_in.astype(F32)
    )
    normed_second, inverse_second = rms_forward(middle, gain_values[1])
    normed_all, g_down = exchange(
        functools.partial(gather_rows, width),
        [normed_second.astype(BF16), down_block.reshape(C, Z, rows_w, width)],
        [((C, Z, half, D), BF16), ((X, C, Z, rows_w, Y * width), BF16)],
        sizes,
        4,
        60,
    )
    normed_all = normed_all.reshape(F * half, D)
    g_down = g_down.reshape(D, Y * width)

    gate_pre = jnp.dot(normed_all, g_gate, preferred_element_type=F32)
    up_pre = jnp.dot(normed_all, g_up, preferred_element_type=F32)
    activated, gelu_back = jax.vjp(jax.nn.gelu, gate_pre)
    hidden = (activated * up_pre).astype(BF16)
    feed_part = lax.dot_general(
        hidden, g_down, CONTRACT_LAST, preferred_element_type=F32
    ).astype(BF16)
    hidden_grad = jnp.dot(down_grad, g_down, preferred_element_type=F32)
    gate_grad = gelu_back(hidden_grad * up_pre)[0].astype(BF16)
    up_grad = (hidden_grad * activated).astype(BF16)
    second_part = lax.dot_general(
        gate_grad, g_gate, CONTRACT_LAST, preferred_element_type=F32
    ) + lax.dot_general(up_grad, g_up, CONTRACT_LAST, preferred_element_type=F32)

    def weight_grad(left, right):
        sides = [
            lax.dot_general(
                left,
                right[:, i * width : (i + 1) * width],
                CONTRACT_FIRST,
                preferred_element_type=F32,
            ).astype(BF16)
            for i in range(Y)
        ]
        return jnp.stack(sides).reshape(Y * X, C, Z, rows_w, width)

    whole_down = weight_grad(down_grad, hidden)
    whole_gate = weight_grad(normed_all, gate_grad)
    whole_up = weight_grad(normed_all, up_grad)

    def over_y_x(whole_grad):
        return lax.psum_scatter(
            whole_grad, ("y", "x"), scatter_dimension=0, tiled=True
        ).reshape(F, rows_w, width)

    def to_owners(grad, *others):
        return lax.all_to_all(after(grad, *others), ("c", "z"), 0, 0, tiled=True)

    part_down, part_gate, part_up = (over_y_x(g) for g in (whole_down, whole_gate, whole_up))

    second_part = after(second_part.astype(BF16), whole_down, whole_gate)
    (second_grad,) = exchange(
        sum_second,
        [second_part.reshape(C, Z, half, D)],
        [((half, D), F32)],
        sizes,
        5,
        60,
        scratch=[((Z, half, D), BF16)] * 4,
        in_vmem=(0,),
    )

    def whole(own, other):
        return jnp.where(
            y == 0, jnp.concatenate([own, other]), jnp.concatenate([other, own])
        )

    middle_norm_grad, gain_two = rms_backward(middle, inverse_second, gain_values[1], second_grad)
    middle_grad = cotangent_half + middle_norm_grad
    branch_half = middle_grad.astype(BF16)
    (branch_in,) = exchange(swap_y, [branch_half], [((half, D), BF16)], sizes, 7, 17)
    branch_grad = whole(branch_half, branch_in)
    new_down = to_owners(part_down, second_grad)
    grad_out = lax.dot_general(
        branch_grad, attended_low, CONTRACT_FIRST, preferred_element_type=F32
    ).astype(BF16)
    attended_grad = jnp.dot(branch_grad, g_out, preferred_element_type=F32).astype(BF16)
    new_gate = to_owners(part_gate, attended_grad)
    attended_grad = attended_grad.reshape(rows, head_count, HD)
    scores_again = jnp.einsum("qhd,kd->hqk", query_rot, keys_all, preferred_element_type=F32)
    scores_again = jnp.where(allowed[None], scores_again, -jnp.inf)
    prob_again = jnp.exp(scores_again - log_total)
    prob_grad = jnp.einsum("qhd,kd->hqk", attended_grad, values_all, preferred_element_type=F32)
    score_grad = (
        prob_again * (prob_grad - jnp.sum(prob_again * prob_grad, axis=-1, keepdims=True))
    ).astype(BF16)
    query_grad_rot = (
        jnp.einsum("hqk,kd->qhd", score_grad, keys_all, preferred_element_type=F32) * scale
    )
    key_grad_all = jnp.einsum("hqk,qhd->kd", score_grad, query_rot, preferred_element_type=F32)
    value_grad_all = jnp.einsum(
        "hqk,qhd->kd", prob_again.astype(BF16), attended_grad, preferred_element_type=F32
    )
    pair_grad = jnp.stack([key_grad_all, value_grad_all]).astype(BF16)
    pair_grad = after(pair_grad, new_down, new_gate)
    pair_parts, feed_out = exchange(
        functools.partial(return_pairs_sum_feed, reach),
        [pair_grad.reshape(2, reach + 1, rows, HD), feed_part.reshape(C, Z, half, D)],
        [((reach + 1, rows, HD), BF16), ((half, D), F32)],
        sizes,
        8,
        70,
        scratch=[((reach + 1, rows, HD), BF16)] * 2
        + [((Z, half, D), BF16)] * 4,
        in_vmem=(1,),
    )
    mixed_half = middle + feed_out
    pair_total = jnp.sum(pair_parts.astype(F32), axis=0)
    new_up = to_owners(part_up, key_grad_all)
    pair_total = jnp.where(
        y == 0, rotate(pair_total[:, None], cosine_table, -sine_table)[:, 0], pair_total
    ).astype(BF16)
    query_grad = (
        rotate(query_grad_rot, cosine_table, -sine_table)
        .reshape(rows, head_count * HD)
        .astype(BF16)
    )
    first_part = (
        lax.dot_general(query_grad, g_query, CONTRACT_LAST, preferred_element_type=F32)
        + lax.dot_general(pair_total, g_pair, CONTRACT_LAST, preferred_element_type=F32)
    )
    gain_one = jnp.sum(first_part * residual_in * inverse_first, axis=0)
    first_part = after(first_part.astype(BF16), new_up)
    grad_gains = jnp.pad(
        jnp.stack([gain_one, gain_two]).reshape(2, N, rows_w).transpose(1, 0, 2),
        ((0, 0), (0, 6), (0, 0)),
    )
    grad_query = lax.dot_general(
        normed_first, query_grad, CONTRACT_FIRST, preferred_element_type=F32
    ).astype(BF16)
    grad_pair = lax.dot_general(
        normed_first, pair_total, CONTRACT_FIRST, preferred_element_type=F32
    ).astype(BF16)
    attention_grads = [
        g.reshape(X, C, Z, rows_w, -1) for g in (grad_query, grad_out, grad_pair)
    ]
    widths = (columns, columns, HD)
    (
        reduced_query,
        reduced_out,
        reduced_half,
        first_in,
        middle_in,
        mixed_in,
        gain_parts,
        half_in,
    ) = exchange(
        sum_weights,
        [
            *attention_grads,
            first_part,
            middle_grad,
            mixed_half,
            grad_gains,
        ],
        [((rows_w, w), F32) for w in widths]
        + [((rows, D), BF16), ((half, D), F32), ((half, D), F32), ((Y, N, 8, rows_w), F32)]
        + [((rows_w, HD), F32)],
        sizes,
        9,
        110,
        scratch=[((X, Z, rows_w, w), BF16) for w in widths] * 2
        + [((X - 1, Z, rows_w, w), BF16) for w in widths]
        + [((Z - 1, rows_w, w), BF16) for w in widths],
        in_vmem=(0, 1, 2),
    )
    first_grad = first_part.astype(F32) + first_in.astype(F32)
    input_norm_grad, _ = rms_backward(residual_in, inverse_first, gain_values[0], first_grad)
    token_grad = whole(middle_grad, middle_in) + input_norm_grad
    mixed = whole(mixed_half, mixed_in)
    reduced_gains = jnp.sum(gain_parts, axis=(0, 1))[:2]
    reduced_mlp = [
        g.transpose(1, 0, 2).reshape(rows_w, F * width)[:, :mlp_columns].astype(F32)
        for g in (new_gate, new_up, new_down)
    ]
    reduced_pair = jnp.where(
        y == 0,
        jnp.concatenate([reduced_half, half_in], axis=1),
        jnp.concatenate([half_in, reduced_half], axis=1),
    )
    reduced = (reduced_query, reduced_pair, reduced_out, *reduced_mlp, reduced_gains)
    dense_rate = 2.0 * D ** (-0.5)
    out_rate = 2.0 * max(1, H * HD // 64) ** (-0.5)
    rates = (dense_rate, dense_rate, out_rate, dense_rate, dense_rate, dense_rate, 0.4)
    decays = (DECAY, DECAY, DECAY, DECAY, DECAY, DECAY, 0.0)
    new_firsts = []
    new_seconds = []
    updated = []
    for weight, moment_old, square_old, gradient, rate_step, decay_rate in zip(
        masters, firsts, seconds, reduced, rates, decays
    ):
        moment_new, square_new, weight_new = adam_update(
            weight, moment_old, square_old, gradient, rate_step, decay_rate
        )
        new_firsts.append(moment_new)
        new_seconds.append(square_new)
        updated.append(weight_new)
    return (mixed, token_grad, *new_firsts, *new_seconds, *updated)


def solution(mesh):
    shape = dict(mesh.shape)
    sizes = {"x": shape["dp"] // 2, "c": 2, "z": shape["group"], "y": shape["tensor"]}
    sizes["n"] = sizes["x"] * sizes["c"] * sizes["z"]
    grid = Mesh(mesh.devices.reshape([sizes[a] for a in AXES]), AXES)
    blocks = ("x", "c", "z")
    by_rows, by_both, gains = P(blocks, None), P(blocks, "y"), P(None, blocks)
    weights = (by_both, by_rows, by_both, by_both, by_both, by_both, gains)
    return jax.shard_map(
        functools.partial(body, sizes),
        mesh=grid,
        in_specs=(by_rows, by_rows, P(), *weights * 3),
        out_specs=(by_rows, by_rows, *weights * 3),
        check_vma=False,
    )
```

```python
import functools
import math

import jax
import jax.numpy as jnp
from jax import lax
from jax.experimental import pallas as pl
from jax.experimental.pallas import tpu as pltpu
from jax.sharding import Mesh
from jax.sharding import PartitionSpec as P

D = 2560
H = 10
HD = 256
WINDOW = 2048
SEQ_LEN = 4096
STEP = 10

EPSILON = 1e-06
BETA_ONE = 0.9
BETA_TWO = 0.95
ADAM_EPS = 1e-08
DECAY = 0.1
CONTRACT_LAST = (((1,), (1,)), ((), ()))
CONTRACT_FIRST = (((0,), (0,)), ((), ()))
BF16 = jnp.bfloat16
F32 = jnp.float32
AXES = ("x", "c", "z", "y")


class Blank:
    @property
    def at(self):
        return self

    def __getitem__(self, _):
        return self

    def landed(self):
        pass


def guarded(condition, step):
    if condition is None:
        step()
    else:
        pl.when(condition)(step)


class Copy:
    def __init__(self, copy, sends, comes):
        self.copy, self.sends, self.comes, self.arrived = copy, sends, comes, False

    def landed(self):
        if not self.arrived:
            guarded(self.comes, self.copy.wait_recv)
            self.arrived = True

    def done(self):
        self.landed()
        guarded(self.sends, self.copy.wait_send)


class Local:
    def __init__(self, copy):
        self.copy, self.arrived = copy, False

    def landed(self):
        if not self.arrived:
            self.copy.wait()
            self.arrived = True

    def done(self):
        self.landed()


class Net:
    def __init__(self, sizes, me, sems):
        self.sizes, self.me, self.sems = sizes, me, sems
        self.sent, self.kept, self.peers, self.open = 0, 0, [], []

    def device(self, where):
        s, me = self.sizes, self.me
        if len(where) == 4:
            return {a: lax.rem(me[a] + d, s[a]) for a, d in zip(AXES, where)}
        flat = lax.rem((me["x"] * s["c"] + me["c"]) * s["z"] + me["z"] + where[0], s["n"])
        return {
            "x": flat // (s["c"] * s["z"]),
            "c": lax.rem(flat // s["z"], s["c"]),
            "z": lax.rem(flat, s["z"]),
            "y": lax.rem(me["y"] + where[1], s["y"]),
        }

    def opposite(self, where):
        if len(where) == 4:
            return tuple((self.sizes[a] - d) % self.sizes[a] for a, d in zip(AXES, where))
        return ((self.sizes["n"] - where[0]) % self.sizes["n"], (self.sizes["y"] - where[1]) % self.sizes["y"])

    def send(self, src, dst, where, sends=None, comes=None, now=True):
        k = self.sent
        self.sent += 1
        if self.sems is None:
            for w in (where, self.opposite(where)):
                if w not in self.peers:
                    self.peers.append(w)
            return Blank()
        copy = pltpu.make_async_remote_copy(
            src_ref=src,
            dst_ref=dst,
            send_sem=self.sems[0].at[k],
            recv_sem=self.sems[1].at[k],
            device_id=self.device(where),
            device_id_type=pl.DeviceIdType.MESH,
        )
        self.open.append(Copy(copy, sends, comes))
        if now:
            guarded(sends, copy.start)
        return self.open[-1]

    def keep(self, src, dst):
        k = self.kept
        self.kept += 1
        if self.sems is None:
            return Blank()
        copy = pltpu.make_async_copy(src, dst, self.sems[2].at[k])
        copy.start()
        self.open.append(Local(copy))
        return self.open[-1]

    def add(self, rows, step):
        if self.sems is not None:
            some = 16 if rows % 16 == 0 else rows

            def one(i, carry):
                step(pl.ds(pl.multiple_of(i * some, some), some))
                return carry

            lax.fori_loop(0, rows // some, one, 0)

    def greet(self, peers):
        barrier = pltpu.get_barrier_semaphore()
        for where in peers:
            pl.semaphore_signal(
                barrier, inc=1, device_id=self.device(where), device_id_type=pl.DeviceIdType.MESH
            )
        pl.semaphore_wait(barrier, len(peers))

    def finish(self):
        for item in self.open:
            item.done()


def exchange(plan, arrays, outs, sizes, number, micros, scratch=(), in_vmem=(), arrays_in_vmem=()):
    count = Net(sizes, {a: 0 for a in AXES}, None)
    plan(count, *[Blank()] * (len(arrays) + len(outs) + len(scratch)))

    def kernel(*refs):
        data, sems = refs[:-3], refs[-3:]
        net = Net(sizes, {a: lax.axis_index(a) for a in AXES}, sems)
        net.greet(count.peers)
        plan(net, *data)
        net.finish()

    anywhere = pl.BlockSpec(memory_space=pl.ANY)
    inside = pl.BlockSpec(memory_space=pltpu.VMEM)
    return pl.pallas_call(
        kernel,
        out_shape=[jax.ShapeDtypeStruct(shape, dtype) for shape, dtype in outs],
        in_specs=[inside if i in arrays_in_vmem else anywhere for i in range(len(arrays))],
        out_specs=[inside if i in in_vmem else anywhere for i in range(len(outs))],
        scratch_shapes=[
            *(pltpu.VMEM(shape, dtype) for shape, dtype in scratch),
            pltpu.SemaphoreType.DMA((count.sent,)),
            pltpu.SemaphoreType.DMA((count.sent,)),
            pltpu.SemaphoreType.DMA((max(1, count.kept),)),
        ],
        compiler_params=pltpu.CompilerParams(
            collective_id=number, has_side_effects=True, vmem_limit_bytes=56 * 2**20
        ),
        cost_estimate=pl.CostEstimate(
            flops=0, bytes_accessed=micros * 3_600_000, transcendentals=0
        ),
    )(*arrays)


SIBLING = (0, 1, 0, 0)
OTHER_Y = (0, 0, 0, 1)


def back(value, step, size):
    return lax.rem(value + size - step, size)


def along_line(net, pairs):
    z, size = net.me["z"], net.sizes["z"]

    def up(pair, step):
        slot = pair[1](back(z, step, size))
        return net.send(
            slot if step else pair[0],
            slot,
            (0, 0, 1, 0),
            sends=(z + 1 < size) & (z - step >= 0),
            comes=z - 1 - step >= 0,
        )

    def down(pair, step):
        slot = pair[1](lax.rem(z + step, size))
        return net.send(
            slot if step else pair[0],
            slot,
            (0, 0, size - 1, 0),
            sends=(z >= 1) & (z + step < size),
            comes=z + 1 + step < size,
        )

    moves = [(up(pair, 0), down(pair, 0)) for pair in pairs]

    def steps():
        for step in range(size - 1):
            for i, pair in enumerate(pairs):
                rising, falling = moves[i]
                rising.landed()
                if step + 1 < size - 1:
                    rising = up(pair, step + 1)
                yield i, (back(z, step + 1, size), z - 1 - step >= 0)
                falling.landed()
                if step + 1 < size - 1:
                    falling = down(pair, step + 1)
                yield i, (lax.rem(z + step + 1, size), z + 1 + step < size)
                moves[i] = (rising, falling)

    return steps()


def gather_x_c_z(net, pairs):
    x, c, z = (net.me[a] for a in "xcz")
    xs = net.sizes["x"]
    line = along_line(net, [(src, lambda j, dst=dst: dst.at[x, c, j]) for src, dst in pairs])
    across = []

    def onward(src, slot, condition):
        for dx in range(1, xs):
            copy = net.send(src, slot(x), (dx, 0, 0, 0), sends=condition, comes=condition)
            across.append((copy, slot(back(x, dx, xs)), condition))
        net.send(src, slot(x), SIBLING, sends=condition, comes=condition)

    for src, dst in pairs:
        net.keep(src, dst.at[x, c, z])
        onward(src, lambda px, dst=dst: dst.at[px, c, z], None)
    yield
    for count, (i, (j, condition)) in enumerate(line):
        dst = pairs[i][1]
        onward(dst.at[x, c, j], lambda px, dst=dst, j=j: dst.at[px, c, j], condition)
        yield
    for copy, slot, condition in across:
        copy.landed()
        net.send(slot, slot, SIBLING, sends=condition, comes=condition)


def gather_small(net, *refs):
    for _ in gather_x_c_z(net, list(zip(refs[:2], refs[2:]))):
        pass


def gather_weights(width, net, *refs):
    w_query, w_out, gate, query_out, out_out, gate_out = refs
    mlp = gather_mlp(net, width, gate, gate_out)
    weights = gather_x_c_z(net, [(w_query, query_out), (w_out, out_out)])
    next(mlp)
    next(weights)
    for _ in range(net.sizes["c"] * net.sizes["z"]):
        next(mlp)
    together(net, weights, mlp)


def gather_rows(net, rows, all_rows):
    c, z = net.me["c"], net.me["z"]
    line = along_line(net, [(rows, lambda j: all_rows.at[c, j])])
    net.keep(rows, all_rows.at[c, z])
    net.send(rows, all_rows.at[c, z], SIBLING)
    yield
    for _, (j, condition) in line:
        slot = all_rows.at[c, j]
        net.send(slot, slot, SIBLING, sends=condition, comes=condition)
        yield


def scatter_block(net, width, src, out):
    c, z = net.me["c"], net.me["z"]
    cs, zs = net.sizes["c"], net.sizes["z"]
    net.keep(src.at[:, pl.ds((c * zs + z) * width, width)], out.at[c, z])
    for dz in far_first(zs):
        for dc in range(cs):
            if dz or dc:
                f = lax.rem(c + dc, cs) * zs + lax.rem(z + dz, zs)
                net.send(src.at[:, pl.ds(f * width, width)], out.at[c, z], (0, dc, dz, 0))


def gather_block(net, width, block, out):
    x, y = net.me["x"], net.me["y"]
    xs, cs, ys = (net.sizes[a] for a in "xcy")

    def slot(px, py, i, j):
        return out.at[px, i, j, :, pl.ds(py * width, width)]

    next_x, next_y = [], []
    for j in range(net.sizes["z"]):
        for i in range(cs):
            src = block.at[i, j]
            net.keep(src, slot(x, y, i, j))
            for dx in range(1, xs):
                copy = net.send(src, slot(x, y, i, j), (dx, 0, 0, 0))
                if i % 2 == 0:
                    next_y.append((copy, slot(back(x, dx, xs), y, i, j)))
            copy = net.send(src, slot(x, y, i, j), OTHER_Y)
            if i % 2 == 1:
                next_x.append((copy, slot(x, back(y, 1, ys), i, j)))
    yield
    for copy, ref in next_y:
        copy.landed()
        net.send(ref, ref, OTHER_Y)
        yield
    for copy, ref in next_x:
        copy.landed()
        for dx in range(1, xs):
            net.send(ref, ref, (dx, 0, 0, 0))
        yield


def gather_mlp(net, width, src, out):
    x, c, z, y = (net.me[a] for a in AXES)
    xs, cs, zs, ys = (net.sizes[a] for a in AXES)

    def slot(px, py, i, j):
        return out.at[px, i, j, :, pl.ds(py * width, width)]

    got = []
    for dz in far_first(zs):
        for dc in range(cs):
            if dz or dc:
                f = lax.rem(c + dc, cs) * zs + lax.rem(z + dz, zs)
                copy = net.send(
                    src.at[:, pl.ds(f * width, width)], slot(x, y, c, z), (0, dc, dz, 0)
                )
                got.append((copy, back(c, dc, cs), back(z, dz, zs)))
    own = src.at[:, pl.ds((c * zs + z) * width, width)]
    net.keep(own, slot(x, y, c, z))
    next_x, next_y = [], []

    def onward(block, i, j, x_first):
        for dx in range(1, xs):
            copy = net.send(block, slot(x, y, i, j), (dx, 0, 0, 0))
            if x_first:
                next_y.append((copy, slot(back(x, dx, xs), y, i, j)))
        copy = net.send(block, slot(x, y, i, j), OTHER_Y)
        if not x_first:
            next_x.append((copy, slot(x, back(y, 1, ys), i, j)))

    yield
    onward(own, c, z, True)
    yield
    for count, (copy, i, j) in enumerate(got):
        copy.landed()
        onward(slot(x, y, i, j), i, j, count % 2 == 1)
        yield
    for copy, ref in next_y:
        copy.landed()
        net.send(ref, ref, OTHER_Y)
        yield
    for copy, ref in next_x:
        copy.landed()
        for dx in range(1, xs):
            net.send(ref, ref, (dx, 0, 0, 0))
        yield


def attention_forward(width, shape, net, *refs):
    normed, cosine, sine, bias, tokens, gain, w_query, w_out, pairs, up, down = refs[:11]
    queries, attended, attended_low, lse, middle, all_rows, all_up, down_block = refs[11:19]
    query_in, out_in, near, table, part_out, part_in, normed_out, flipped = refs[19:]
    blocks, heads, rows = shape
    x, c, z, y = (net.me[a] for a in AXES)
    n, ys = net.sizes["n"], net.sizes["y"]
    half = rows // ys
    mlp = gather_mlp(net, width, up, all_up)
    next(mlp)
    scatter_block(net, width, down, down_block)
    loads = [net.keep(w_query, query_in), net.keep(w_out, out_in)]
    me = (x * net.sizes["c"] + c) * net.sizes["z"] + z
    for j in range(blocks):
        for side in range(2):
            loads.append(net.keep(pairs.at[side, back(me, blocks - 1 - j, n)], near.at[side, j]))
    next(mlp)

    def head(h, carry):
        at = pl.ds(pl.multiple_of(h * HD, HD), HD)
        raw = jnp.dot(normed[...], query_in[:, at], preferred_element_type=F32)
        turned = raw[:, : HD // 2]
        turned = turned * cosine[...] + pltpu.roll(turned, HD // 4, 1) * sine[...]
        queries[:, at] = (
            jnp.concatenate([turned, raw[:, HD // 2 :]], axis=1) * HD ** (-0.5)
        ).astype(BF16)
        query = queries[:, at]
        top = None
        for j in range(blocks):
            scores = lax.dot_general(near[0, j], query, CONTRACT_LAST, preferred_element_type=F32)
            scores = scores + bias[j].astype(F32)
            table[j] = scores
            best = jnp.max(scores, axis=0, keepdims=True)
            top = best if top is None else jnp.maximum(top, best)
        total = jnp.zeros_like(top)
        for j in range(blocks):
            grown = jnp.exp(table[j] - top)
            table[j] = grown
            total = total + jnp.sum(grown, axis=0, keepdims=True)
        lse[h] = top + jnp.log(total)
        share = 1.0 / total
        result = jnp.zeros((HD, rows), F32)
        for j in range(blocks):
            probs = (table[j] * share).astype(BF16)
            result = result + jnp.dot(flipped[j], probs, preferred_element_type=F32)
        result = result.T
        attended[:, at] = result
        attended_low[:, at] = result.astype(BF16)
        return carry

    some = 256

    def other_half(i, carry):
        at = pl.ds(pl.multiple_of(i * some, some), some)
        mine = pl.ds(pl.multiple_of(back(y, 1, ys) * half, half), half)
        part_out[:, at] = lax.dot_general(
            attended_low[mine], out_in[at], CONTRACT_LAST, preferred_element_type=F32
        ).astype(BF16)
        return carry

    def own_half(i, carry):
        at = pl.ds(pl.multiple_of(i * some, some), some)
        mine = pl.ds(pl.multiple_of(y * half, half), half)
        middle[:, at] = tokens[:, at].astype(F32) + lax.dot_general(
            attended_low[mine], out_in[at], CONTRACT_LAST, preferred_element_type=F32
        )
        return carry

    for load in loads:
        load.landed()
    if net.sems is not None:
        for j in range(blocks):
            flipped[j] = near[1, j].T
        lax.fori_loop(0, heads, head, 0)
        lax.fori_loop(0, D // some, other_half, 0)
    swap = net.send(part_out, part_in, OTHER_Y)
    if net.sems is not None:
        lax.fori_loop(0, D // some, own_half, 0)
    for _ in range(3):
        next(mlp)
    swap.landed()

    def norm(at):
        values = middle[at] + part_in[at].astype(F32)
        middle[at] = values
        inverse = lax.rsqrt(jnp.mean(values * values, axis=-1, keepdims=True) + EPSILON)
        normed_out[at] = (values * inverse * gain[...]).astype(BF16)

    net.add(half, norm)
    together(net, gather_rows(net, normed_out, all_rows), mlp)


def mlp_forward(width, net, rows, block, normed, gate, up, all_rows, all_blocks, *refs):
    outs, (normed_in, gate_in, up_in), results = refs[:3], refs[3:6], refs[6:9]

    def products():
        first = net.keep(normed, normed_in)
        some, tiles = 256, 4
        if net.sems is not None:
            tiles = gate.shape[1] // some
        ats = [pl.ds(i * some, some) for i in range(tiles)]
        loads = [
            (net.keep(gate.at[:, at], gate_in.at[:, at]), net.keep(up.at[:, at], up_in.at[:, at]))
            for at in ats
        ]
        yield
        first.landed()
        for at, pair in zip(ats, loads):
            for load in pair:
                load.landed()
            if net.sems is not None:
                gate_pre = jnp.dot(normed_in[...], gate_in[:, at], preferred_element_type=F32)
                up_pre = jnp.dot(normed_in[...], up_in[:, at], preferred_element_type=F32)
                factor = math.sqrt(2.0 / math.pi)
                square = gate_pre * gate_pre
                bent = jnp.tanh(factor * gate_pre * (1.0 + 0.044715 * square))
                share = 0.5 + 0.5 * bent
                active = gate_pre * share
                slope = share + 0.5 * gate_pre * (1.0 - bent * bent) * factor * (
                    1.0 + 3.0 * 0.044715 * square
                )
                results[0][:, at] = active
                results[1][:, at] = up_pre * slope
                results[2][:, at] = (active * up_pre).astype(BF16)
            for result, out in zip(results, outs):
                net.keep(result.at[:, at], out.at[:, at])
            yield

    together(
        net,
        products(),
        gather_rows(net, rows, all_rows),
        gather_block(net, width, block, all_blocks),
    )


def together(net, *plans):
    plans = [plan if isinstance(plan, tuple) else (plan, 1) for plan in plans]
    while plans:
        for entry in list(plans):
            for _ in range(entry[1]):
                if next(entry[0], plans) is plans:
                    plans.remove(entry)
                    break


def far_first(size):
    return sorted(range(size), key=lambda d: -min(d, size - d))


def ends_first(size):
    return sorted(range(size), key=lambda t: min(t, size - 1 - t))


def add_low(net, target, other, rows):
    def step(at):
        target[at] = (target[at].astype(F32) + other[at].astype(F32)).astype(BF16)

    net.add(rows, step)


def sum_along_line(net, own, rising, falling, rows):
    z, size = net.me["z"], net.sizes["z"]
    ups = [(t, True) for t in range(size - 1, 0, -1)]
    downs = [(t, False) for t in range(size - 1)]
    copies = {}
    for t, up in ups + downs:
        copies[t, up] = net.send(
            own.at[t],
            (rising if up else falling).at[t],
            (0, 0, 1 if up else size - 1, 0),
            sends=(z < t) if up else (z > t),
            comes=((z > 0) & (z <= t)) if up else ((z < size - 1) & (z >= t)),
            now=False,
        )

    def take(t, up):
        copies[t, up].copy.wait_recv()
        add_low(net, own.at[t], (rising if up else falling).at[t], rows)

    def move(t, up):
        inner = ((z > 0) & (z < t)) if up else ((z < size - 1) & (z > t))

        def onward():
            take(t, up)
            copies[t, up].copy.start()

        pl.when(inner)(onward)

    def from_ends(count, skip):
        if net.sems is not None:
            for step in list(zip(ups, downs))[skip : skip + count]:
                for end, key in zip((0, size - 1), step):
                    pl.when(z == end)(copies[key].copy.start)

    from_ends(1, 0)
    yield
    from_ends(size, 1)
    for first, second in zip(ups + downs, downs + ups):
        if net.sems is not None:
            pl.when(z < size // 2)(lambda: move(*first))
            pl.when(z >= size // 2)(lambda: move(*second))
        yield
    for t, up in ups + downs:
        if net.sems is not None:
            last = (z == t) & ((z > 0) if up else (z < size - 1))
            pl.when(last)(lambda: take(t, up))
            copies[t, up].arrived = True
        yield


def sum_products(net, produce, out, part, own, got, rising, falling):
    z, zs = net.me["z"], net.sizes["z"]
    rows = 0 if net.sems is None else out.shape[0]
    line = sum_along_line(net, own, rising, falling, rows)
    order = ends_first(zs)
    for some in (order[:2], order[2:]):
        ready = {}
        for t in some:
            produce(t)
            ready[t] = net.send(part.at[t], got.at[t], SIBLING)
        for t in some:
            ready[t].landed()
            add_low(net, own.at[t], got.at[t], rows)
        if some[0] == order[0]:
            next(line)
    yield from line

    def result(at):
        out[at] = own[z, at].astype(F32)

    net.add(rows, result)


def sum_rows(net, part, out, own, got, rising, falling):
    c, z = net.me["c"], net.me["z"]
    zs = net.sizes["z"]
    rows = 0 if net.sems is None else out.shape[0]
    ready = {}
    for t in ends_first(zs):
        ready[t] = (
            net.send(part.at[lax.rem(c + 1, net.sizes["c"]), t], got.at[t], SIBLING),
            net.keep(part.at[c, t], own.at[t]),
        )
    yield
    for t in ends_first(zs):
        for copy in ready[t]:
            copy.landed()
        add_low(net, own.at[t], got.at[t], rows)
    yield from sum_along_line(net, own, rising, falling, rows)

    def result(at):
        out[at] = own[z, at].astype(F32)

    net.add(rows, result)


def sum_weights(net, *refs):
    x, c, z, y = (net.me[a] for a in AXES)
    xs, cs, zs = (net.sizes[a] for a in "xcz")
    sources, swapped, gains, grad_up = refs[0:3], refs[3:6], refs[6], refs[7]
    outs, swapped_out, gains_out, other_pair = refs[8:11], refs[11:14], refs[14], refs[15]
    up_out = refs[16]
    own, got, from_x, from_z = (refs[17 + 3 * i : 20 + 3 * i] for i in range(4))
    rows = 0 if net.sems is None else outs[0].shape[0]
    order = far_first(zs)
    ready = {}
    for dx in [*range(1, xs), 0]:
        i = lax.rem(x + dx, xs)
        for dz in order:
            j = lax.rem(z + dz, zs)
            for k in range(3):
                ready[dx, dz, k] = (
                    net.send(
                        sources[k].at[i, lax.rem(c + 1, cs), j], got[k].at[i, j], SIBLING
                    ),
                    net.keep(sources[k].at[i, c, j], own[k].at[i, j]),
                )
    for src, dst in zip(swapped, swapped_out):
        net.send(src, dst, OTHER_Y)
    gains_to_owners(net, gains, gains_out)
    scatter_columns(net, grad_up, up_out)
    over = {}
    for dx in range(1, xs):
        i = lax.rem(x + dx, xs)
        for dz in order:
            j = lax.rem(z + dz, zs)
            for k in range(3):
                for copy in ready[dx, dz, k]:
                    copy.landed()

                def pair(at, mine=own[k], other=got[k], i=i, j=j):
                    mine[i, j, at] = (
                        mine[i, j, at].astype(F32) + other[i, j, at].astype(F32)
                    ).astype(BF16)

                net.add(rows, pair)
                over[dx, dz, k] = net.send(
                    own[k].at[i, j], from_x[k].at[dx - 1, j], (dx, 0, 0, 0)
                )
    sent = {}
    for dz in order:
        j = lax.rem(z + dz, zs)
        for k in range(3):
            for copy in ready[0, dz, k]:
                copy.landed()
            for dx in range(1, xs):
                over[dx, dz, k].landed()

            def chips(at, mine=own[k], other=got[k], far=from_x[k], j=j):
                total = mine[x, j, at].astype(F32) + other[x, j, at].astype(F32)
                for dx in range(1, xs):
                    total = total + far[dx - 1, j, at].astype(F32)
                return total

            if dz:

                def keep_low(at, mine=own[k], chips=chips, j=j):
                    mine[x, j, at] = chips(at).astype(BF16)

                net.add(rows, keep_low)
                sent[dz, k] = net.send(own[k].at[x, j], from_z[k].at[dz - 1], (0, 0, dz, 0))
            else:

                def keep_wide(at, out=outs[k], chips=chips):
                    out[at] = chips(at)

                net.add(rows, keep_wide)
    for k in (2, 0, 1):
        for dz in order[:-1]:
            sent[dz, k].landed()

            def more(at, out=outs[k], far=from_z[k], dz=dz):
                out[at] += far[dz - 1, at].astype(F32)

            net.add(rows, more)
        if k == 2:
            net.send(outs[2], other_pair, OTHER_Y)


def swap_y(net, *refs):
    count = len(refs) // 2
    for src, dst in zip(refs[:count], refs[count:]):
        net.send(src, dst, OTHER_Y)


def scatter_columns(net, src, dst):
    c, z = net.me["c"], net.me["z"]
    cs, zs = net.sizes["c"], net.sizes["z"]
    width = 0 if net.sems is None else src.shape[-1]
    slot = dst.at[:, pl.ds((c * zs + z) * width, width)]
    net.keep(src.at[c, z], slot)
    for dz in range(zs):
        for dc in range(cs):
            if dz or dc:
                piece = src.at[lax.rem(c + dc, cs), lax.rem(z + dz, zs)]
                net.send(piece, slot, (0, dc, dz, 0))


def swap_rows_scatter(net, rows, grad, rows_out, grad_out):
    swap_y(net, rows, rows_out)
    scatter_columns(net, grad, grad_out)


def attention_back(
    net, shape, queries, bias, lse, attended, cosine, sine, loads, out, query_out, branch, w_out, grads, parts, got,
    own, sums, pairs, query_sum
):
    y, n = net.me["y"], net.sizes["n"]
    blocks, heads, rows = shape
    for load in loads:
        load.landed()
    delta = []
    if net.sems is not None:
        for h in range(heads):
            at = pl.ds(h * HD, HD)
            grad = jnp.dot(branch[...], w_out[:, at], preferred_element_type=F32).astype(BF16)
            grads[:, at] = grad
            delta.append(
                jnp.sum((grad.astype(F32) * attended[:, at]).T, axis=0, keepdims=True)
            )

    def block(j, carry):
        keys, values, hidden = pairs[0, j], pairs[1, j], bias[j].astype(F32)
        flipped = keys.T
        for h in range(heads):
            at = pl.ds(h * HD, HD)
            query, grad = queries[:, at], grads[:, at]
            scores = lax.dot_general(keys, query, CONTRACT_LAST, preferred_element_type=F32)
            probs = jnp.exp(scores + hidden - lse[h])
            prob_grad = lax.dot_general(values, grad, CONTRACT_LAST, preferred_element_type=F32)
            score_grad = (probs * (prob_grad - delta[h])).astype(BF16)
            value_sum = jnp.dot(probs.astype(BF16), grad, preferred_element_type=F32)
            key_sum = jnp.dot(score_grad, query, preferred_element_type=F32)
            if h:
                sums[0] += key_sum
                sums[1] += value_sum
            else:
                sums[0] = key_sum
                sums[1] = value_sum
            query_sum[at] += jnp.dot(flipped, score_grad, preferred_element_type=F32)
        parts[0, j] = sums[0].astype(BF16)
        parts[1, j] = sums[1].astype(BF16)
        return carry

    def deliver(some):
        for j in some:
            over[j].landed()

            def both(at, j=j):
                own[j, at] = (parts[y, j, at].astype(F32) + got[j, at].astype(F32)).astype(BF16)

            net.add(rows, both)
            offset = blocks - 1 - j
            if offset:
                net.send(own.at[j], out.at[offset], ((n - offset) % n, 0))
            else:
                net.keep(own.at[j], out.at[0])

    if net.sems is not None:
        query_sum[...] = jnp.zeros_like(query_sum)
    over, before = {}, ()
    for first in range(0, blocks, 3):
        some = range(first, min(first + 3, blocks))
        if net.sems is not None:
            lax.fori_loop(some.start, some.stop, block, 0)
        for j in some:
            over[j] = net.send(parts.at[back(y, 1, net.sizes["y"]), j], got.at[j], OTHER_Y)
        yield
        deliver(before)
        yield
        before = some
    if net.sems is not None:
        for h in range(heads):
            at = pl.ds(h * HD, HD)
            raw = query_sum[at].T
            turned = raw[:, : HD // 2]
            turned = turned * cosine[...] - pltpu.roll(turned, HD // 4, 1) * sine[...]
            query_out[:, at] = (
                jnp.concatenate([turned, raw[:, HD // 2 :]], axis=1) * HD ** (-0.5)
            ).astype(BF16)
    deliver(before)


def multiply(net, shape, transposed, loads, out, left_in, right_in, result, busy):
    sides, tall, width = shape
    for load in loads:
        load.landed()
    some, group = 256, 2
    for first in range(0, tall // some, group):
        last = min(first + group, tall // some)
        for copy in busy.get(first, ()):
            copy.landed()

        def tile(i, carry):
            at = pl.ds(pl.multiple_of(i * some, some), some)
            if transposed:
                result[:, at] = lax.dot_general(
                    left_in[...], right_in[at], CONTRACT_LAST, preferred_element_type=F32
                ).astype(BF16)
            else:
                product = lax.dot_general(
                    left_in[:, at], right_in[...], CONTRACT_FIRST, preferred_element_type=F32
                ).astype(BF16)
                for side in range(sides):
                    result[side, at] = product[:, side * width : (side + 1) * width]
            return carry

        if net.sems is not None:
            lax.fori_loop(first, last, tile, 0)
        at = pl.ds(first * some, (last - first) * some)
        if transposed:
            net.keep(result.at[:, at], out.at[:, at])
        else:
            busy[first] = [net.keep(result.at[i, at], out.at[i, at]) for i in range(sides)]
        yield


def sum_second(shape, net, *refs):
    arrays, (out, out_up, out_feed), scratch = refs[:7], refs[7:10], refs[10:]
    sums, inside, result, feed = scratch[:5], scratch[5:12], scratch[12], scratch[13]
    gate_grad, up_grad, gate, up, normed, hidden, down = inside
    loads = [net.keep(src, dst) for src, dst in zip(arrays, inside)]
    part, own = sums[:2]
    half = 0 if net.sems is None else out.shape[0]
    c, zs = net.me["c"], net.sizes["z"]

    def produce(t):
        for load in loads[:4]:
            load.landed()

        def rows_of(ref):
            return jnp.concatenate(
                [ref[pl.ds((i * zs + t) * half, half)] for i in range(net.sizes["c"])]
            )

        def tile(i, carry):
            at = pl.ds(pl.multiple_of(i * 256, 256), 256)
            both = lax.dot_general(
                rows_of(gate_grad), gate[at], CONTRACT_LAST, preferred_element_type=F32
            ) + lax.dot_general(
                rows_of(up_grad), up[at], CONTRACT_LAST, preferred_element_type=F32
            )
            first, second = both[:half].astype(BF16), both[half:].astype(BF16)
            own[t, :, at] = jnp.where(c == 0, first, second)
            part[t, :, at] = jnp.where(c == 0, second, first)
            return carry

        if net.sems is not None:
            lax.fori_loop(0, D // 256, tile, 0)

    def others():
        yield from multiply(net, shape, False, loads, out_up, normed, up_grad, result, {})
        yield from multiply(net, shape, True, (), out_feed, hidden, down, feed, {})

    line = sum_products(net, produce, out, *sums)
    next(line)
    together(net, (others(), 3), line)


def attention_back_sum_feed(shape, dims, net, *refs):
    inside, (all_pairs, branch, w_out, low, normed, feed, grad_gate) = refs[:6], refs[6:13]
    pairs_out, query_out, feed_out, grad_out, grad_query, gate_out = refs[13:19]
    scratch = refs[19:]
    branch_in, out_in, grads, parts, got, own, sums, pairs, query_sum = scratch[:9]
    low_in, normed_in, result = scratch[13:]
    me = (net.me["x"] * net.sizes["c"] + net.me["c"]) * net.sizes["z"] + net.me["z"]
    loads = [net.keep(branch, branch_in), net.keep(w_out, out_in)]
    loads += [
        net.keep(all_pairs.at[i, back(me, shape[0] - 1 - j, net.sizes["n"])], pairs.at[i, j])
        for j in range(shape[0])
        for i in range(2)
    ]
    later = [net.keep(low, low_in), net.keep(normed, normed_in)]
    scatter_columns(net, grad_gate, gate_out)

    def attention():
        yield
        yield from attention_back(
            net, shape, *inside, loads, pairs_out, query_out, *scratch[:9]
        )
        busy = {}
        yield from multiply(net, dims, False, later, grad_out, branch_in, low_in, result, busy)
        yield from multiply(net, dims, False, (), grad_query, normed_in, query_out, result, busy)

    line = sum_rows(net, feed, feed_out, *scratch[9:13])
    next(line)
    together(net, attention(), line)


def gains_to_owners(net, gains, gains_out):
    x, c, z, y = (net.me[a] for a in AXES)
    n = net.sizes["n"]
    me = (x * net.sizes["c"] + c) * net.sizes["z"] + z
    for offset in range(n):
        for dy in range(net.sizes["y"]):
            slot, piece = gains_out.at[y, me], gains.at[lax.rem(me + offset, n)]
            if offset == 0 and dy == 0:
                net.keep(piece, slot)
            else:
                net.send(piece, slot, (offset, dy))


def rms_forward(values, gain_row):
    inverse = lax.rsqrt(jnp.mean(values * values, axis=-1, keepdims=True) + EPSILON)
    return (values * inverse * gain_row, inverse)


def rms_backward(values, inverse, gain_row, incoming):
    scaled = incoming * gain_row
    gain_grad = jnp.sum(incoming * values * inverse, axis=0)
    value_grad = inverse * scaled - values * inverse * inverse * inverse * jnp.mean(
        scaled * values, axis=-1, keepdims=True
    )
    return (value_grad, gain_grad)


def rope_tables(positions):
    quarter = HD // 4
    freqs = jnp.exp(-math.log(10000.0) * jnp.arange(quarter, dtype=jnp.float32) * 2.0 / (HD // 2))
    angles = positions.astype(jnp.float32)[:, None] * freqs[None, :]
    return (jnp.cos(angles), jnp.sin(angles))


def rotate(values, cosine_table, sine_table):
    quarter = cosine_table.shape[1]
    lead_part = values[..., :quarter]
    pair_part = values[..., quarter : 2 * quarter]
    tail_part = values[..., 2 * quarter :]
    cos_wide = cosine_table[:, None, :]
    sin_wide = sine_table[:, None, :]
    return jnp.concatenate(
        [
            lead_part * cos_wide - pair_part * sin_wide,
            pair_part * cos_wide + lead_part * sin_wide,
            tail_part,
        ],
        axis=-1,
    )


def segment_of(index, doc_ends):
    return jnp.sum((doc_ends[None, :] <= index[:, None]).astype(jnp.int32), axis=1)


def adam_update(weight, moment_old, square_old, gradient, rate_step, decay_rate):
    moment_new = BETA_ONE * moment_old + (1.0 - BETA_ONE) * gradient
    square_new = BETA_TWO * square_old + (1.0 - BETA_TWO) * gradient * gradient
    corrected = moment_new / (1.0 - BETA_ONE**STEP)
    corrected_square = square_new / (1.0 - BETA_TWO**STEP)
    weight_new = weight - rate_step * (
        corrected / (jnp.sqrt(corrected_square) + ADAM_EPS) + decay_rate * weight
    )
    return (moment_new, square_new, weight_new)


def body(
    sizes,
    tokens,
    cotangent,
    doc_lengths,
    w_query,
    w_keyvalue,
    w_out,
    w_gate,
    w_up,
    w_down,
    norm_gains,
    first_query,
    first_keyvalue,
    first_out,
    first_gate,
    first_up,
    first_down,
    first_gains,
    second_query,
    second_keyvalue,
    second_out,
    second_gate,
    second_up,
    second_down,
    second_gains,
):
    masters = (w_query, w_keyvalue, w_out, w_gate, w_up, w_down, norm_gains)
    firsts = (first_query, first_keyvalue, first_out, first_gate, first_up, first_down, first_gains)
    seconds = (
        second_query,
        second_keyvalue,
        second_out,
        second_gate,
        second_up,
        second_down,
        second_gains,
    )
    x, c, z, y = (lax.axis_index(a) for a in AXES)
    X, C, Z, Y, N = (sizes[a] for a in (*AXES, "n"))
    F = C * Z
    rows_w = w_query.shape[0]
    columns = w_query.shape[1]
    rows = tokens.shape[0]
    half = rows // Y
    head_count = columns // HD
    mlp_columns = w_gate.shape[1]
    width = -(-mlp_columns // (F * 128)) * 128
    device = (x * C + c) * Z + z

    def pick(values, index):
        return lax.dynamic_index_in_dim(values, index, 0, keepdims=False)

    def after(value, *others):
        return lax.optimization_barrier((value, *others))[0]

    def pieces(weight):
        return jnp.pad(weight.astype(BF16), ((0, 0), (0, F * width - mlp_columns)))

    low_gains = jnp.pad(norm_gains.astype(BF16).astype(F32), ((0, 6), (0, 0)))
    pair_weight = lax.dynamic_slice_in_dim(w_keyvalue, y * HD, HD, 1).astype(BF16)
    g_pair, g_gains = exchange(
        gather_small,
        [pair_weight, low_gains],
        [((X, C, Z, rows_w, HD), BF16), ((X, C, Z, 8, rows_w), F32)],
        sizes,
        2,
        18,
    )
    g_pair = g_pair.reshape(D, HD)
    gain_values = g_gains.reshape(N, 8, rows_w)[:, :2].transpose(1, 0, 2).reshape(2, D)
    start_row = device * rows
    query_index = start_row + jnp.arange(rows, dtype=jnp.int32)
    doc_ends = jnp.cumsum(doc_lengths.reshape(-1))
    query_segment = segment_of(query_index, doc_ends)
    cosine_table, sine_table = rope_tables(query_index % SEQ_LEN)
    reach = (WINDOW - 1) // rows + 1
    scale = HD ** (-0.5)
    residual_in = tokens.astype(F32)
    normed_first, inverse_first = rms_forward(residual_in, gain_values[0])
    normed_first = normed_first.astype(BF16)
    pair_raw = jnp.dot(normed_first, g_pair, preferred_element_type=F32)
    own_pair = jnp.where(
        y == 0, rotate(pair_raw[:, None], cosine_table, sine_table)[:, 0], pair_raw
    ).astype(BF16)

    all_pairs = lax.all_gather(own_pair, ("y", "x", "c", "z"), axis=0, tiled=True)
    g_query, g_out, g_gate = exchange(
        functools.partial(gather_weights, width),
        [after(w_query.astype(BF16), own_pair), w_out.astype(BF16), pieces(w_gate)],
        [((X, C, Z, rows_w, columns), BF16)] * 2
        + [((X, C, Z, rows_w, Y * width), BF16)],
        sizes,
        1,
        120,
    )
    g_query, g_out = g_query.reshape(D, columns), g_out.reshape(D, columns)
    g_gate = g_gate.reshape(D, Y * width)
    cotangent_half = pick(cotangent.reshape(Y, half, D), y)
    all_pairs = all_pairs.reshape(Y, N, rows, HD)
    key_index = start_row - reach * rows + jnp.arange((reach + 1) * rows, dtype=jnp.int32)
    key_segment = segment_of(key_index, doc_ends)
    allowed = (
        (query_segment[:, None] == key_segment[None, :])
        & (key_index[None, :] <= query_index[:, None])
        & (query_index[:, None] - key_index[None, :] < WINDOW)
        & (key_index[None, :] >= 0)
    )
    bias = jnp.where(allowed.T, 0.0, -jnp.inf).astype(BF16).reshape(reach + 1, rows, rows)
    cosine_wide = jnp.concatenate([cosine_table, cosine_table], axis=1)
    sine_wide = jnp.concatenate([-sine_table, sine_table], axis=1)
    tokens_half = pick(tokens.reshape(Y, half, D), y)
    query_rot, attended, attended_low, log_total, middle, normed_all, g_up, down_block = exchange(
        functools.partial(attention_forward, width, (reach + 1, head_count, rows)),
        [
            normed_first,
            cosine_wide,
            sine_wide,
            bias,
            tokens_half,
            gain_values[1:],
            g_query,
            g_out,
            all_pairs,
            pieces(w_up),
            pieces(w_down),
        ],
        [
            ((rows, columns), BF16),
            ((rows, columns), F32),
            ((rows, columns), BF16),
            ((head_count, 1, rows), F32),
            ((half, D), F32),
            ((C, Z, half, D), BF16),
            ((X, C, Z, rows_w, Y * width), BF16),
            ((C, Z, rows_w, width), BF16),
        ],
        sizes,
        3,
        90,
        scratch=[
            ((D, columns), BF16),
            ((D, columns), BF16),
            ((2, reach + 1, rows, HD), BF16),
            ((reach + 1, rows, rows), F32),
            ((half, D), BF16),
            ((half, D), BF16),
            ((half, D), BF16),
            ((reach + 1, HD, rows), BF16),
        ],
        in_vmem=range(5),
        arrays_in_vmem=range(6),
    )
    inverse_second = lax.rsqrt(jnp.mean(middle * middle, axis=-1, keepdims=True) + EPSILON)
    normed_all = normed_all.reshape(F * half, D)
    g_up = g_up.reshape(D, Y * width)
    wide, tall = (F * half, Y * width), (D, Y * width)
    down_grad, g_down, active, up_slope, hidden = exchange(
        functools.partial(mlp_forward, width),
        [cotangent_half.astype(BF16), down_block, normed_all, g_gate, g_up],
        [((C, Z, half, D), BF16), ((X, C, Z, rows_w, Y * width), BF16)]
        + [(wide, F32), (wide, F32), (wide, BF16)],
        sizes,
        4,
        50,
        scratch=[
            ((F * half, D), BF16),
            (tall, BF16),
            (tall, BF16),
            (wide, F32),
            (wide, F32),
            (wide, BF16),
        ],
    )
    down_grad = down_grad.reshape(F * half, D)
    g_down = g_down.reshape(D, Y * width)
    hidden_grad = jnp.dot(down_grad, g_down, preferred_element_type=F32)
    gate_grad = (hidden_grad * up_slope).astype(BF16)
    up_grad = (hidden_grad * active).astype(BF16)

    def weight_grad(left, right):
        sides = [
            lax.dot_general(
                left,
                right[:, i * width : (i + 1) * width],
                CONTRACT_FIRST,
                preferred_element_type=F32,
            ).astype(BF16)
            for i in range(Y)
        ]
        return jnp.stack(sides).reshape(Y * X, C, Z, rows_w, width)

    whole_down = weight_grad(down_grad, hidden)

    def over_y_x(whole_grad):
        return lax.psum_scatter(
            whole_grad, ("y", "x"), scatter_dimension=0, tiled=True
        ).reshape(F, rows_w, width)

    whole_gate = weight_grad(normed_all, gate_grad)
    part_down, part_gate = over_y_x(whole_down), over_y_x(whole_gate)
    second_grad, whole_up, feed_part = exchange(
        functools.partial(sum_second, (Y, D, width)),
        [after(gate_grad, whole_down, whole_gate), up_grad, g_gate, g_up, normed_all, hidden, g_down],
        [((half, D), F32), ((Y, D, width), BF16), ((F * half, D), BF16)],
        sizes,
        5,
        65,
        scratch=[((Z, half, D), BF16)] * 5
        + [(wide, BF16)] * 2
        + [(tall, BF16)] * 2
        + [((F * half, D), BF16), (wide, BF16), (tall, BF16)]
        + [((Y, D, width), BF16), ((F * half, D), BF16)],
        in_vmem=(0,),
    )
    part_up = over_y_x(whole_up.reshape(Y * X, C, Z, rows_w, width))

    def whole(own, other):
        return jnp.where(
            y == 0, jnp.concatenate([own, other]), jnp.concatenate([other, own])
        )

    middle_norm_grad, gain_two = rms_backward(middle, inverse_second, gain_values[1], second_grad)
    middle_grad = cotangent_half + middle_norm_grad
    branch_half = middle_grad.astype(BF16)
    branch_in, new_down = exchange(
        swap_rows_scatter,
        [branch_half, part_down.reshape(C, Z, rows_w, width)],
        [((half, D), BF16), ((rows_w, F * width), BF16)],
        sizes,
        7,
        35,
    )
    branch_grad = whole(branch_half, branch_in)
    pair_parts, query_grad, feed_out, grad_out, grad_query, new_gate = exchange(
        functools.partial(
            attention_back_sum_feed, (reach + 1, head_count, rows), (1, D, columns)
        ),
        [
            query_rot,
            bias,
            log_total,
            attended,
            cosine_wide,
            sine_wide,
            all_pairs,
            branch_grad,
            g_out,
            attended_low,
            normed_first,
            feed_part.reshape(C, Z, half, D),
            part_gate.reshape(C, Z, rows_w, width),
        ],
        [
            ((reach + 1, rows, HD), BF16),
            ((rows, columns), BF16),
            ((half, D), F32),
            ((1, D, columns), BF16),
            ((1, D, columns), BF16),
            ((rows_w, F * width), BF16),
        ],
        sizes,
        8,
        95,
        scratch=[
            ((rows, D), BF16),
            ((D, columns), BF16),
            ((rows, columns), BF16),
            ((2, reach + 1, rows, HD), BF16),
            ((reach + 1, rows, HD), BF16),
            ((reach + 1, rows, HD), BF16),
            ((2, rows, HD), F32),
            ((2, reach + 1, rows, HD), BF16),
            ((columns, rows), F32),
        ]
        + [((Z, half, D), BF16)] * 4
        + [((rows, columns), BF16), ((rows, D), BF16), ((1, D, columns), BF16)],
        in_vmem=(1, 2),
        arrays_in_vmem=range(6),
    )
    mixed_half = middle + feed_out
    pair_total = jnp.sum(pair_parts.astype(F32), axis=0)
    pair_total = jnp.where(
        y == 0, rotate(pair_total[:, None], cosine_table, -sine_table)[:, 0], pair_total
    ).astype(BF16)
    first_part = (
        lax.dot_general(query_grad, g_query, CONTRACT_LAST, preferred_element_type=F32)
        + lax.dot_general(pair_total, g_pair, CONTRACT_LAST, preferred_element_type=F32)
    )
    gain_one = jnp.sum(first_part * residual_in * inverse_first, axis=0)
    first_part = first_part.astype(BF16)
    grad_gains = jnp.pad(
        jnp.stack([gain_one, gain_two]).reshape(2, N, rows_w).transpose(1, 0, 2),
        ((0, 0), (0, 6), (0, 0)),
    )
    grad_pair = lax.dot_general(
        normed_first, pair_total, CONTRACT_FIRST, preferred_element_type=F32
    ).astype(BF16)
    attention_grads = [
        g.reshape(X, C, Z, rows_w, -1) for g in (grad_query, grad_out, grad_pair)
    ]
    widths = (columns, columns, HD)
    (
        reduced_query,
        reduced_out,
        reduced_half,
        first_in,
        middle_in,
        mixed_in,
        gain_parts,
        half_in,
        new_up,
    ) = exchange(
        sum_weights,
        [
            *attention_grads,
            first_part,
            middle_grad,
            mixed_half,
            grad_gains,
            part_up.reshape(C, Z, rows_w, width),
        ],
        [((rows_w, w), F32) for w in widths]
        + [((rows, D), BF16), ((half, D), F32), ((half, D), F32), ((Y, N, 8, rows_w), F32)]
        + [((rows_w, HD), F32), ((rows_w, F * width), BF16)],
        sizes,
        9,
        110,
        scratch=[((X, Z, rows_w, w), BF16) for w in widths] * 2
        + [((X - 1, Z, rows_w, w), BF16) for w in widths]
        + [((Z - 1, rows_w, w), BF16) for w in widths],
        in_vmem=(0, 1, 2),
    )
    first_grad = first_part.astype(F32) + first_in.astype(F32)
    input_norm_grad, _ = rms_backward(residual_in, inverse_first, gain_values[0], first_grad)
    token_grad = whole(middle_grad, middle_in) + input_norm_grad
    mixed = whole(mixed_half, mixed_in)
    reduced_gains = jnp.sum(gain_parts, axis=(0, 1))[:2]
    reduced_mlp = [g[:, :mlp_columns].astype(F32) for g in (new_gate, new_up, new_down)]
    reduced_pair = jnp.where(
        y == 0,
        jnp.concatenate([reduced_half, half_in], axis=1),
        jnp.concatenate([half_in, reduced_half], axis=1),
    )
    reduced = (reduced_query, reduced_pair, reduced_out, *reduced_mlp, reduced_gains)
    dense_rate = 2.0 * D ** (-0.5)
    out_rate = 2.0 * max(1, H * HD // 64) ** (-0.5)
    rates = (dense_rate, dense_rate, out_rate, dense_rate, dense_rate, dense_rate, 0.4)
    decays = (DECAY, DECAY, DECAY, DECAY, DECAY, DECAY, 0.0)
    new_firsts = []
    new_seconds = []
    updated = []
    for weight, moment_old, square_old, gradient, rate_step, decay_rate in zip(
        masters, firsts, seconds, reduced, rates, decays
    ):
        moment_new, square_new, weight_new = adam_update(
            weight, moment_old, square_old, gradient, rate_step, decay_rate
        )
        new_firsts.append(moment_new)
        new_seconds.append(square_new)
        updated.append(weight_new)
    return (mixed, token_grad, *new_firsts, *new_seconds, *updated)


def solution(mesh):
    shape = dict(mesh.shape)
    sizes = {"x": shape["dp"] // 2, "c": 2, "z": shape["group"], "y": shape["tensor"]}
    sizes["n"] = sizes["x"] * sizes["c"] * sizes["z"]
    grid = Mesh(mesh.devices.reshape([sizes[a] for a in AXES]), AXES)
    blocks = ("x", "c", "z")
    by_rows, by_both, gains = P(blocks, None), P(blocks, "y"), P(None, blocks)
    weights = (by_both, by_rows, by_both, by_both, by_both, by_both, gains)
    return jax.shard_map(
        functools.partial(body, sizes),
        mesh=grid,
        in_specs=(by_rows, by_rows, P(), *weights * 3),
        out_specs=(by_rows, by_rows, *weights * 3),
        check_vma=False,
    )
```

```python
import functools
import math

import jax
import jax.numpy as jnp
from jax import lax
from jax.experimental import pallas as pl
from jax.experimental.layout import Layout, with_layout_constraint
from jax.experimental.pallas import tpu as pltpu
from jax.sharding import Mesh
from jax.sharding import PartitionSpec as P

D = 2560
H = 10
HD = 256
WINDOW = 2048
SEQ_LEN = 4096
STEP = 10

EPSILON = 1e-06
BETA_ONE = 0.9
BETA_TWO = 0.95
ADAM_EPS = 1e-08
DECAY = 0.1
CONTRACT_LAST = (((1,), (1,)), ((), ()))
CONTRACT_FIRST = (((0,), (0,)), ((), ()))
BF16 = jnp.bfloat16
F32 = jnp.float32
AXES = ("x", "c", "z", "y")


class Blank:
    @property
    def at(self):
        return self

    def __getitem__(self, _):
        return self

    def landed(self):
        pass


def guarded(condition, step):
    if condition is None:
        step()
    else:
        pl.when(condition)(step)


class Copy:
    def __init__(self, copy, sends, comes):
        self.copy, self.sends, self.comes, self.arrived = copy, sends, comes, False

    def landed(self):
        if not self.arrived:
            guarded(self.comes, self.copy.wait_recv)
            self.arrived = True

    def done(self):
        self.landed()
        guarded(self.sends, self.copy.wait_send)


class Local:
    def __init__(self, copy):
        self.copy, self.arrived = copy, False

    def landed(self):
        if not self.arrived:
            self.copy.wait()
            self.arrived = True

    def done(self):
        self.landed()


class Net:
    def __init__(self, sizes, me, sems):
        self.sizes, self.me, self.sems = sizes, me, sems
        self.sent, self.kept, self.peers, self.open = 0, 0, [], []

    def device(self, where):
        s, me = self.sizes, self.me
        if len(where) == 4:
            return {a: lax.rem(me[a] + d, s[a]) for a, d in zip(AXES, where)}
        flat = lax.rem((me["x"] * s["c"] + me["c"]) * s["z"] + me["z"] + where[0], s["n"])
        return {
            "x": flat // (s["c"] * s["z"]),
            "c": lax.rem(flat // s["z"], s["c"]),
            "z": lax.rem(flat, s["z"]),
            "y": lax.rem(me["y"] + where[1], s["y"]),
        }

    def opposite(self, where):
        if len(where) == 4:
            return tuple((self.sizes[a] - d) % self.sizes[a] for a, d in zip(AXES, where))
        return ((self.sizes["n"] - where[0]) % self.sizes["n"], (self.sizes["y"] - where[1]) % self.sizes["y"])

    def send(self, src, dst, where, sends=None, comes=None, now=True):
        k = self.sent
        self.sent += 1
        if self.sems is None:
            for w in (where, self.opposite(where)):
                if w not in self.peers:
                    self.peers.append(w)
            return Blank()
        copy = pltpu.make_async_remote_copy(
            src_ref=src,
            dst_ref=dst,
            send_sem=self.sems[0].at[k],
            recv_sem=self.sems[1].at[k],
            device_id=self.device(where),
            device_id_type=pl.DeviceIdType.MESH,
        )
        self.open.append(Copy(copy, sends, comes))
        if now:
            guarded(sends, copy.start)
        return self.open[-1]

    def keep(self, src, dst):
        k = self.kept
        self.kept += 1
        if self.sems is None:
            return Blank()
        copy = pltpu.make_async_copy(src, dst, self.sems[2].at[k])
        copy.start()
        self.open.append(Local(copy))
        return self.open[-1]

    def add(self, rows, step):
        if self.sems is not None:
            some = 16 if rows % 16 == 0 else rows

            def one(i, carry):
                step(pl.ds(pl.multiple_of(i * some, some), some))
                return carry

            lax.fori_loop(0, rows // some, one, 0)

    def greet(self, peers):
        barrier = pltpu.get_barrier_semaphore()
        for where in peers:
            pl.semaphore_signal(
                barrier, inc=1, device_id=self.device(where), device_id_type=pl.DeviceIdType.MESH
            )
        pl.semaphore_wait(barrier, len(peers))

    def finish(self):
        for item in self.open:
            item.done()


def exchange(plan, arrays, outs, sizes, number, micros, scratch=(), in_vmem=(), arrays_in_vmem=()):
    count = Net(sizes, {a: 0 for a in AXES}, None)
    plan(count, *[Blank()] * (len(arrays) + len(outs) + len(scratch)))

    def kernel(*refs):
        data, sems = refs[:-3], refs[-3:]
        net = Net(sizes, {a: lax.axis_index(a) for a in AXES}, sems)
        net.greet(count.peers)
        plan(net, *data)
        net.finish()

    anywhere = pl.BlockSpec(memory_space=pl.ANY)
    inside = pl.BlockSpec(memory_space=pltpu.VMEM)
    return pl.pallas_call(
        kernel,
        out_shape=[jax.ShapeDtypeStruct(shape, dtype) for shape, dtype in outs],
        in_specs=[inside if i in arrays_in_vmem else anywhere for i in range(len(arrays))],
        out_specs=[inside if i in in_vmem else anywhere for i in range(len(outs))],
        scratch_shapes=[
            *(pltpu.VMEM(shape, dtype) for shape, dtype in scratch),
            pltpu.SemaphoreType.DMA((count.sent,)),
            pltpu.SemaphoreType.DMA((count.sent,)),
            pltpu.SemaphoreType.DMA((max(1, count.kept),)),
        ],
        compiler_params=pltpu.CompilerParams(
            collective_id=number, has_side_effects=True, vmem_limit_bytes=56 * 2**20
        ),
        cost_estimate=pl.CostEstimate(
            flops=0, bytes_accessed=micros * 3_600_000, transcendentals=0
        ),
    )(*arrays)


SIBLING = (0, 1, 0, 0)
OTHER_Y = (0, 0, 0, 1)


def back(value, step, size):
    return lax.rem(value + size - step, size)


def along_line(net, pairs):
    z, size = net.me["z"], net.sizes["z"]

    def up(pair, step):
        slot = pair[1](back(z, step, size))
        return net.send(
            slot if step else pair[0],
            slot,
            (0, 0, 1, 0),
            sends=(z + 1 < size) & (z - step >= 0),
            comes=z - 1 - step >= 0,
        )

    def down(pair, step):
        slot = pair[1](lax.rem(z + step, size))
        return net.send(
            slot if step else pair[0],
            slot,
            (0, 0, size - 1, 0),
            sends=(z >= 1) & (z + step < size),
            comes=z + 1 + step < size,
        )

    moves = [(up(pair, 0), down(pair, 0)) for pair in pairs]

    def steps():
        for step in range(size - 1):
            for i, pair in enumerate(pairs):
                rising, falling = moves[i]
                rising.landed()
                if step + 1 < size - 1:
                    rising = up(pair, step + 1)
                yield i, (back(z, step + 1, size), z - 1 - step >= 0)
                falling.landed()
                if step + 1 < size - 1:
                    falling = down(pair, step + 1)
                yield i, (lax.rem(z + step + 1, size), z + 1 + step < size)
                moves[i] = (rising, falling)

    return steps()


def gather_x_c_z(net, pairs):
    x, c, z = (net.me[a] for a in "xcz")
    xs = net.sizes["x"]
    line = along_line(net, [(src, lambda j, dst=dst: dst.at[x, c, j]) for src, dst in pairs])
    across = []

    def onward(src, slot, condition):
        for dx in range(1, xs):
            copy = net.send(src, slot(x), (dx, 0, 0, 0), sends=condition, comes=condition)
            across.append((copy, slot(back(x, dx, xs)), condition))
        net.send(src, slot(x), SIBLING, sends=condition, comes=condition)

    for src, dst in pairs:
        net.keep(src, dst.at[x, c, z])
        onward(src, lambda px, dst=dst: dst.at[px, c, z], None)
    yield
    for count, (i, (j, condition)) in enumerate(line):
        dst = pairs[i][1]
        onward(dst.at[x, c, j], lambda px, dst=dst, j=j: dst.at[px, c, j], condition)
        yield
    for copy, slot, condition in across:
        copy.landed()
        net.send(slot, slot, SIBLING, sends=condition, comes=condition)


def gather_small(count, net, *refs):
    weights, outs = refs[2 : 2 + count], refs[4 + count : 4 + 2 * count]
    inside, rounded = refs[4 + 2 * count : 4 + 3 * count], refs[4 + 3 * count :]
    gather = gather_x_c_z(net, list(zip(refs[:2], refs[2 + count : 4 + count])))
    next(gather)
    loads = [net.keep(src, dst) for src, dst in zip(weights, inside)]

    def casts():
        for load, src, dst, out in zip(loads, inside, rounded, outs):
            load.landed()

            def cast(at, src=src, dst=dst):
                columns = src.shape[1]
                dst[at, :columns] = src[at].astype(BF16)
                if dst.shape[1] > columns:
                    few = (src[at].shape[0], dst.shape[1] - columns)
                    dst[at, columns:] = jnp.zeros(few, BF16)

            net.add(0 if net.sems is None else src.shape[0], cast)
            net.keep(dst, out)
            yield

    together(net, gather, casts())


def gather_weights(width, net, *refs):
    w_query, w_out, gate, down, query_out, out_out, gate_out, down_block = refs
    mlp = gather_mlp(net, width, gate, gate_out)
    weights = gather_x_c_z(net, [(w_query, query_out), (w_out, out_out)])
    next(mlp)
    next(weights)
    for _ in range(net.sizes["c"] * net.sizes["z"]):
        next(mlp)
    scatter_block(net, width, down, down_block)
    together(net, weights, mlp)


def gather_rows(net, rows, all_rows):
    c, z = net.me["c"], net.me["z"]
    line = along_line(net, [(rows, lambda j: all_rows.at[c, j])])
    net.keep(rows, all_rows.at[c, z])
    net.send(rows, all_rows.at[c, z], SIBLING)
    yield
    for _, (j, condition) in line:
        slot = all_rows.at[c, j]
        net.send(slot, slot, SIBLING, sends=condition, comes=condition)
        yield


def scatter_block(net, width, src, out):
    c, z = net.me["c"], net.me["z"]
    cs, zs = net.sizes["c"], net.sizes["z"]
    net.keep(src.at[:, pl.ds((c * zs + z) * width, width)], out.at[c, z])
    for dz in far_first(zs):
        for dc in range(cs):
            if dz or dc:
                f = lax.rem(c + dc, cs) * zs + lax.rem(z + dz, zs)
                net.send(src.at[:, pl.ds(f * width, width)], out.at[c, z], (0, dc, dz, 0))


def gather_block(net, width, block, out):
    x, y = net.me["x"], net.me["y"]
    xs, cs, ys = (net.sizes[a] for a in "xcy")

    def slot(px, py, i, j):
        return out.at[px, i, j, :, pl.ds(py * width, width)]

    next_x, next_y = [], []
    for j in range(net.sizes["z"]):
        for i in range(cs):
            src = block.at[i, j]
            net.keep(src, slot(x, y, i, j))
            for dx in range(1, xs):
                copy = net.send(src, slot(x, y, i, j), (dx, 0, 0, 0))
                if i % 2 == 0:
                    next_y.append((copy, slot(back(x, dx, xs), y, i, j)))
            copy = net.send(src, slot(x, y, i, j), OTHER_Y)
            if i % 2 == 1:
                next_x.append((copy, slot(x, back(y, 1, ys), i, j)))
    yield
    for copy, ref in next_y:
        copy.landed()
        net.send(ref, ref, OTHER_Y)
        yield
    for copy, ref in next_x:
        copy.landed()
        for dx in range(1, xs):
            net.send(ref, ref, (dx, 0, 0, 0))
        yield


def gather_mlp(net, width, src, out):
    x, c, z, y = (net.me[a] for a in AXES)
    xs, cs, zs, ys = (net.sizes[a] for a in AXES)

    def slot(px, py, i, j):
        return out.at[px, i, j, :, pl.ds(py * width, width)]

    got = []
    for dz in far_first(zs):
        for dc in range(cs):
            if dz or dc:
                f = lax.rem(c + dc, cs) * zs + lax.rem(z + dz, zs)
                copy = net.send(
                    src.at[:, pl.ds(f * width, width)], slot(x, y, c, z), (0, dc, dz, 0)
                )
                got.append((copy, back(c, dc, cs), back(z, dz, zs)))
    own = src.at[:, pl.ds((c * zs + z) * width, width)]
    net.keep(own, slot(x, y, c, z))
    next_x, next_y = [], []

    def onward(block, i, j, x_first):
        for dx in range(1, xs):
            copy = net.send(block, slot(x, y, i, j), (dx, 0, 0, 0))
            if x_first:
                next_y.append((copy, slot(back(x, dx, xs), y, i, j)))
        copy = net.send(block, slot(x, y, i, j), OTHER_Y)
        if not x_first:
            next_x.append((copy, slot(x, back(y, 1, ys), i, j)))

    yield
    onward(own, c, z, True)
    yield
    for count, (copy, i, j) in enumerate(got):
        copy.landed()
        onward(slot(x, y, i, j), i, j, count % 2 == 1)
        yield
    for copy, ref in next_y:
        copy.landed()
        net.send(ref, ref, OTHER_Y)
        yield
    for copy, ref in next_x:
        copy.landed()
        for dx in range(1, xs):
            net.send(ref, ref, (dx, 0, 0, 0))
        yield


def attention_forward(width, shape, net, *refs):
    normed, cosine, sine, bias, tokens, gain, w_query, w_out, pairs, up = refs[:10]
    queries, attended, attended_low, lse, middle, all_rows, all_up = refs[10:17]
    query_in, out_in, near, table, part_out, part_in, normed_out, flipped = refs[17:]
    blocks, heads, rows = shape
    x, c, z, y = (net.me[a] for a in AXES)
    n, ys = net.sizes["n"], net.sizes["y"]
    half = rows // ys
    mlp = gather_mlp(net, width, up, all_up)
    next(mlp)
    loads = [net.keep(w_query, query_in), net.keep(w_out, out_in)]
    me = (x * net.sizes["c"] + c) * net.sizes["z"] + z
    for j in range(blocks):
        for side in range(2):
            loads.append(net.keep(pairs.at[side, back(me, blocks - 1 - j, n)], near.at[side, j]))
    next(mlp)

    def head(h):
        at = pl.ds(h * HD, HD)
        raw = jnp.dot(normed[...], query_in[:, at], preferred_element_type=F32)
        turned = raw[:, : HD // 2]
        turned = turned * cosine[...] + pltpu.roll(turned, HD // 4, 1) * sine[...]
        queries[:, at] = (
            jnp.concatenate([turned, raw[:, HD // 2 :]], axis=1) * HD ** (-0.5)
        ).astype(BF16)
        query = queries[:, at]
        top = None
        for j in range(blocks):
            scores = lax.dot_general(near[0, j], query, CONTRACT_LAST, preferred_element_type=F32)
            scores = scores + bias[j].astype(F32)
            table[h % 2, j] = scores
            best = jnp.max(scores, axis=0, keepdims=True)
            top = best if top is None else jnp.maximum(top, best)
        total = jnp.zeros_like(top)
        result = jnp.zeros((HD, rows), F32)
        for j in range(blocks):
            grown = jnp.exp(table[h % 2, j] - top)
            total = total + jnp.sum(grown, axis=0, keepdims=True)
            result = result + jnp.dot(
                flipped[j], grown.astype(BF16), preferred_element_type=F32
            )
        lse[h] = top + jnp.log(total)
        result = (result / total).T
        attended[:, at] = result
        attended_low[:, at] = result.astype(BF16)

    some = 256

    def project(i, carry):
        at = pl.ds(pl.multiple_of(i * some, some), some)
        both = lax.dot_general(
            attended_low[...], out_in[at], CONTRACT_LAST, preferred_element_type=F32
        )
        first, second = both[:half], both[half:]
        part_out[:, at] = jnp.where(y == 0, second, first).astype(BF16)
        middle[:, at] = tokens[:, at].astype(F32) + jnp.where(y == 0, first, second)
        return carry

    for load in loads:
        load.landed()
    if net.sems is not None:
        for j in range(blocks):
            flipped[j] = near[1, j].T
        for h in range(heads):
            head(h)
        lax.fori_loop(0, D // some, project, 0)
    swap = net.send(part_out, part_in, OTHER_Y)
    for _ in range(3):
        next(mlp)
    swap.landed()

    def norm(at):
        values = middle[at] + part_in[at].astype(F32)
        middle[at] = values
        inverse = lax.rsqrt(jnp.mean(values * values, axis=-1, keepdims=True) + EPSILON)
        normed_out[at] = (values * inverse * gain[...]).astype(BF16)

    net.add(half, norm)
    together(net, gather_rows(net, normed_out, all_rows), mlp)


def mlp_forward(width, net, rows, block, normed, gate, up, all_rows, all_blocks, *refs):
    outs, (normed_in, gate_in, up_in), results = refs[:3], refs[3:6], refs[6:9]

    def products():
        first = net.keep(normed, normed_in)
        some, tiles = 256, 4
        if net.sems is not None:
            tiles = gate.shape[1] // some
        ats = [pl.ds(i * some, some) for i in range(tiles)]
        loads = [
            (net.keep(gate.at[:, at], gate_in.at[:, at]), net.keep(up.at[:, at], up_in.at[:, at]))
            for at in ats
        ]
        yield
        first.landed()
        for at, pair in zip(ats, loads):
            for load in pair:
                load.landed()
            if net.sems is not None:
                results[0][:, at] = jnp.dot(
                    normed_in[...], gate_in[:, at], preferred_element_type=F32
                )
            yield
            if net.sems is not None:
                results[1][:, at] = jnp.dot(
                    normed_in[...], up_in[:, at], preferred_element_type=F32
                )
            yield
            if net.sems is not None:
                gate_pre, up_pre = results[0][:, at], results[1][:, at]
                factor = math.sqrt(2.0 / math.pi)
                square = gate_pre * gate_pre
                bent = jnp.tanh(factor * gate_pre * (1.0 + 0.044715 * square))
                share = 0.5 + 0.5 * bent
                active = gate_pre * share
                slope = share + 0.5 * gate_pre * (1.0 - bent * bent) * factor * (
                    1.0 + 3.0 * 0.044715 * square
                )
                results[0][:, at] = active
                results[1][:, at] = up_pre * slope
                results[2][:, at] = (active * up_pre).astype(BF16)
            for result, out in zip(results, outs):
                net.keep(result.at[:, at], out.at[:, at])
            yield

    together(
        net,
        products(),
        gather_rows(net, rows, all_rows),
        gather_block(net, width, block, all_blocks),
    )


def together(net, *plans):
    plans = [plan if isinstance(plan, tuple) else (plan, 1) for plan in plans]
    while plans:
        for entry in list(plans):
            for _ in range(entry[1]):
                if next(entry[0], plans) is plans:
                    plans.remove(entry)
                    break


def far_first(size):
    return sorted(range(size), key=lambda d: -min(d, size - d))


def ends_first(size):
    return sorted(range(size), key=lambda t: min(t, size - 1 - t))


def add_low(net, target, other, rows):
    def step(at):
        target[at] = (target[at].astype(F32) + other[at].astype(F32)).astype(BF16)

    net.add(rows, step)


def sum_along_line(net, own, rising, falling, rows):
    z, size = net.me["z"], net.sizes["z"]
    ups = [(t, True) for t in range(size - 1, 0, -1)]
    downs = [(t, False) for t in range(size - 1)]
    copies = {}
    for t, up in ups + downs:
        copies[t, up] = net.send(
            own.at[t],
            (rising if up else falling).at[t],
            (0, 0, 1 if up else size - 1, 0),
            sends=(z < t) if up else (z > t),
            comes=((z > 0) & (z <= t)) if up else ((z < size - 1) & (z >= t)),
            now=False,
        )

    def take(t, up):
        copies[t, up].copy.wait_recv()
        add_low(net, own.at[t], (rising if up else falling).at[t], rows)

    def move(t, up):
        inner = ((z > 0) & (z < t)) if up else ((z < size - 1) & (z > t))

        def onward():
            take(t, up)
            copies[t, up].copy.start()

        pl.when(inner)(onward)

    def from_ends(count, skip):
        if net.sems is not None:
            for step in list(zip(ups, downs))[skip : skip + count]:
                for end, key in zip((0, size - 1), step):
                    pl.when(z == end)(copies[key].copy.start)

    from_ends(1, 0)
    yield
    from_ends(size, 1)
    for first, second in zip(ups + downs, downs + ups):
        if net.sems is not None:
            pl.when(z < size // 2)(lambda: move(*first))
            pl.when(z >= size // 2)(lambda: move(*second))
        yield
    for t, up in ups + downs:
        if net.sems is not None:
            last = (z == t) & ((z > 0) if up else (z < size - 1))
            pl.when(last)(lambda: take(t, up))
            copies[t, up].arrived = True
        yield


def sum_products(net, produce, out, part, own, got, rising, falling):
    z, zs = net.me["z"], net.sizes["z"]
    rows = 0 if net.sems is None else out.shape[0]
    line = sum_along_line(net, own, rising, falling, rows)
    order = ends_first(zs)
    for some in (order[:2], order[2:]):
        ready = {}
        for t in some:
            produce(t)
            ready[t] = net.send(part.at[t], got.at[t], SIBLING)
        for t in some:
            ready[t].landed()
            add_low(net, own.at[t], got.at[t], rows)
        if some[0] == order[0]:
            next(line)
    yield from line

    def result(at):
        out[at] = own[z, at].astype(F32)

    net.add(rows, result)


def sum_rows(net, part, out, own, got, rising, falling):
    c, z = net.me["c"], net.me["z"]
    zs = net.sizes["z"]
    rows = 0 if net.sems is None else out.shape[0]
    ready = {}
    for t in ends_first(zs):
        ready[t] = (
            net.send(part.at[lax.rem(c + 1, net.sizes["c"]), t], got.at[t], SIBLING),
            net.keep(part.at[c, t], own.at[t]),
        )
    yield
    for t in ends_first(zs):
        for copy in ready[t]:
            copy.landed()
        add_low(net, own.at[t], got.at[t], rows)
    yield from sum_along_line(net, own, rising, falling, rows)

    def result(at):
        out[at] = own[z, at].astype(F32)

    net.add(rows, result)


def sum_weights(net, *refs):
    x, c, z, y = (net.me[a] for a in AXES)
    xs, cs, zs = (net.sizes[a] for a in "xcz")
    sources, swapped, gains, grad_up = refs[0:3], refs[3:6], refs[6], refs[7]
    outs, swapped_out, gains_out, other_pair = refs[8:11], refs[11:14], refs[14], refs[15]
    up_out = refs[16]
    own, got, from_x, from_z = (refs[17 + 3 * i : 20 + 3 * i] for i in range(4))
    rows = 0 if net.sems is None else outs[0].shape[0]
    order = far_first(zs)
    ready = {}
    for dx in [*range(1, xs), 0]:
        i = lax.rem(x + dx, xs)
        for dz in order:
            j = lax.rem(z + dz, zs)
            for k in range(3):
                ready[dx, dz, k] = (
                    net.send(
                        sources[k].at[i, lax.rem(c + 1, cs), j], got[k].at[i, j], SIBLING
                    ),
                    net.keep(sources[k].at[i, c, j], own[k].at[i, j]),
                )
    for src, dst in zip(swapped, swapped_out):
        net.send(src, dst, OTHER_Y)
    gains_to_owners(net, gains, gains_out)
    scatter_columns(net, grad_up, up_out)
    over = {}
    for dx in range(1, xs):
        i = lax.rem(x + dx, xs)
        for dz in order:
            j = lax.rem(z + dz, zs)
            for k in range(3):
                for copy in ready[dx, dz, k]:
                    copy.landed()

                def pair(at, mine=own[k], other=got[k], i=i, j=j):
                    mine[i, j, at] = (
                        mine[i, j, at].astype(F32) + other[i, j, at].astype(F32)
                    ).astype(BF16)

                net.add(rows, pair)
                over[dx, dz, k] = net.send(
                    own[k].at[i, j], from_x[k].at[dx - 1, j], (dx, 0, 0, 0)
                )
    sent = {}
    for dz in order:
        j = lax.rem(z + dz, zs)
        for k in range(3):
            for copy in ready[0, dz, k]:
                copy.landed()
            for dx in range(1, xs):
                over[dx, dz, k].landed()

            def chips(at, mine=own[k], other=got[k], far=from_x[k], j=j):
                total = mine[x, j, at].astype(F32) + other[x, j, at].astype(F32)
                for dx in range(1, xs):
                    total = total + far[dx - 1, j, at].astype(F32)
                return total

            if dz:

                def keep_low(at, mine=own[k], chips=chips, j=j):
                    mine[x, j, at] = chips(at).astype(BF16)

                net.add(rows, keep_low)
                sent[dz, k] = net.send(own[k].at[x, j], from_z[k].at[dz - 1], (0, 0, dz, 0))
            else:

                def keep_wide(at, out=outs[k], chips=chips):
                    out[at] = chips(at)

                net.add(rows, keep_wide)
    for k in (2, 0, 1):
        for dz in order[:-1]:
            sent[dz, k].landed()

            def more(at, out=outs[k], far=from_z[k], dz=dz):
                out[at] += far[dz - 1, at].astype(F32)

            net.add(rows, more)
        if k == 2:
            net.send(outs[2], other_pair, OTHER_Y)


def swap_y(net, *refs):
    count = len(refs) // 2
    for src, dst in zip(refs[:count], refs[count:]):
        net.send(src, dst, OTHER_Y)


def scatter_columns(net, src, dst):
    c, z = net.me["c"], net.me["z"]
    cs, zs = net.sizes["c"], net.sizes["z"]
    width = 0 if net.sems is None else src.shape[-1]
    slot = dst.at[:, pl.ds((c * zs + z) * width, width)]
    net.keep(src.at[c, z], slot)
    for dz in range(zs):
        for dc in range(cs):
            if dz or dc:
                piece = src.at[lax.rem(c + dc, cs), lax.rem(z + dz, zs)]
                net.send(piece, slot, (0, dc, dz, 0))


def swap_rows_scatter(net, rows, grad, rows_out, grad_out):
    swap_y(net, rows, rows_out)
    scatter_columns(net, grad, grad_out)


def attention_back(
    net, shape, queries, bias, lse, attended, cosine, sine, loads, out, query_out, branch, w_out, grads, parts, got,
    own, sums, pairs, query_sum
):
    y, n = net.me["y"], net.sizes["n"]
    blocks, heads, rows = shape
    for load in loads:
        load.landed()
    delta = []
    if net.sems is not None:
        for h in range(heads):
            at = pl.ds(h * HD, HD)
            grad = jnp.dot(branch[...], w_out[:, at], preferred_element_type=F32).astype(BF16)
            grads[:, at] = grad
            delta.append(
                jnp.sum((grad.astype(F32) * attended[:, at]).T, axis=0, keepdims=True)
            )

    def block(j, carry):
        keys, values, hidden = pairs[0, j], pairs[1, j], bias[j].astype(F32)
        flipped = keys.T
        for h in range(heads):
            at = pl.ds(h * HD, HD)
            query, grad = queries[:, at], grads[:, at]
            scores = lax.dot_general(keys, query, CONTRACT_LAST, preferred_element_type=F32)
            probs = jnp.exp(scores + hidden - lse[h])
            prob_grad = lax.dot_general(values, grad, CONTRACT_LAST, preferred_element_type=F32)
            score_grad = (probs * (prob_grad - delta[h])).astype(BF16)
            value_sum = jnp.dot(probs.astype(BF16), grad, preferred_element_type=F32)
            key_sum = jnp.dot(score_grad, query, preferred_element_type=F32)
            if h:
                sums[0] += key_sum
                sums[1] += value_sum
            else:
                sums[0] = key_sum
                sums[1] = value_sum
            query_sum[at] += jnp.dot(flipped, score_grad, preferred_element_type=F32)
        parts[0, j] = sums[0].astype(BF16)
        parts[1, j] = sums[1].astype(BF16)
        return carry

    def deliver(some):
        for j in some:
            over[j].landed()

            def both(at, j=j):
                own[j, at] = (parts[y, j, at].astype(F32) + got[j, at].astype(F32)).astype(BF16)

            net.add(rows, both)
            offset = blocks - 1 - j
            if offset:
                net.send(own.at[j], out.at[offset], ((n - offset) % n, 0))
            else:
                net.keep(own.at[j], out.at[0])

    if net.sems is not None:
        query_sum[...] = jnp.zeros_like(query_sum)
    over, before = {}, ()
    for first in range(0, blocks, 3):
        some = range(first, min(first + 3, blocks))
        if net.sems is not None:
            lax.fori_loop(some.start, some.stop, block, 0)
        for j in some:
            over[j] = net.send(parts.at[back(y, 1, net.sizes["y"]), j], got.at[j], OTHER_Y)
        yield
        deliver(before)
        yield
        before = some
    if net.sems is not None:
        for h in range(heads):
            at = pl.ds(h * HD, HD)
            raw = query_sum[at].T
            turned = raw[:, : HD // 2]
            turned = turned * cosine[...] - pltpu.roll(turned, HD // 4, 1) * sine[...]
            query_out[:, at] = (
                jnp.concatenate([turned, raw[:, HD // 2 :]], axis=1) * HD ** (-0.5)
            ).astype(BF16)
    deliver(before)


def multiply(net, shape, transposed, loads, out, left_in, right_in, result, busy):
    sides, tall, width = shape
    for load in loads:
        load.landed()
    some, group = 256, 2
    for first in range(0, tall // some, group):
        last = min(first + group, tall // some)
        for copy in busy.get(first, ()):
            copy.landed()

        def tile(i, carry):
            at = pl.ds(pl.multiple_of(i * some, some), some)
            if transposed:
                result[:, at] = lax.dot_general(
                    left_in[...], right_in[at], CONTRACT_LAST, preferred_element_type=F32
                ).astype(BF16)
            else:
                product = lax.dot_general(
                    left_in[:, at], right_in[...], CONTRACT_FIRST, preferred_element_type=F32
                ).astype(BF16)
                for side in range(sides):
                    result[side, at] = product[:, side * width : (side + 1) * width]
            return carry

        if net.sems is not None:
            lax.fori_loop(first, last, tile, 0)
        at = pl.ds(first * some, (last - first) * some)
        if transposed:
            net.keep(result.at[:, at], out.at[:, at])
        else:
            busy[first] = [net.keep(result.at[i, at], out.at[i, at]) for i in range(sides)]
        yield


def sum_second(shape, net, *refs):
    arrays, (out, out_up, out_feed), scratch = refs[:7], refs[7:10], refs[10:]
    sums, inside, result, feed = scratch[:5], scratch[5:12], scratch[12], scratch[13]
    gate_grad, up_grad, gate, up, normed, hidden, down = inside
    loads = [net.keep(src, dst) for src, dst in zip(arrays, inside)]
    part, own = sums[:2]
    half = 0 if net.sems is None else out.shape[0]
    c, zs = net.me["c"], net.sizes["z"]

    def produce(t):
        for load in loads[:4]:
            load.landed()

        def rows_of(ref):
            return jnp.concatenate(
                [ref[pl.ds((i * zs + t) * half, half)] for i in range(net.sizes["c"])]
            )

        def tile(i, carry):
            at = pl.ds(pl.multiple_of(i * 256, 256), 256)
            both = lax.dot_general(
                rows_of(gate_grad), gate[at], CONTRACT_LAST, preferred_element_type=F32
            ) + lax.dot_general(
                rows_of(up_grad), up[at], CONTRACT_LAST, preferred_element_type=F32
            )
            first, second = both[:half].astype(BF16), both[half:].astype(BF16)
            own[t, :, at] = jnp.where(c == 0, first, second)
            part[t, :, at] = jnp.where(c == 0, second, first)
            return carry

        if net.sems is not None:
            lax.fori_loop(0, D // 256, tile, 0)

    def others():
        yield from multiply(net, shape, False, loads, out_up, normed, up_grad, result, {})
        yield from multiply(net, shape, True, (), out_feed, hidden, down, feed, {})

    line = sum_products(net, produce, out, *sums)
    next(line)
    together(net, (others(), 3), line)


def attention_back_sum_feed(shape, dims, net, *refs):
    inside, (all_pairs, branch, w_out, low, normed, feed, grad_gate) = refs[:6], refs[6:13]
    pairs_out, query_out, feed_out, grad_out, grad_query, gate_out = refs[13:19]
    scratch = refs[19:]
    branch_in, out_in, grads, parts, got, own, sums, pairs, query_sum = scratch[:9]
    low_in, normed_in, result = scratch[13:]
    me = (net.me["x"] * net.sizes["c"] + net.me["c"]) * net.sizes["z"] + net.me["z"]
    loads = [net.keep(branch, branch_in), net.keep(w_out, out_in)]
    loads += [
        net.keep(all_pairs.at[i, back(me, shape[0] - 1 - j, net.sizes["n"])], pairs.at[i, j])
        for j in range(shape[0])
        for i in range(2)
    ]
    later = [net.keep(low, low_in), net.keep(normed, normed_in)]
    scatter_columns(net, grad_gate, gate_out)

    def attention():
        yield
        yield from attention_back(
            net, shape, *inside, loads, pairs_out, query_out, *scratch[:9]
        )
        busy = {}
        yield from multiply(net, dims, False, later, grad_out, branch_in, low_in, result, busy)
        yield from multiply(net, dims, False, (), grad_query, normed_in, query_out, result, busy)

    line = sum_rows(net, feed, feed_out, *scratch[9:13])
    next(line)
    together(net, attention(), line)


def gains_to_owners(net, gains, gains_out):
    x, c, z, y = (net.me[a] for a in AXES)
    n = net.sizes["n"]
    me = (x * net.sizes["c"] + c) * net.sizes["z"] + z
    for offset in range(n):
        for dy in range(net.sizes["y"]):
            slot, piece = gains_out.at[y, me], gains.at[lax.rem(me + offset, n)]
            if offset == 0 and dy == 0:
                net.keep(piece, slot)
            else:
                net.send(piece, slot, (offset, dy))


def rms_forward(values, gain_row):
    inverse = lax.rsqrt(jnp.mean(values * values, axis=-1, keepdims=True) + EPSILON)
    return (values * inverse * gain_row, inverse)


def rms_backward(values, inverse, gain_row, incoming):
    scaled = incoming * gain_row
    gain_grad = jnp.sum(incoming * values * inverse, axis=0)
    value_grad = inverse * scaled - values * inverse * inverse * inverse * jnp.mean(
        scaled * values, axis=-1, keepdims=True
    )
    return (value_grad, gain_grad)


def rope_tables(positions):
    quarter = HD // 4
    freqs = jnp.exp(-math.log(10000.0) * jnp.arange(quarter, dtype=jnp.float32) * 2.0 / (HD // 2))
    angles = positions.astype(jnp.float32)[:, None] * freqs[None, :]
    return (jnp.cos(angles), jnp.sin(angles))


def rotate(values, cosine_table, sine_table):
    quarter = cosine_table.shape[1]
    lead_part = values[..., :quarter]
    pair_part = values[..., quarter : 2 * quarter]
    tail_part = values[..., 2 * quarter :]
    cos_wide = cosine_table[:, None, :]
    sin_wide = sine_table[:, None, :]
    return jnp.concatenate(
        [
            lead_part * cos_wide - pair_part * sin_wide,
            pair_part * cos_wide + lead_part * sin_wide,
            tail_part,
        ],
        axis=-1,
    )


def segment_of(index, doc_ends):
    return jnp.sum((doc_ends[None, :] <= index[:, None]).astype(jnp.int32), axis=1)


def adam_update(weight, moment_old, square_old, gradient, rate_step, decay_rate):
    moment_new = BETA_ONE * moment_old + (1.0 - BETA_ONE) * gradient
    square_new = BETA_TWO * square_old + (1.0 - BETA_TWO) * gradient * gradient
    corrected = moment_new / (1.0 - BETA_ONE**STEP)
    corrected_square = square_new / (1.0 - BETA_TWO**STEP)
    weight_new = weight - rate_step * (
        corrected / (jnp.sqrt(corrected_square) + ADAM_EPS) + decay_rate * weight
    )
    return (moment_new, square_new, weight_new)


def body(
    sizes,
    tokens,
    cotangent,
    doc_lengths,
    w_query,
    w_keyvalue,
    w_out,
    w_gate,
    w_up,
    w_down,
    norm_gains,
    first_query,
    first_keyvalue,
    first_out,
    first_gate,
    first_up,
    first_down,
    first_gains,
    second_query,
    second_keyvalue,
    second_out,
    second_gate,
    second_up,
    second_down,
    second_gains,
):
    masters = (w_query, w_keyvalue, w_out, w_gate, w_up, w_down, norm_gains)
    firsts = (first_query, first_keyvalue, first_out, first_gate, first_up, first_down, first_gains)
    seconds = (
        second_query,
        second_keyvalue,
        second_out,
        second_gate,
        second_up,
        second_down,
        second_gains,
    )
    x, c, z, y = (lax.axis_index(a) for a in AXES)
    X, C, Z, Y, N = (sizes[a] for a in (*AXES, "n"))
    F = C * Z
    rows_w = w_query.shape[0]
    columns = w_query.shape[1]
    rows = tokens.shape[0]
    half = rows // Y
    head_count = columns // HD
    mlp_columns = w_gate.shape[1]
    width = -(-mlp_columns // (F * 128)) * 128
    device = (x * C + c) * Z + z

    def pick(values, index):
        return lax.dynamic_index_in_dim(values, index, 0, keepdims=False)

    def after(value, *others):
        return lax.optimization_barrier((value, *others))[0]

    low_gains = jnp.pad(norm_gains.astype(BF16).astype(F32), ((0, 6), (0, 0)))
    pair_weight = lax.dynamic_slice_in_dim(w_keyvalue, y * HD, HD, 1).astype(BF16)
    square, oblong = (rows_w, columns), (rows_w, mlp_columns)
    padded = (rows_w, F * width)
    g_pair, g_gains, low_query, low_out, low_gate, low_up, low_down = exchange(
        functools.partial(gather_small, 5),
        [pair_weight, low_gains, w_query, w_out, w_gate, w_up, w_down],
        [((X, C, Z, rows_w, HD), BF16), ((X, C, Z, 8, rows_w), F32)]
        + [(square, BF16)] * 2
        + [(padded, BF16)] * 3,
        sizes,
        2,
        20,
        scratch=[(square, F32)] * 2
        + [(oblong, F32)] * 3
        + [(square, BF16)] * 2
        + [(padded, BF16)] * 3,
    )
    g_pair = g_pair.reshape(D, HD)
    gain_values = g_gains.reshape(N, 8, rows_w)[:, :2].transpose(1, 0, 2).reshape(2, D)
    start_row = device * rows
    query_index = start_row + jnp.arange(rows, dtype=jnp.int32)
    doc_ends = jnp.cumsum(doc_lengths.reshape(-1))
    query_segment = segment_of(query_index, doc_ends)
    cosine_table, sine_table = rope_tables(query_index % SEQ_LEN)
    reach = (WINDOW - 1) // rows + 1
    scale = HD ** (-0.5)
    residual_in = tokens.astype(F32)
    normed_first, inverse_first = rms_forward(residual_in, gain_values[0])
    normed_first = normed_first.astype(BF16)
    pair_raw = jnp.dot(normed_first, g_pair, preferred_element_type=F32)
    own_pair = jnp.where(
        y == 0, rotate(pair_raw[:, None], cosine_table, sine_table)[:, 0], pair_raw
    ).astype(BF16)

    own_pair = with_layout_constraint(own_pair, Layout((0, 1)))
    all_pairs = lax.all_gather(own_pair, ("y", "x", "c", "z"), axis=0, tiled=True)
    g_query, g_out, g_gate, down_block = exchange(
        functools.partial(gather_weights, width),
        [after(low_query, own_pair), low_out, low_gate, low_down],
        [((X, C, Z, rows_w, columns), BF16)] * 2
        + [((X, C, Z, rows_w, Y * width), BF16), ((C, Z, rows_w, width), BF16)],
        sizes,
        1,
        130,
    )
    g_query, g_out = g_query.reshape(D, columns), g_out.reshape(D, columns)
    g_gate = g_gate.reshape(D, Y * width)
    cotangent_half = pick(cotangent.reshape(Y, half, D), y)
    all_pairs = all_pairs.reshape(Y, N, rows, HD)
    key_index = start_row - reach * rows + jnp.arange((reach + 1) * rows, dtype=jnp.int32)
    key_segment = segment_of(key_index, doc_ends)
    allowed = (
        (query_segment[:, None] == key_segment[None, :])
        & (key_index[None, :] <= query_index[:, None])
        & (query_index[:, None] - key_index[None, :] < WINDOW)
        & (key_index[None, :] >= 0)
    )
    bias = jnp.where(allowed.T, 0.0, -jnp.inf).astype(BF16).reshape(reach + 1, rows, rows)
    cosine_wide = jnp.concatenate([cosine_table, cosine_table], axis=1)
    sine_wide = jnp.concatenate([-sine_table, sine_table], axis=1)
    tokens_half = pick(tokens.reshape(Y, half, D), y)
    query_rot, attended, attended_low, log_total, middle, normed_all, g_up = exchange(
        functools.partial(attention_forward, width, (reach + 1, head_count, rows)),
        [
            normed_first,
            cosine_wide,
            sine_wide,
            bias,
            tokens_half,
            gain_values[1:],
            g_query,
            g_out,
            all_pairs,
            low_up,
        ],
        [
            ((rows, columns), BF16),
            ((rows, columns), F32),
            ((rows, columns), BF16),
            ((head_count, 1, rows), F32),
            ((half, D), F32),
            ((C, Z, half, D), BF16),
            ((X, C, Z, rows_w, Y * width), BF16),
        ],
        sizes,
        3,
        90,
        scratch=[
            ((D, columns), BF16),
            ((D, columns), BF16),
            ((2, reach + 1, rows, HD), BF16),
            ((2, reach + 1, rows, rows), F32),
            ((half, D), BF16),
            ((half, D), BF16),
            ((half, D), BF16),
            ((reach + 1, HD, rows), BF16),
        ],
        in_vmem=range(5),
        arrays_in_vmem=range(6),
    )
    inverse_second = lax.rsqrt(jnp.mean(middle * middle, axis=-1, keepdims=True) + EPSILON)
    normed_all = normed_all.reshape(F * half, D)
    g_up = g_up.reshape(D, Y * width)
    wide, tall = (F * half, Y * width), (D, Y * width)
    down_grad, g_down, active, up_slope, hidden = exchange(
        functools.partial(mlp_forward, width),
        [cotangent_half.astype(BF16), down_block, normed_all, g_gate, g_up],
        [((C, Z, half, D), BF16), ((X, C, Z, rows_w, Y * width), BF16)]
        + [(wide, F32), (wide, F32), (wide, BF16)],
        sizes,
        4,
        50,
        scratch=[
            ((F * half, D), BF16),
            (tall, BF16),
            (tall, BF16),
            (wide, F32),
            (wide, F32),
            (wide, BF16),
        ],
    )
    down_grad = down_grad.reshape(F * half, D)
    g_down = g_down.reshape(D, Y * width)
    hidden_grad = jnp.dot(down_grad, g_down, preferred_element_type=F32)
    gate_grad = (hidden_grad * up_slope).astype(BF16)
    up_grad = (hidden_grad * active).astype(BF16)

    def weight_grad(left, right):
        sides = [
            lax.dot_general(
                left,
                right[:, i * width : (i + 1) * width],
                CONTRACT_FIRST,
                preferred_element_type=F32,
            ).astype(BF16)
            for i in range(Y)
        ]
        return jnp.stack(sides).reshape(Y * X, C, Z, rows_w, width)

    whole_down = weight_grad(down_grad, hidden)

    def over_y_x(whole_grad):
        return lax.psum_scatter(
            whole_grad, ("y", "x"), scatter_dimension=0, tiled=True
        ).reshape(F, rows_w, width)

    whole_gate = weight_grad(normed_all, gate_grad)
    part_down, part_gate = over_y_x(whole_down), over_y_x(whole_gate)
    second_grad, whole_up, feed_part = exchange(
        functools.partial(sum_second, (Y, D, width)),
        [after(gate_grad, whole_down, whole_gate), up_grad, g_gate, g_up, normed_all, hidden, g_down],
        [((half, D), F32), ((Y, D, width), BF16), ((F * half, D), BF16)],
        sizes,
        5,
        65,
        scratch=[((Z, half, D), BF16)] * 5
        + [(wide, BF16)] * 2
        + [(tall, BF16)] * 2
        + [((F * half, D), BF16), (wide, BF16), (tall, BF16)]
        + [((Y, D, width), BF16), ((F * half, D), BF16)],
        in_vmem=(0,),
    )
    part_up = over_y_x(whole_up.reshape(Y * X, C, Z, rows_w, width))

    def whole(own, other):
        return jnp.where(
            y == 0, jnp.concatenate([own, other]), jnp.concatenate([other, own])
        )

    middle_norm_grad, gain_two = rms_backward(middle, inverse_second, gain_values[1], second_grad)
    middle_grad = cotangent_half + middle_norm_grad
    branch_half = middle_grad.astype(BF16)
    branch_in, new_down = exchange(
        swap_rows_scatter,
        [branch_half, part_down.reshape(C, Z, rows_w, width)],
        [((half, D), BF16), ((rows_w, F * width), BF16)],
        sizes,
        7,
        35,
    )
    branch_grad = whole(branch_half, branch_in)
    pair_parts, query_grad, feed_out, grad_out, grad_query, new_gate = exchange(
        functools.partial(
            attention_back_sum_feed, (reach + 1, head_count, rows), (1, D, columns)
        ),
        [
            query_rot,
            bias,
            log_total,
            attended,
            cosine_wide,
            sine_wide,
            all_pairs,
            branch_grad,
            g_out,
            attended_low,
            normed_first,
            feed_part.reshape(C, Z, half, D),
            part_gate.reshape(C, Z, rows_w, width),
        ],
        [
            ((reach + 1, rows, HD), BF16),
            ((rows, columns), BF16),
            ((half, D), F32),
            ((1, D, columns), BF16),
            ((1, D, columns), BF16),
            ((rows_w, F * width), BF16),
        ],
        sizes,
        8,
        95,
        scratch=[
            ((rows, D), BF16),
            ((D, columns), BF16),
            ((rows, columns), BF16),
            ((2, reach + 1, rows, HD), BF16),
            ((reach + 1, rows, HD), BF16),
            ((reach + 1, rows, HD), BF16),
            ((2, rows, HD), F32),
            ((2, reach + 1, rows, HD), BF16),
            ((columns, rows), F32),
        ]
        + [((Z, half, D), BF16)] * 4
        + [((rows, columns), BF16), ((rows, D), BF16), ((1, D, columns), BF16)],
        in_vmem=(1, 2),
        arrays_in_vmem=range(6),
    )
    mixed_half = middle + feed_out
    pair_total = jnp.sum(pair_parts.astype(F32), axis=0)
    pair_total = jnp.where(
        y == 0, rotate(pair_total[:, None], cosine_table, -sine_table)[:, 0], pair_total
    ).astype(BF16)
    first_part = (
        lax.dot_general(query_grad, g_query, CONTRACT_LAST, preferred_element_type=F32)
        + lax.dot_general(pair_total, g_pair, CONTRACT_LAST, preferred_element_type=F32)
    )
    gain_one = jnp.sum(first_part * residual_in * inverse_first, axis=0)
    first_part = first_part.astype(BF16)
    grad_gains = jnp.pad(
        jnp.stack([gain_one, gain_two]).reshape(2, N, rows_w).transpose(1, 0, 2),
        ((0, 0), (0, 6), (0, 0)),
    )
    grad_pair = lax.dot_general(
        normed_first, pair_total, CONTRACT_FIRST, preferred_element_type=F32
    ).astype(BF16)
    attention_grads = [
        g.reshape(X, C, Z, rows_w, -1) for g in (grad_query, grad_out, grad_pair)
    ]
    widths = (columns, columns, HD)
    (
        reduced_query,
        reduced_out,
        reduced_half,
        first_in,
        middle_in,
        mixed_in,
        gain_parts,
        half_in,
        new_up,
    ) = exchange(
        sum_weights,
        [
            *attention_grads,
            first_part,
            middle_grad,
            mixed_half,
            grad_gains,
            part_up.reshape(C, Z, rows_w, width),
        ],
        [((rows_w, w), F32) for w in widths]
        + [((rows, D), BF16), ((half, D), F32), ((half, D), F32), ((Y, N, 8, rows_w), F32)]
        + [((rows_w, HD), F32), ((rows_w, F * width), BF16)],
        sizes,
        9,
        110,
        scratch=[((X, Z, rows_w, w), BF16) for w in widths] * 2
        + [((X - 1, Z, rows_w, w), BF16) for w in widths]
        + [((Z - 1, rows_w, w), BF16) for w in widths],
        in_vmem=(0, 1, 2),
    )
    first_grad = first_part.astype(F32) + first_in.astype(F32)
    input_norm_grad, _ = rms_backward(residual_in, inverse_first, gain_values[0], first_grad)
    token_grad = whole(middle_grad, middle_in) + input_norm_grad
    mixed = whole(mixed_half, mixed_in)
    reduced_gains = jnp.sum(gain_parts, axis=(0, 1))[:2]
    reduced_mlp = [g[:, :mlp_columns].astype(F32) for g in (new_gate, new_up, new_down)]
    reduced_pair = jnp.where(
        y == 0,
        jnp.concatenate([reduced_half, half_in], axis=1),
        jnp.concatenate([half_in, reduced_half], axis=1),
    )
    reduced = (reduced_query, reduced_pair, reduced_out, *reduced_mlp, reduced_gains)
    dense_rate = 2.0 * D ** (-0.5)
    out_rate = 2.0 * max(1, H * HD // 64) ** (-0.5)
    rates = (dense_rate, dense_rate, out_rate, dense_rate, dense_rate, dense_rate, 0.4)
    decays = (DECAY, DECAY, DECAY, DECAY, DECAY, DECAY, 0.0)
    new_firsts = []
    new_seconds = []
    updated = []
    for weight, moment_old, square_old, gradient, rate_step, decay_rate in zip(
        masters, firsts, seconds, reduced, rates, decays
    ):
        moment_new, square_new, weight_new = adam_update(
            weight, moment_old, square_old, gradient, rate_step, decay_rate
        )
        new_firsts.append(moment_new)
        new_seconds.append(square_new)
        updated.append(weight_new)
    return (mixed, token_grad, *new_firsts, *new_seconds, *updated)


def solution(mesh):
    shape = dict(mesh.shape)
    sizes = {"x": shape["dp"] // 2, "c": 2, "z": shape["group"], "y": shape["tensor"]}
    sizes["n"] = sizes["x"] * sizes["c"] * sizes["z"]
    grid = Mesh(mesh.devices.reshape([sizes[a] for a in AXES]), AXES)
    blocks = ("x", "c", "z")
    by_rows, by_both, gains = P(blocks, None), P(blocks, "y"), P(None, blocks)
    weights = (by_both, by_rows, by_both, by_both, by_both, by_both, gains)
    return jax.shard_map(
        functools.partial(body, sizes),
        mesh=grid,
        in_specs=(by_rows, by_rows, P(), *weights * 3),
        out_specs=(by_rows, by_rows, *weights * 3),
        check_vma=False,
    )
```

```python
import functools
import math

import jax
import jax.numpy as jnp
from jax import lax
from jax.experimental import pallas as pl
from jax.experimental.layout import Layout, with_layout_constraint
from jax.experimental.pallas import tpu as pltpu
from jax.sharding import Mesh
from jax.sharding import PartitionSpec as P

D = 2560
H = 10
HD = 256
WINDOW = 2048
SEQ_LEN = 4096
STEP = 10

EPSILON = 1e-06
BETA_ONE = 0.9
BETA_TWO = 0.95
ADAM_EPS = 1e-08
DECAY = 0.1
CONTRACT_LAST = (((1,), (1,)), ((), ()))
CONTRACT_FIRST = (((0,), (0,)), ((), ()))
BF16 = jnp.bfloat16
F32 = jnp.float32
AXES = ("x", "c", "z", "y")


class Blank:
    @property
    def at(self):
        return self

    def __getitem__(self, _):
        return self

    def landed(self):
        pass


def guarded(condition, step):
    if condition is None:
        step()
    else:
        pl.when(condition)(step)


class Copy:
    def __init__(self, copy, sends, comes):
        self.copy, self.sends, self.comes, self.arrived = copy, sends, comes, False

    def landed(self):
        if not self.arrived:
            guarded(self.comes, self.copy.wait_recv)
            self.arrived = True

    def done(self):
        self.landed()
        guarded(self.sends, self.copy.wait_send)


class Local:
    def __init__(self, copy):
        self.copy, self.arrived = copy, False

    def landed(self):
        if not self.arrived:
            self.copy.wait()
            self.arrived = True

    def done(self):
        self.landed()


class Net:
    def __init__(self, sizes, me, sems):
        self.sizes, self.me, self.sems = sizes, me, sems
        self.sent, self.kept, self.peers, self.open = 0, 0, [], []

    def device(self, where):
        s, me = self.sizes, self.me
        if len(where) == 4:
            return {a: lax.rem(me[a] + d, s[a]) for a, d in zip(AXES, where)}
        flat = lax.rem((me["x"] * s["c"] + me["c"]) * s["z"] + me["z"] + where[0], s["n"])
        return {
            "x": flat // (s["c"] * s["z"]),
            "c": lax.rem(flat // s["z"], s["c"]),
            "z": lax.rem(flat, s["z"]),
            "y": lax.rem(me["y"] + where[1], s["y"]),
        }

    def opposite(self, where):
        if len(where) == 4:
            return tuple((self.sizes[a] - d) % self.sizes[a] for a, d in zip(AXES, where))
        return ((self.sizes["n"] - where[0]) % self.sizes["n"], (self.sizes["y"] - where[1]) % self.sizes["y"])

    def send(self, src, dst, where, sends=None, comes=None, now=True):
        k = self.sent
        self.sent += 1
        if self.sems is None:
            for w in (where, self.opposite(where)):
                if w not in self.peers:
                    self.peers.append(w)
            return Blank()
        copy = pltpu.make_async_remote_copy(
            src_ref=src,
            dst_ref=dst,
            send_sem=self.sems[0].at[k],
            recv_sem=self.sems[1].at[k],
            device_id=self.device(where),
            device_id_type=pl.DeviceIdType.MESH,
        )
        self.open.append(Copy(copy, sends, comes))
        if now:
            guarded(sends, copy.start)
        return self.open[-1]

    def keep(self, src, dst):
        k = self.kept
        self.kept += 1
        if self.sems is None:
            return Blank()
        copy = pltpu.make_async_copy(src, dst, self.sems[2].at[k])
        copy.start()
        self.open.append(Local(copy))
        return self.open[-1]

    def add(self, rows, step):
        if self.sems is not None:
            some = 16 if rows % 16 == 0 else rows

            def one(i, carry):
                step(pl.ds(pl.multiple_of(i * some, some), some))
                return carry

            lax.fori_loop(0, rows // some, one, 0)

    def greet(self, peers):
        barrier = pltpu.get_barrier_semaphore()
        for where in peers:
            pl.semaphore_signal(
                barrier, inc=1, device_id=self.device(where), device_id_type=pl.DeviceIdType.MESH
            )
        pl.semaphore_wait(barrier, len(peers))

    def finish(self):
        for item in self.open:
            item.done()


def exchange(plan, arrays, outs, sizes, number, micros, scratch=(), in_vmem=(), arrays_in_vmem=()):
    count = Net(sizes, {a: 0 for a in AXES}, None)
    plan(count, *[Blank()] * (len(arrays) + len(outs) + len(scratch)))

    def kernel(*refs):
        data, sems = refs[:-3], refs[-3:]
        net = Net(sizes, {a: lax.axis_index(a) for a in AXES}, sems)
        net.greet(count.peers)
        plan(net, *data)
        net.finish()

    anywhere = pl.BlockSpec(memory_space=pl.ANY)
    inside = pl.BlockSpec(memory_space=pltpu.VMEM)
    return pl.pallas_call(
        kernel,
        out_shape=[jax.ShapeDtypeStruct(shape, dtype) for shape, dtype in outs],
        in_specs=[inside if i in arrays_in_vmem else anywhere for i in range(len(arrays))],
        out_specs=[inside if i in in_vmem else anywhere for i in range(len(outs))],
        scratch_shapes=[
            *(pltpu.VMEM(shape, dtype) for shape, dtype in scratch),
            pltpu.SemaphoreType.DMA((count.sent,)),
            pltpu.SemaphoreType.DMA((count.sent,)),
            pltpu.SemaphoreType.DMA((max(1, count.kept),)),
        ],
        compiler_params=pltpu.CompilerParams(
            collective_id=number, has_side_effects=True, vmem_limit_bytes=56 * 2**20
        ),
        cost_estimate=pl.CostEstimate(
            flops=0, bytes_accessed=micros * 3_600_000, transcendentals=0
        ),
    )(*arrays)


SIBLING = (0, 1, 0, 0)
OTHER_Y = (0, 0, 0, 1)


def back(value, step, size):
    return lax.rem(value + size - step, size)


def along_line(net, pairs):
    z, size = net.me["z"], net.sizes["z"]

    def up(pair, step):
        slot = pair[1](back(z, step, size))
        return net.send(
            slot if step else pair[0],
            slot,
            (0, 0, 1, 0),
            sends=(z + 1 < size) & (z - step >= 0),
            comes=z - 1 - step >= 0,
        )

    def down(pair, step):
        slot = pair[1](lax.rem(z + step, size))
        return net.send(
            slot if step else pair[0],
            slot,
            (0, 0, size - 1, 0),
            sends=(z >= 1) & (z + step < size),
            comes=z + 1 + step < size,
        )

    moves = [(up(pair, 0), down(pair, 0)) for pair in pairs]

    def steps():
        for step in range(size - 1):
            for i, pair in enumerate(pairs):
                rising, falling = moves[i]
                rising.landed()
                if step + 1 < size - 1:
                    rising = up(pair, step + 1)
                yield i, (back(z, step + 1, size), z - 1 - step >= 0)
                falling.landed()
                if step + 1 < size - 1:
                    falling = down(pair, step + 1)
                yield i, (lax.rem(z + step + 1, size), z + 1 + step < size)
                moves[i] = (rising, falling)

    return steps()


def gather_x_c_z(net, pairs):
    x, c, z = (net.me[a] for a in "xcz")
    xs = net.sizes["x"]
    line = along_line(net, [(src, lambda j, dst=dst: dst.at[x, c, j]) for src, dst in pairs])
    across = []

    def onward(src, slot, condition):
        for dx in range(1, xs):
            copy = net.send(src, slot(x), (dx, 0, 0, 0), sends=condition, comes=condition)
            across.append((copy, slot(back(x, dx, xs)), condition))
        net.send(src, slot(x), SIBLING, sends=condition, comes=condition)

    for src, dst in pairs:
        net.keep(src, dst.at[x, c, z])
        onward(src, lambda px, dst=dst: dst.at[px, c, z], None)
    yield
    for count, (i, (j, condition)) in enumerate(line):
        dst = pairs[i][1]
        onward(dst.at[x, c, j], lambda px, dst=dst, j=j: dst.at[px, c, j], condition)
        yield
    for copy, slot, condition in across:
        copy.landed()
        net.send(slot, slot, SIBLING, sends=condition, comes=condition)


def gather_small(count, net, *refs):
    weights, outs = refs[2 : 2 + count], refs[4 + count : 4 + 2 * count]
    inside, rounded = refs[4 + 2 * count : 4 + 3 * count], refs[4 + 3 * count :]
    gather = gather_x_c_z(net, list(zip(refs[:2], refs[2 + count : 4 + count])))
    next(gather)
    loads = [net.keep(src, dst) for src, dst in zip(weights, inside)]

    def casts():
        for load, src, dst, out in zip(loads, inside, rounded, outs):
            load.landed()

            def cast(at, src=src, dst=dst):
                columns = src.shape[1]
                dst[at, :columns] = src[at].astype(BF16)
                if dst.shape[1] > columns:
                    few = (src[at].shape[0], dst.shape[1] - columns)
                    dst[at, columns:] = jnp.zeros(few, BF16)

            net.add(0 if net.sems is None else src.shape[0], cast)
            net.keep(dst, out)
            yield

    together(net, gather, casts())


def gather_weights(width, net, *refs):
    w_query, w_out, gate, down, query_out, out_out, gate_out, down_block = refs
    mlp = gather_mlp(net, width, gate, gate_out)
    weights = gather_x_c_z(net, [(w_query, query_out), (w_out, out_out)])
    next(mlp)
    next(weights)
    for _ in range(net.sizes["c"] * net.sizes["z"]):
        next(mlp)
    scatter_block(net, width, down, down_block)
    together(net, weights, mlp)


def gather_rows(net, rows, all_rows):
    c, z = net.me["c"], net.me["z"]
    line = along_line(net, [(rows, lambda j: all_rows.at[c, j])])
    net.keep(rows, all_rows.at[c, z])
    net.send(rows, all_rows.at[c, z], SIBLING)
    yield
    for _, (j, condition) in line:
        slot = all_rows.at[c, j]
        net.send(slot, slot, SIBLING, sends=condition, comes=condition)
        yield


def scatter_block(net, width, src, out):
    c, z = net.me["c"], net.me["z"]
    cs, zs = net.sizes["c"], net.sizes["z"]
    net.keep(src.at[:, pl.ds((c * zs + z) * width, width)], out.at[c, z])
    for dz in far_first(zs):
        for dc in range(cs):
            if dz or dc:
                f = lax.rem(c + dc, cs) * zs + lax.rem(z + dz, zs)
                net.send(src.at[:, pl.ds(f * width, width)], out.at[c, z], (0, dc, dz, 0))


def gather_block(net, width, block, out):
    x, y = net.me["x"], net.me["y"]
    xs, cs, ys = (net.sizes[a] for a in "xcy")

    def slot(px, py, i, j):
        return out.at[px, i, j, :, pl.ds(py * width, width)]

    next_x, next_y = [], []
    for j in range(net.sizes["z"]):
        for i in range(cs):
            src = block.at[i, j]
            net.keep(src, slot(x, y, i, j))
            for dx in range(1, xs):
                copy = net.send(src, slot(x, y, i, j), (dx, 0, 0, 0))
                if i % 2 == 0:
                    next_y.append((copy, slot(back(x, dx, xs), y, i, j)))
            copy = net.send(src, slot(x, y, i, j), OTHER_Y)
            if i % 2 == 1:
                next_x.append((copy, slot(x, back(y, 1, ys), i, j)))
    yield
    for copy, ref in next_y:
        copy.landed()
        net.send(ref, ref, OTHER_Y)
        yield
    for copy, ref in next_x:
        copy.landed()
        for dx in range(1, xs):
            net.send(ref, ref, (dx, 0, 0, 0))
        yield


def gather_mlp(net, width, src, out):
    x, c, z, y = (net.me[a] for a in AXES)
    xs, cs, zs, ys = (net.sizes[a] for a in AXES)

    def slot(px, py, i, j):
        return out.at[px, i, j, :, pl.ds(py * width, width)]

    got = []
    for dz in far_first(zs):
        for dc in range(cs):
            if dz or dc:
                f = lax.rem(c + dc, cs) * zs + lax.rem(z + dz, zs)
                copy = net.send(
                    src.at[:, pl.ds(f * width, width)], slot(x, y, c, z), (0, dc, dz, 0)
                )
                got.append((copy, back(c, dc, cs), back(z, dz, zs)))
    own = src.at[:, pl.ds((c * zs + z) * width, width)]
    net.keep(own, slot(x, y, c, z))
    next_x, next_y = [], []

    def onward(block, i, j, x_first):
        for dx in range(1, xs):
            copy = net.send(block, slot(x, y, i, j), (dx, 0, 0, 0))
            if x_first:
                next_y.append((copy, slot(back(x, dx, xs), y, i, j)))
        copy = net.send(block, slot(x, y, i, j), OTHER_Y)
        if not x_first:
            next_x.append((copy, slot(x, back(y, 1, ys), i, j)))

    yield
    onward(own, c, z, True)
    yield
    for count, (copy, i, j) in enumerate(got):
        copy.landed()
        onward(slot(x, y, i, j), i, j, count % 2 == 1)
        yield
    for copy, ref in next_y:
        copy.landed()
        net.send(ref, ref, OTHER_Y)
        yield
    for copy, ref in next_x:
        copy.landed()
        for dx in range(1, xs):
            net.send(ref, ref, (dx, 0, 0, 0))
        yield


def attention_forward(width, shape, net, *refs):
    normed, cosine, sine, bias, tokens, gain, w_query, w_out, pairs, up = refs[:10]
    queries, attended, attended_low, lse, middle, all_rows, all_up = refs[10:17]
    query_in, out_in, near, table, part_out, part_in, normed_out, flipped = refs[17:]
    blocks, heads, rows = shape
    x, c, z, y = (net.me[a] for a in AXES)
    n, ys = net.sizes["n"], net.sizes["y"]
    half = rows // ys
    mlp = gather_mlp(net, width, up, all_up)
    next(mlp)
    loads = [net.keep(w_query, query_in), net.keep(w_out, out_in)]
    me = (x * net.sizes["c"] + c) * net.sizes["z"] + z
    for j in range(blocks):
        for side in range(2):
            loads.append(net.keep(pairs.at[side, back(me, blocks - 1 - j, n)], near.at[side, j]))
    next(mlp)

    def head(h):
        at = pl.ds(h * HD, HD)
        raw = jnp.dot(normed[...], query_in[:, at], preferred_element_type=F32)
        turned = raw[:, : HD // 2]
        turned = turned * cosine[...] + pltpu.roll(turned, HD // 4, 1) * sine[...]
        queries[:, at] = (
            jnp.concatenate([turned, raw[:, HD // 2 :]], axis=1) * HD ** (-0.5)
        ).astype(BF16)
        query = queries[:, at]
        top = None
        for j in range(blocks):
            scores = lax.dot_general(near[0, j], query, CONTRACT_LAST, preferred_element_type=F32)
            scores = scores + bias[j].astype(F32)
            table[h % 2, j] = scores
            best = jnp.max(scores, axis=0, keepdims=True)
            top = best if top is None else jnp.maximum(top, best)
        total = jnp.zeros_like(top)
        result = jnp.zeros((HD, rows), F32)
        for j in range(blocks):
            grown = jnp.exp(table[h % 2, j] - top)
            total = total + jnp.sum(grown, axis=0, keepdims=True)
            result = result + jnp.dot(
                flipped[j], grown.astype(BF16), preferred_element_type=F32
            )
        lse[h] = top + jnp.log(total)
        result = (result / total).T
        attended[:, at] = result
        attended_low[:, at] = result.astype(BF16)

    some = 256

    def project(i, carry):
        at = pl.ds(pl.multiple_of(i * some, some), some)
        both = lax.dot_general(
            attended_low[...], out_in[at], CONTRACT_LAST, preferred_element_type=F32
        )
        first, second = both[:half], both[half:]
        part_out[:, at] = jnp.where(y == 0, second, first).astype(BF16)
        middle[:, at] = tokens[:, at].astype(F32) + jnp.where(y == 0, first, second)
        return carry

    for load in loads:
        load.landed()
    if net.sems is not None:
        for j in range(blocks):
            flipped[j] = near[1, j].T
        for h in range(heads):
            head(h)
        lax.fori_loop(0, D // some, project, 0)
    swap = net.send(part_out, part_in, OTHER_Y)
    for _ in range(3):
        next(mlp)
    swap.landed()

    def norm(at):
        values = middle[at] + part_in[at].astype(F32)
        middle[at] = values
        inverse = lax.rsqrt(jnp.mean(values * values, axis=-1, keepdims=True) + EPSILON)
        normed_out[at] = (values * inverse * gain[...]).astype(BF16)

    net.add(half, norm)
    together(net, gather_rows(net, normed_out, all_rows), mlp)


def mlp_forward(width, net, rows, block, normed, gate, up, all_rows, all_blocks, *refs):
    outs, (normed_in, gate_in, up_in), results = refs[:3], refs[3:6], refs[6:9]

    def products():
        first = net.keep(normed, normed_in)
        some, tiles = 512, 2
        if net.sems is not None:
            tiles = gate.shape[1] // some
        ats = [pl.ds(i * some, some) for i in range(tiles)]
        loads = [
            (net.keep(gate.at[:, at], gate_in.at[:, at]), net.keep(up.at[:, at], up_in.at[:, at]))
            for at in ats
        ]
        yield
        first.landed()
        for at, pair in zip(ats, loads):
            for load in pair:
                load.landed()
            if net.sems is not None:
                results[0][:, at] = jnp.dot(
                    normed_in[...], gate_in[:, at], preferred_element_type=F32
                )
            yield
            if net.sems is not None:
                results[1][:, at] = jnp.dot(
                    normed_in[...], up_in[:, at], preferred_element_type=F32
                )
            yield
            if net.sems is not None:
                gate_pre, up_pre = results[0][:, at], results[1][:, at]
                factor = math.sqrt(2.0 / math.pi)
                square = gate_pre * gate_pre
                bent = jnp.tanh(factor * gate_pre * (1.0 + 0.044715 * square))
                share = 0.5 + 0.5 * bent
                active = gate_pre * share
                slope = share + 0.5 * gate_pre * (1.0 - bent * bent) * factor * (
                    1.0 + 3.0 * 0.044715 * square
                )
                results[0][:, at] = active
                results[1][:, at] = up_pre * slope
                results[2][:, at] = (active * up_pre).astype(BF16)
            for result, out in zip(results, outs):
                net.keep(result.at[:, at], out.at[:, at])
            yield

    together(
        net,
        products(),
        gather_rows(net, rows, all_rows),
        gather_block(net, width, block, all_blocks),
    )


def together(net, *plans):
    plans = [plan if isinstance(plan, tuple) else (plan, 1) for plan in plans]
    while plans:
        for entry in list(plans):
            for _ in range(entry[1]):
                if next(entry[0], plans) is plans:
                    plans.remove(entry)
                    break


def far_first(size):
    return sorted(range(size), key=lambda d: -min(d, size - d))


def ends_first(size):
    return sorted(range(size), key=lambda t: min(t, size - 1 - t))


def add_low(net, target, other, rows):
    def step(at):
        target[at] = (target[at].astype(F32) + other[at].astype(F32)).astype(BF16)

    net.add(rows, step)


def sum_along_line(net, own, rising, falling, rows):
    z, size = net.me["z"], net.sizes["z"]
    ups = [(t, True) for t in range(size - 1, 0, -1)]
    downs = [(t, False) for t in range(size - 1)]
    copies = {}
    for t, up in ups + downs:
        copies[t, up] = net.send(
            own.at[t],
            (rising if up else falling).at[t],
            (0, 0, 1 if up else size - 1, 0),
            sends=(z < t) if up else (z > t),
            comes=((z > 0) & (z <= t)) if up else ((z < size - 1) & (z >= t)),
            now=False,
        )

    def take(t, up):
        copies[t, up].copy.wait_recv()
        add_low(net, own.at[t], (rising if up else falling).at[t], rows)

    def move(t, up):
        inner = ((z > 0) & (z < t)) if up else ((z < size - 1) & (z > t))

        def onward():
            take(t, up)
            copies[t, up].copy.start()

        pl.when(inner)(onward)

    def from_ends(count, skip):
        if net.sems is not None:
            for step in list(zip(ups, downs))[skip : skip + count]:
                for end, key in zip((0, size - 1), step):
                    pl.when(z == end)(copies[key].copy.start)

    from_ends(1, 0)
    yield
    from_ends(size, 1)
    for first, second in zip(ups + downs, downs + ups):
        if net.sems is not None:
            pl.when(z < size // 2)(lambda: move(*first))
            pl.when(z >= size // 2)(lambda: move(*second))
        yield
    for t, up in ups + downs:
        if net.sems is not None:
            last = (z == t) & ((z > 0) if up else (z < size - 1))
            pl.when(last)(lambda: take(t, up))
            copies[t, up].arrived = True
        yield


def sum_products(net, produce, out, part, own, got, rising, falling):
    z, zs = net.me["z"], net.sizes["z"]
    rows = 0 if net.sems is None else out.shape[0]
    line = sum_along_line(net, own, rising, falling, rows)
    order = ends_first(zs)
    for some in (order[:2], order[2:]):
        ready = {}
        for t in some:
            produce(t)
            ready[t] = net.send(part.at[t], got.at[t], SIBLING)
        for t in some:
            ready[t].landed()
            add_low(net, own.at[t], got.at[t], rows)
        if some[0] == order[0]:
            next(line)
    yield from line

    def result(at):
        out[at] = own[z, at].astype(F32)

    net.add(rows, result)


def sum_rows(net, part, out, own, got, rising, falling):
    c, z = net.me["c"], net.me["z"]
    zs = net.sizes["z"]
    rows = 0 if net.sems is None else out.shape[0]
    ready = {}
    for t in ends_first(zs):
        ready[t] = (
            net.send(part.at[lax.rem(c + 1, net.sizes["c"]), t], got.at[t], SIBLING),
            net.keep(part.at[c, t], own.at[t]),
        )
    yield
    for t in ends_first(zs):
        for copy in ready[t]:
            copy.landed()
        add_low(net, own.at[t], got.at[t], rows)
    yield from sum_along_line(net, own, rising, falling, rows)

    def result(at):
        out[at] = own[z, at].astype(F32)

    net.add(rows, result)


def sum_weights(net, *refs):
    x, c, z, y = (net.me[a] for a in AXES)
    xs, cs, zs = (net.sizes[a] for a in "xcz")
    sources, swapped, gains, grad_up = refs[0:3], refs[3:6], refs[6], refs[7]
    outs, swapped_out, gains_out, other_pair = refs[8:11], refs[11:14], refs[14], refs[15]
    up_out = refs[16]
    own, got, from_x, from_z = (refs[17 + 3 * i : 20 + 3 * i] for i in range(4))
    rows = 0 if net.sems is None else outs[0].shape[0]
    order = far_first(zs)
    ready = {}
    for dx in [*range(1, xs), 0]:
        i = lax.rem(x + dx, xs)
        for dz in order:
            j = lax.rem(z + dz, zs)
            for k in range(3):
                ready[dx, dz, k] = (
                    net.send(
                        sources[k].at[i, lax.rem(c + 1, cs), j], got[k].at[i, j], SIBLING
                    ),
                    net.keep(sources[k].at[i, c, j], own[k].at[i, j]),
                )
    for src, dst in zip(swapped, swapped_out):
        net.send(src, dst, OTHER_Y)
    gains_to_owners(net, gains, gains_out)
    scatter_columns(net, grad_up, up_out)
    over = {}
    for dx in range(1, xs):
        i = lax.rem(x + dx, xs)
        for dz in order:
            j = lax.rem(z + dz, zs)
            for k in range(3):
                for copy in ready[dx, dz, k]:
                    copy.landed()

                def pair(at, mine=own[k], other=got[k], i=i, j=j):
                    mine[i, j, at] = (
                        mine[i, j, at].astype(F32) + other[i, j, at].astype(F32)
                    ).astype(BF16)

                net.add(rows, pair)
                over[dx, dz, k] = net.send(
                    own[k].at[i, j], from_x[k].at[dx - 1, j], (dx, 0, 0, 0)
                )
    sent = {}
    for dz in order:
        j = lax.rem(z + dz, zs)
        for k in range(3):
            for copy in ready[0, dz, k]:
                copy.landed()
            for dx in range(1, xs):
                over[dx, dz, k].landed()

            def chips(at, mine=own[k], other=got[k], far=from_x[k], j=j):
                total = mine[x, j, at].astype(F32) + other[x, j, at].astype(F32)
                for dx in range(1, xs):
                    total = total + far[dx - 1, j, at].astype(F32)
                return total

            if dz:

                def keep_low(at, mine=own[k], chips=chips, j=j):
                    mine[x, j, at] = chips(at).astype(BF16)

                net.add(rows, keep_low)
                sent[dz, k] = net.send(own[k].at[x, j], from_z[k].at[dz - 1], (0, 0, dz, 0))
            else:

                def keep_wide(at, out=outs[k], chips=chips):
                    out[at] = chips(at)

                net.add(rows, keep_wide)
    for k in (2, 0, 1):
        for dz in order[:-1]:
            sent[dz, k].landed()

            def more(at, out=outs[k], far=from_z[k], dz=dz):
                out[at] += far[dz - 1, at].astype(F32)

            net.add(rows, more)
        if k == 2:
            net.send(outs[2], other_pair, OTHER_Y)


def swap_y(net, *refs):
    count = len(refs) // 2
    for src, dst in zip(refs[:count], refs[count:]):
        net.send(src, dst, OTHER_Y)


def scatter_columns(net, src, dst):
    c, z = net.me["c"], net.me["z"]
    cs, zs = net.sizes["c"], net.sizes["z"]
    width = 0 if net.sems is None else src.shape[-1]
    slot = dst.at[:, pl.ds((c * zs + z) * width, width)]
    net.keep(src.at[c, z], slot)
    for dz in range(zs):
        for dc in range(cs):
            if dz or dc:
                piece = src.at[lax.rem(c + dc, cs), lax.rem(z + dz, zs)]
                net.send(piece, slot, (0, dc, dz, 0))


def swap_rows_scatter(net, rows, grad, rows_out, grad_out):
    swap_y(net, rows, rows_out)
    scatter_columns(net, grad, grad_out)


def attention_back(
    net, shape, queries, bias, lse, attended, cosine, sine, loads, out, query_out, branch, w_out, grads, parts, got,
    own, sums, pairs, query_sum
):
    y, n = net.me["y"], net.sizes["n"]
    blocks, heads, rows = shape
    for load in loads:
        load.landed()
    delta = []
    if net.sems is not None:
        for h in range(heads):
            at = pl.ds(h * HD, HD)
            grad = jnp.dot(branch[...], w_out[:, at], preferred_element_type=F32).astype(BF16)
            grads[:, at] = grad
            delta.append(
                jnp.sum((grad.astype(F32) * attended[:, at]).T, axis=0, keepdims=True)
            )

    def block(j, carry):
        keys, values, hidden = pairs[0, j], pairs[1, j], bias[j].astype(F32)
        flipped = keys.T
        for h in range(heads):
            at = pl.ds(h * HD, HD)
            query, grad = queries[:, at], grads[:, at]
            scores = lax.dot_general(keys, query, CONTRACT_LAST, preferred_element_type=F32)
            probs = jnp.exp(scores + hidden - lse[h])
            prob_grad = lax.dot_general(values, grad, CONTRACT_LAST, preferred_element_type=F32)
            score_grad = (probs * (prob_grad - delta[h])).astype(BF16)
            value_sum = jnp.dot(probs.astype(BF16), grad, preferred_element_type=F32)
            key_sum = jnp.dot(score_grad, query, preferred_element_type=F32)
            if h:
                sums[0] += key_sum
                sums[1] += value_sum
            else:
                sums[0] = key_sum
                sums[1] = value_sum
            query_sum[at] += jnp.dot(flipped, score_grad, preferred_element_type=F32)
        parts[0, j] = sums[0].astype(BF16)
        parts[1, j] = sums[1].astype(BF16)
        return carry

    def deliver(some):
        for j in some:
            over[j].landed()

            def both(at, j=j):
                own[j, at] = (parts[y, j, at].astype(F32) + got[j, at].astype(F32)).astype(BF16)

            net.add(rows, both)
            offset = blocks - 1 - j
            if offset:
                net.send(own.at[j], out.at[offset], ((n - offset) % n, 0))
            else:
                net.keep(own.at[j], out.at[0])

    if net.sems is not None:
        query_sum[...] = jnp.zeros_like(query_sum)
    over, before = {}, ()
    for first in range(0, blocks, 3):
        some = range(first, min(first + 3, blocks))
        if net.sems is not None:
            lax.fori_loop(some.start, some.stop, block, 0)
        for j in some:
            over[j] = net.send(parts.at[back(y, 1, net.sizes["y"]), j], got.at[j], OTHER_Y)
        yield
        deliver(before)
        yield
        before = some
    if net.sems is not None:
        for h in range(heads):
            at = pl.ds(h * HD, HD)
            raw = query_sum[at].T
            turned = raw[:, : HD // 2]
            turned = turned * cosine[...] - pltpu.roll(turned, HD // 4, 1) * sine[...]
            query_out[:, at] = (
                jnp.concatenate([turned, raw[:, HD // 2 :]], axis=1) * HD ** (-0.5)
            ).astype(BF16)
    deliver(before)


def multiply(net, shape, transposed, loads, out, left_in, right_in, result, busy):
    sides, tall, width = shape
    for load in loads:
        load.landed()
    some, group = 256, 2
    for first in range(0, tall // some, group):
        last = min(first + group, tall // some)
        for copy in busy.get(first, ()):
            copy.landed()

        def tile(i, carry):
            at = pl.ds(pl.multiple_of(i * some, some), some)
            if transposed:
                result[:, at] = lax.dot_general(
                    left_in[...], right_in[at], CONTRACT_LAST, preferred_element_type=F32
                ).astype(BF16)
            else:
                product = lax.dot_general(
                    left_in[:, at], right_in[...], CONTRACT_FIRST, preferred_element_type=F32
                ).astype(BF16)
                for side in range(sides):
                    result[side, at] = product[:, side * width : (side + 1) * width]
            return carry

        if net.sems is not None:
            lax.fori_loop(first, last, tile, 0)
        at = pl.ds(first * some, (last - first) * some)
        if transposed:
            net.keep(result.at[:, at], out.at[:, at])
        else:
            busy[first] = [net.keep(result.at[i, at], out.at[i, at]) for i in range(sides)]
        yield


def sum_second(shape, net, *refs):
    arrays, (out, out_up, out_feed), scratch = refs[:7], refs[7:10], refs[10:]
    sums, inside, result, feed = scratch[:5], scratch[5:12], scratch[12], scratch[13]
    gate_grad, up_grad, gate, up, normed, hidden, down = inside
    loads = [net.keep(src, dst) for src, dst in zip(arrays, inside)]
    part, own = sums[:2]
    half = 0 if net.sems is None else out.shape[0]
    c, zs = net.me["c"], net.sizes["z"]

    def produce(t):
        for load in loads[:4]:
            load.landed()

        def rows_of(ref):
            return jnp.concatenate(
                [ref[pl.ds((i * zs + t) * half, half)] for i in range(net.sizes["c"])]
            )

        def tile(i, carry):
            at = pl.ds(pl.multiple_of(i * 256, 256), 256)
            both = lax.dot_general(
                rows_of(gate_grad), gate[at], CONTRACT_LAST, preferred_element_type=F32
            ) + lax.dot_general(
                rows_of(up_grad), up[at], CONTRACT_LAST, preferred_element_type=F32
            )
            first, second = both[:half].astype(BF16), both[half:].astype(BF16)
            own[t, :, at] = jnp.where(c == 0, first, second)
            part[t, :, at] = jnp.where(c == 0, second, first)
            return carry

        if net.sems is not None:
            lax.fori_loop(0, D // 256, tile, 0)

    def others():
        yield from multiply(net, shape, False, loads, out_up, normed, up_grad, result, {})
        yield from multiply(net, shape, True, (), out_feed, hidden, down, feed, {})

    line = sum_products(net, produce, out, *sums)
    next(line)
    together(net, (others(), 3), line)


def attention_back_sum_feed(shape, dims, net, *refs):
    inside, (all_pairs, branch, other, w_out, low, normed, feed, grad_gate) = refs[:6], refs[6:14]
    pairs_out, query_out, feed_out, grad_out, grad_query, gate_out = refs[14:20]
    scratch = refs[20:]
    branch_in, out_in, grads, parts, got, own, sums, pairs, query_sum = scratch[:9]
    low_in, normed_in, result = scratch[13:]
    me = (net.me["x"] * net.sizes["c"] + net.me["c"]) * net.sizes["z"] + net.me["z"]
    half, y = 0 if net.sems is None else branch.shape[0], net.me["y"]
    loads = [net.keep(w_out, out_in)]
    for src, i in ((branch, y), (other, back(y, 1, net.sizes["y"]))):
        at = pl.ds(pl.multiple_of(i * half, half or 1), half)
        loads.append(net.keep(src, branch_in.at[at]))
    loads += [
        net.keep(all_pairs.at[i, back(me, shape[0] - 1 - j, net.sizes["n"])], pairs.at[i, j])
        for j in range(shape[0])
        for i in range(2)
    ]
    later = [net.keep(low, low_in), net.keep(normed, normed_in)]
    scatter_columns(net, grad_gate, gate_out)

    def attention():
        yield
        yield from attention_back(
            net, shape, *inside, loads, pairs_out, query_out, *scratch[:9]
        )
        busy = {}
        yield from multiply(net, dims, False, later, grad_out, branch_in, low_in, result, busy)
        yield from multiply(net, dims, False, (), grad_query, normed_in, query_out, result, busy)

    line = sum_rows(net, feed, feed_out, *scratch[9:13])
    next(line)
    together(net, attention(), line)


def gains_to_owners(net, gains, gains_out):
    x, c, z, y = (net.me[a] for a in AXES)
    n = net.sizes["n"]
    me = (x * net.sizes["c"] + c) * net.sizes["z"] + z
    for offset in range(n):
        for dy in range(net.sizes["y"]):
            slot, piece = gains_out.at[y, me], gains.at[lax.rem(me + offset, n)]
            if offset == 0 and dy == 0:
                net.keep(piece, slot)
            else:
                net.send(piece, slot, (offset, dy))


def rms_forward(values, gain_row):
    inverse = lax.rsqrt(jnp.mean(values * values, axis=-1, keepdims=True) + EPSILON)
    return (values * inverse * gain_row, inverse)


def rms_backward(values, inverse, gain_row, incoming):
    scaled = incoming * gain_row
    gain_grad = jnp.sum(incoming * values * inverse, axis=0)
    value_grad = inverse * scaled - values * inverse * inverse * inverse * jnp.mean(
        scaled * values, axis=-1, keepdims=True
    )
    return (value_grad, gain_grad)


def rope_tables(positions):
    quarter = HD // 4
    freqs = jnp.exp(-math.log(10000.0) * jnp.arange(quarter, dtype=jnp.float32) * 2.0 / (HD // 2))
    angles = positions.astype(jnp.float32)[:, None] * freqs[None, :]
    return (jnp.cos(angles), jnp.sin(angles))


def rotate(values, cosine_table, sine_table):
    quarter = cosine_table.shape[1]
    lead_part = values[..., :quarter]
    pair_part = values[..., quarter : 2 * quarter]
    tail_part = values[..., 2 * quarter :]
    cos_wide = cosine_table[:, None, :]
    sin_wide = sine_table[:, None, :]
    return jnp.concatenate(
        [
            lead_part * cos_wide - pair_part * sin_wide,
            pair_part * cos_wide + lead_part * sin_wide,
            tail_part,
        ],
        axis=-1,
    )


def segment_of(index, doc_ends):
    return jnp.sum((doc_ends[None, :] <= index[:, None]).astype(jnp.int32), axis=1)


def adam_update(weight, moment_old, square_old, gradient, rate_step, decay_rate):
    moment_new = BETA_ONE * moment_old + (1.0 - BETA_ONE) * gradient
    square_new = BETA_TWO * square_old + (1.0 - BETA_TWO) * gradient * gradient
    corrected = moment_new / (1.0 - BETA_ONE**STEP)
    corrected_square = square_new / (1.0 - BETA_TWO**STEP)
    weight_new = weight - rate_step * (
        corrected / (jnp.sqrt(corrected_square) + ADAM_EPS) + decay_rate * weight
    )
    return (moment_new, square_new, weight_new)


def body(
    sizes,
    tokens,
    cotangent,
    doc_lengths,
    w_query,
    w_keyvalue,
    w_out,
    w_gate,
    w_up,
    w_down,
    norm_gains,
    first_query,
    first_keyvalue,
    first_out,
    first_gate,
    first_up,
    first_down,
    first_gains,
    second_query,
    second_keyvalue,
    second_out,
    second_gate,
    second_up,
    second_down,
    second_gains,
):
    masters = (w_query, w_keyvalue, w_out, w_gate, w_up, w_down, norm_gains)
    firsts = (first_query, first_keyvalue, first_out, first_gate, first_up, first_down, first_gains)
    seconds = (
        second_query,
        second_keyvalue,
        second_out,
        second_gate,
        second_up,
        second_down,
        second_gains,
    )
    x, c, z, y = (lax.axis_index(a) for a in AXES)
    X, C, Z, Y, N = (sizes[a] for a in (*AXES, "n"))
    F = C * Z
    rows_w = w_query.shape[0]
    columns = w_query.shape[1]
    rows = tokens.shape[0]
    half = rows // Y
    head_count = columns // HD
    mlp_columns = w_gate.shape[1]
    width = -(-mlp_columns // (F * 128)) * 128
    device = (x * C + c) * Z + z

    def pick(values, index):
        return lax.dynamic_index_in_dim(values, index, 0, keepdims=False)

    def after(value, *others):
        return lax.optimization_barrier((value, *others))[0]

    low_gains = jnp.pad(norm_gains.astype(BF16).astype(F32), ((0, 6), (0, 0)))
    pair_weight = lax.dynamic_slice_in_dim(w_keyvalue, y * HD, HD, 1).astype(BF16)
    square, oblong = (rows_w, columns), (rows_w, mlp_columns)
    padded = (rows_w, F * width)
    g_pair, g_gains, low_query, low_out, low_gate, low_up, low_down = exchange(
        functools.partial(gather_small, 5),
        [pair_weight, low_gains, w_query, w_out, w_gate, w_up, w_down],
        [((X, C, Z, rows_w, HD), BF16), ((X, C, Z, 8, rows_w), F32)]
        + [(square, BF16)] * 2
        + [(padded, BF16)] * 3,
        sizes,
        2,
        20,
        scratch=[(square, F32)] * 2
        + [(oblong, F32)] * 3
        + [(square, BF16)] * 2
        + [(padded, BF16)] * 3,
    )
    g_pair = g_pair.reshape(D, HD)
    gain_values = g_gains.reshape(N, 8, rows_w)[:, :2].transpose(1, 0, 2).reshape(2, D)
    start_row = device * rows
    query_index = start_row + jnp.arange(rows, dtype=jnp.int32)
    doc_ends = jnp.cumsum(doc_lengths.reshape(-1))
    query_segment = segment_of(query_index, doc_ends)
    cosine_table, sine_table = rope_tables(query_index % SEQ_LEN)
    reach = (WINDOW - 1) // rows + 1
    scale = HD ** (-0.5)
    residual_in = tokens.astype(F32)
    normed_first, inverse_first = rms_forward(residual_in, gain_values[0])
    normed_first = normed_first.astype(BF16)
    pair_raw = jnp.dot(normed_first, g_pair, preferred_element_type=F32)
    own_pair = jnp.where(
        y == 0, rotate(pair_raw[:, None], cosine_table, sine_table)[:, 0], pair_raw
    ).astype(BF16)

    own_pair = with_layout_constraint(own_pair, Layout((0, 1)))
    all_pairs = lax.all_gather(own_pair, ("y", "x", "c", "z"), axis=0, tiled=True)
    g_query, g_out, g_gate, down_block = exchange(
        functools.partial(gather_weights, width),
        [after(low_query, own_pair), low_out, low_gate, low_down],
        [((X, C, Z, rows_w, columns), BF16)] * 2
        + [((X, C, Z, rows_w, Y * width), BF16), ((C, Z, rows_w, width), BF16)],
        sizes,
        1,
        130,
    )
    g_query, g_out = g_query.reshape(D, columns), g_out.reshape(D, columns)
    g_gate = g_gate.reshape(D, Y * width)
    cotangent_half = pick(cotangent.reshape(Y, half, D), y)
    all_pairs = all_pairs.reshape(Y, N, rows, HD)
    key_index = start_row - reach * rows + jnp.arange((reach + 1) * rows, dtype=jnp.int32)
    key_segment = segment_of(key_index, doc_ends)
    allowed = (
        (query_segment[:, None] == key_segment[None, :])
        & (key_index[None, :] <= query_index[:, None])
        & (query_index[:, None] - key_index[None, :] < WINDOW)
        & (key_index[None, :] >= 0)
    )
    bias = jnp.where(allowed.T, 0.0, -jnp.inf).astype(BF16).reshape(reach + 1, rows, rows)
    cosine_wide = jnp.concatenate([cosine_table, cosine_table], axis=1)
    sine_wide = jnp.concatenate([-sine_table, sine_table], axis=1)
    tokens_half = pick(tokens.reshape(Y, half, D), y)
    query_rot, attended, attended_low, log_total, middle, normed_all, g_up = exchange(
        functools.partial(attention_forward, width, (reach + 1, head_count, rows)),
        [
            normed_first,
            cosine_wide,
            sine_wide,
            bias,
            tokens_half,
            gain_values[1:],
            g_query,
            g_out,
            all_pairs,
            low_up,
        ],
        [
            ((rows, columns), BF16),
            ((rows, columns), F32),
            ((rows, columns), BF16),
            ((head_count, 1, rows), F32),
            ((half, D), F32),
            ((C, Z, half, D), BF16),
            ((X, C, Z, rows_w, Y * width), BF16),
        ],
        sizes,
        3,
        90,
        scratch=[
            ((D, columns), BF16),
            ((D, columns), BF16),
            ((2, reach + 1, rows, HD), BF16),
            ((2, reach + 1, rows, rows), F32),
            ((half, D), BF16),
            ((half, D), BF16),
            ((half, D), BF16),
            ((reach + 1, HD, rows), BF16),
        ],
        in_vmem=range(5),
        arrays_in_vmem=range(6),
    )
    inverse_second = lax.rsqrt(jnp.mean(middle * middle, axis=-1, keepdims=True) + EPSILON)
    normed_all = normed_all.reshape(F * half, D)
    g_up = g_up.reshape(D, Y * width)
    wide, tall = (F * half, Y * width), (D, Y * width)
    down_grad, g_down, active, up_slope, hidden = exchange(
        functools.partial(mlp_forward, width),
        [cotangent_half.astype(BF16), down_block, normed_all, g_gate, g_up],
        [((C, Z, half, D), BF16), ((X, C, Z, rows_w, Y * width), BF16)]
        + [(wide, F32), (wide, F32), (wide, BF16)],
        sizes,
        4,
        50,
        scratch=[
            ((F * half, D), BF16),
            (tall, BF16),
            (tall, BF16),
            (wide, F32),
            (wide, F32),
            (wide, BF16),
        ],
    )
    down_grad = down_grad.reshape(F * half, D)
    g_down = g_down.reshape(D, Y * width)
    hidden_grad = jnp.dot(down_grad, g_down, preferred_element_type=F32)
    gate_grad = (hidden_grad * up_slope).astype(BF16)
    up_grad = (hidden_grad * active).astype(BF16)

    def weight_grad(left, right):
        sides = [
            lax.dot_general(
                left,
                right[:, i * width : (i + 1) * width],
                CONTRACT_FIRST,
                preferred_element_type=F32,
            ).astype(BF16)
            for i in range(Y)
        ]
        return jnp.stack(sides).reshape(Y * X, C, Z, rows_w, width)

    whole_down = weight_grad(down_grad, hidden)

    def over_y_x(whole_grad):
        return lax.psum_scatter(
            whole_grad, ("y", "x"), scatter_dimension=0, tiled=True
        ).reshape(F, rows_w, width)

    whole_gate = weight_grad(normed_all, gate_grad)
    part_down, part_gate = over_y_x(whole_down), over_y_x(whole_gate)
    second_grad, whole_up, feed_part = exchange(
        functools.partial(sum_second, (Y, D, width)),
        [after(gate_grad, whole_down, whole_gate), up_grad, g_gate, g_up, normed_all, hidden, g_down],
        [((half, D), F32), ((Y, D, width), BF16), ((F * half, D), BF16)],
        sizes,
        5,
        65,
        scratch=[((Z, half, D), BF16)] * 5
        + [(wide, BF16)] * 2
        + [(tall, BF16)] * 2
        + [((F * half, D), BF16), (wide, BF16), (tall, BF16)]
        + [((Y, D, width), BF16), ((F * half, D), BF16)],
        in_vmem=(0,),
    )
    part_up = over_y_x(whole_up.reshape(Y * X, C, Z, rows_w, width))

    def whole(own, other):
        return jnp.where(
            y == 0, jnp.concatenate([own, other]), jnp.concatenate([other, own])
        )

    middle_norm_grad, gain_two = rms_backward(middle, inverse_second, gain_values[1], second_grad)
    middle_grad = cotangent_half + middle_norm_grad
    branch_half = middle_grad.astype(BF16)
    branch_in, new_down = exchange(
        swap_rows_scatter,
        [branch_half, part_down.reshape(C, Z, rows_w, width)],
        [((half, D), BF16), ((rows_w, F * width), BF16)],
        sizes,
        7,
        35,
    )
    pair_parts, query_grad, feed_out, grad_out, grad_query, new_gate = exchange(
        functools.partial(
            attention_back_sum_feed, (reach + 1, head_count, rows), (1, D, columns)
        ),
        [
            query_rot,
            bias,
            log_total,
            attended,
            cosine_wide,
            sine_wide,
            all_pairs,
            branch_half,
            branch_in,
            g_out,
            attended_low,
            normed_first,
            feed_part.reshape(C, Z, half, D),
            part_gate.reshape(C, Z, rows_w, width),
        ],
        [
            ((reach + 1, rows, HD), BF16),
            ((rows, columns), BF16),
            ((half, D), F32),
            ((1, D, columns), BF16),
            ((1, D, columns), BF16),
            ((rows_w, F * width), BF16),
        ],
        sizes,
        8,
        95,
        scratch=[
            ((rows, D), BF16),
            ((D, columns), BF16),
            ((rows, columns), BF16),
            ((2, reach + 1, rows, HD), BF16),
            ((reach + 1, rows, HD), BF16),
            ((reach + 1, rows, HD), BF16),
            ((2, rows, HD), F32),
            ((2, reach + 1, rows, HD), BF16),
            ((columns, rows), F32),
        ]
        + [((Z, half, D), BF16)] * 4
        + [((rows, columns), BF16), ((rows, D), BF16), ((1, D, columns), BF16)],
        in_vmem=(1, 2),
        arrays_in_vmem=range(6),
    )
    mixed_half = middle + feed_out
    pair_total = jnp.sum(pair_parts.astype(F32), axis=0)
    pair_total = jnp.where(
        y == 0, rotate(pair_total[:, None], cosine_table, -sine_table)[:, 0], pair_total
    ).astype(BF16)
    first_part = (
        lax.dot_general(query_grad, g_query, CONTRACT_LAST, preferred_element_type=F32)
        + lax.dot_general(pair_total, g_pair, CONTRACT_LAST, preferred_element_type=F32)
    )
    gain_one = jnp.sum(first_part * residual_in * inverse_first, axis=0)
    first_part = first_part.astype(BF16)
    grad_gains = jnp.pad(
        jnp.stack([gain_one, gain_two]).reshape(2, N, rows_w).transpose(1, 0, 2),
        ((0, 0), (0, 6), (0, 0)),
    )
    grad_pair = lax.dot_general(
        normed_first, pair_total, CONTRACT_FIRST, preferred_element_type=F32
    ).astype(BF16)
    attention_grads = [
        g.reshape(X, C, Z, rows_w, -1) for g in (grad_query, grad_out, grad_pair)
    ]
    widths = (columns, columns, HD)
    (
        reduced_query,
        reduced_out,
        reduced_half,
        first_in,
        middle_in,
        mixed_in,
        gain_parts,
        half_in,
        new_up,
    ) = exchange(
        sum_weights,
        [
            *attention_grads,
            first_part,
            middle_grad,
            mixed_half,
            grad_gains,
            part_up.reshape(C, Z, rows_w, width),
        ],
        [((rows_w, w), F32) for w in widths]
        + [((rows, D), BF16), ((half, D), F32), ((half, D), F32), ((Y, N, 8, rows_w), F32)]
        + [((rows_w, HD), F32), ((rows_w, F * width), BF16)],
        sizes,
        9,
        110,
        scratch=[((X, Z, rows_w, w), BF16) for w in widths] * 2
        + [((X - 1, Z, rows_w, w), BF16) for w in widths]
        + [((Z - 1, rows_w, w), BF16) for w in widths],
        in_vmem=(0, 1, 2),
    )
    first_grad = first_part.astype(F32) + first_in.astype(F32)
    input_norm_grad, _ = rms_backward(residual_in, inverse_first, gain_values[0], first_grad)
    token_grad = whole(middle_grad, middle_in) + input_norm_grad
    mixed = whole(mixed_half, mixed_in)
    reduced_gains = jnp.sum(gain_parts, axis=(0, 1))[:2]
    reduced_mlp = [g[:, :mlp_columns].astype(F32) for g in (new_gate, new_up, new_down)]
    reduced_pair = jnp.where(
        y == 0,
        jnp.concatenate([reduced_half, half_in], axis=1),
        jnp.concatenate([half_in, reduced_half], axis=1),
    )
    reduced = (reduced_query, reduced_pair, reduced_out, *reduced_mlp, reduced_gains)
    dense_rate = 2.0 * D ** (-0.5)
    out_rate = 2.0 * max(1, H * HD // 64) ** (-0.5)
    rates = (dense_rate, dense_rate, out_rate, dense_rate, dense_rate, dense_rate, 0.4)
    decays = (DECAY, DECAY, DECAY, DECAY, DECAY, DECAY, 0.0)
    new_firsts = []
    new_seconds = []
    updated = []
    for weight, moment_old, square_old, gradient, rate_step, decay_rate in zip(
        masters, firsts, seconds, reduced, rates, decays
    ):
        moment_new, square_new, weight_new = adam_update(
            weight, moment_old, square_old, gradient, rate_step, decay_rate
        )
        new_firsts.append(moment_new)
        new_seconds.append(square_new)
        updated.append(weight_new)
    return (mixed, token_grad, *new_firsts, *new_seconds, *updated)


def solution(mesh):
    shape = dict(mesh.shape)
    sizes = {"x": shape["dp"] // 2, "c": 2, "z": shape["group"], "y": shape["tensor"]}
    sizes["n"] = sizes["x"] * sizes["c"] * sizes["z"]
    grid = Mesh(mesh.devices.reshape([sizes[a] for a in AXES]), AXES)
    blocks = ("x", "c", "z")
    by_rows, by_both, gains = P(blocks, None), P(blocks, "y"), P(None, blocks)
    weights = (by_both, by_rows, by_both, by_both, by_both, by_both, gains)
    return jax.shard_map(
        functools.partial(body, sizes),
        mesh=grid,
        in_specs=(by_rows, by_rows, P(), *weights * 3),
        out_specs=(by_rows, by_rows, *weights * 3),
        check_vma=False,
    )
```

```python
import functools
import math

import jax
import jax.numpy as jnp
from jax import lax
from jax.experimental import pallas as pl
from jax.experimental.layout import Layout, with_layout_constraint
from jax.experimental.pallas import tpu as pltpu
from jax.sharding import Mesh
from jax.sharding import PartitionSpec as P

D = 2560
H = 10
HD = 256
WINDOW = 2048
SEQ_LEN = 4096
STEP = 10

EPSILON = 1e-06
BETA_ONE = 0.9
BETA_TWO = 0.95
ADAM_EPS = 1e-08
DECAY = 0.1
CONTRACT_LAST = (((1,), (1,)), ((), ()))
CONTRACT_FIRST = (((0,), (0,)), ((), ()))
BF16 = jnp.bfloat16
F32 = jnp.float32
AXES = ("x", "c", "z", "y")


class Blank:
    @property
    def at(self):
        return self

    def __getitem__(self, _):
        return self

    def landed(self):
        pass


def guarded(condition, step):
    if condition is None:
        step()
    else:
        pl.when(condition)(step)


class Copy:
    def __init__(self, copy, sends, comes):
        self.copy, self.sends, self.comes, self.arrived = copy, sends, comes, False

    def landed(self):
        if not self.arrived:
            guarded(self.comes, self.copy.wait_recv)
            self.arrived = True

    def done(self):
        self.landed()
        guarded(self.sends, self.copy.wait_send)


class Local:
    def __init__(self, copy):
        self.copy, self.arrived = copy, False

    def landed(self):
        if not self.arrived:
            self.copy.wait()
            self.arrived = True

    def done(self):
        self.landed()


class Net:
    def __init__(self, sizes, me, sems):
        self.sizes, self.me, self.sems = sizes, me, sems
        self.sent, self.kept, self.peers, self.open = 0, 0, [], []

    def device(self, where):
        s, me = self.sizes, self.me
        if len(where) == 4:
            return {a: lax.rem(me[a] + d, s[a]) for a, d in zip(AXES, where)}
        flat = lax.rem((me["x"] * s["c"] + me["c"]) * s["z"] + me["z"] + where[0], s["n"])
        return {
            "x": flat // (s["c"] * s["z"]),
            "c": lax.rem(flat // s["z"], s["c"]),
            "z": lax.rem(flat, s["z"]),
            "y": lax.rem(me["y"] + where[1], s["y"]),
        }

    def opposite(self, where):
        if len(where) == 4:
            return tuple((self.sizes[a] - d) % self.sizes[a] for a, d in zip(AXES, where))
        return ((self.sizes["n"] - where[0]) % self.sizes["n"], (self.sizes["y"] - where[1]) % self.sizes["y"])

    def send(self, src, dst, where, sends=None, comes=None, now=True):
        k = self.sent
        self.sent += 1
        if self.sems is None:
            for w in (where, self.opposite(where)):
                if w not in self.peers:
                    self.peers.append(w)
            return Blank()
        copy = pltpu.make_async_remote_copy(
            src_ref=src,
            dst_ref=dst,
            send_sem=self.sems[0].at[k],
            recv_sem=self.sems[1].at[k],
            device_id=self.device(where),
            device_id_type=pl.DeviceIdType.MESH,
        )
        self.open.append(Copy(copy, sends, comes))
        if now:
            guarded(sends, copy.start)
        return self.open[-1]

    def keep(self, src, dst):
        k = self.kept
        self.kept += 1
        if self.sems is None:
            return Blank()
        copy = pltpu.make_async_copy(src, dst, self.sems[2].at[k])
        copy.start()
        self.open.append(Local(copy))
        return self.open[-1]

    def add(self, rows, step):
        if self.sems is not None:
            some = 16 if rows % 16 == 0 else rows

            def one(i, carry):
                step(pl.ds(pl.multiple_of(i * some, some), some))
                return carry

            lax.fori_loop(0, rows // some, one, 0)

    def greet(self, peers):
        barrier = pltpu.get_barrier_semaphore()
        for where in peers:
            pl.semaphore_signal(
                barrier, inc=1, device_id=self.device(where), device_id_type=pl.DeviceIdType.MESH
            )
        pl.semaphore_wait(barrier, len(peers))

    def finish(self):
        for item in self.open:
            item.done()


def exchange(plan, arrays, outs, sizes, number, micros, scratch=(), in_vmem=(), arrays_in_vmem=()):
    count = Net(sizes, {a: 0 for a in AXES}, None)
    plan(count, *[Blank()] * (len(arrays) + len(outs) + len(scratch)))

    def kernel(*refs):
        data, sems = refs[:-3], refs[-3:]
        net = Net(sizes, {a: lax.axis_index(a) for a in AXES}, sems)
        net.greet(count.peers)
        plan(net, *data)
        net.finish()

    anywhere = pl.BlockSpec(memory_space=pl.ANY)
    inside = pl.BlockSpec(memory_space=pltpu.VMEM)
    return pl.pallas_call(
        kernel,
        out_shape=[jax.ShapeDtypeStruct(shape, dtype) for shape, dtype in outs],
        in_specs=[inside if i in arrays_in_vmem else anywhere for i in range(len(arrays))],
        out_specs=[inside if i in in_vmem else anywhere for i in range(len(outs))],
        scratch_shapes=[
            *(pltpu.VMEM(shape, dtype) for shape, dtype in scratch),
            pltpu.SemaphoreType.DMA((count.sent,)),
            pltpu.SemaphoreType.DMA((count.sent,)),
            pltpu.SemaphoreType.DMA((max(1, count.kept),)),
        ],
        compiler_params=pltpu.CompilerParams(
            collective_id=number, has_side_effects=True, vmem_limit_bytes=56 * 2**20
        ),
        cost_estimate=pl.CostEstimate(
            flops=0, bytes_accessed=micros * 3_600_000, transcendentals=0
        ),
    )(*arrays)


SIBLING = (0, 1, 0, 0)
OTHER_Y = (0, 0, 0, 1)


def back(value, step, size):
    return lax.rem(value + size - step, size)


def along_line(net, pairs):
    z, size = net.me["z"], net.sizes["z"]

    def up(pair, step):
        slot = pair[1](back(z, step, size))
        return net.send(
            slot if step else pair[0],
            slot,
            (0, 0, 1, 0),
            sends=(z + 1 < size) & (z - step >= 0),
            comes=z - 1 - step >= 0,
        )

    def down(pair, step):
        slot = pair[1](lax.rem(z + step, size))
        return net.send(
            slot if step else pair[0],
            slot,
            (0, 0, size - 1, 0),
            sends=(z >= 1) & (z + step < size),
            comes=z + 1 + step < size,
        )

    moves = [(up(pair, 0), down(pair, 0)) for pair in pairs]

    def steps():
        for step in range(size - 1):
            for i, pair in enumerate(pairs):
                rising, falling = moves[i]
                rising.landed()
                if step + 1 < size - 1:
                    rising = up(pair, step + 1)
                yield i, (back(z, step + 1, size), z - 1 - step >= 0)
                falling.landed()
                if step + 1 < size - 1:
                    falling = down(pair, step + 1)
                yield i, (lax.rem(z + step + 1, size), z + 1 + step < size)
                moves[i] = (rising, falling)

    return steps()


def gather_x_c_z(net, pairs):
    x, c, z = (net.me[a] for a in "xcz")
    xs = net.sizes["x"]
    line = along_line(net, [(src, lambda j, dst=dst: dst.at[x, c, j]) for src, dst in pairs])
    across = []

    def onward(src, slot, condition):
        for dx in range(1, xs):
            copy = net.send(src, slot(x), (dx, 0, 0, 0), sends=condition, comes=condition)
            across.append((copy, slot(back(x, dx, xs)), condition))
        net.send(src, slot(x), SIBLING, sends=condition, comes=condition)

    for src, dst in pairs:
        net.keep(src, dst.at[x, c, z])
        onward(src, lambda px, dst=dst: dst.at[px, c, z], None)
    yield
    for count, (i, (j, condition)) in enumerate(line):
        dst = pairs[i][1]
        onward(dst.at[x, c, j], lambda px, dst=dst, j=j: dst.at[px, c, j], condition)
        yield
    for copy, slot, condition in across:
        copy.landed()
        net.send(slot, slot, SIBLING, sends=condition, comes=condition)


def gather_small(count, net, *refs):
    weights, outs = refs[2 : 2 + count], refs[4 + count : 4 + 2 * count]
    inside, rounded = refs[4 + 2 * count : 4 + 3 * count], refs[4 + 3 * count :]
    gather = gather_x_c_z(net, list(zip(refs[:2], refs[2 + count : 4 + count])))
    next(gather)
    loads = [net.keep(src, dst) for src, dst in zip(weights, inside)]

    def casts():
        for load, src, dst, out in zip(loads, inside, rounded, outs):
            load.landed()

            def cast(at, src=src, dst=dst):
                columns = src.shape[1]
                dst[at, :columns] = src[at].astype(BF16)
                if dst.shape[1] > columns:
                    few = (src[at].shape[0], dst.shape[1] - columns)
                    dst[at, columns:] = jnp.zeros(few, BF16)

            net.add(0 if net.sems is None else src.shape[0], cast)
            net.keep(dst, out)
            yield

    together(net, gather, casts())


def gather_weights(width, net, *refs):
    w_query, w_out, gate, down, query_out, out_out, gate_out, down_block = refs
    mlp = gather_mlp(net, width, gate, gate_out)
    weights = gather_x_c_z(net, [(w_query, query_out), (w_out, out_out)])
    next(mlp)
    next(weights)
    for _ in range(net.sizes["c"] * net.sizes["z"]):
        next(mlp)
    scatter_block(net, width, down, down_block)
    together(net, weights, mlp)


def gather_rows(net, rows, all_rows):
    c, z = net.me["c"], net.me["z"]
    line = along_line(net, [(rows, lambda j: all_rows.at[c, j])])
    net.keep(rows, all_rows.at[c, z])
    net.send(rows, all_rows.at[c, z], SIBLING)
    yield
    for _, (j, condition) in line:
        slot = all_rows.at[c, j]
        net.send(slot, slot, SIBLING, sends=condition, comes=condition)
        yield


def scatter_block(net, width, src, out):
    c, z = net.me["c"], net.me["z"]
    cs, zs = net.sizes["c"], net.sizes["z"]
    net.keep(src.at[:, pl.ds((c * zs + z) * width, width)], out.at[c, z])
    for dz in far_first(zs):
        for dc in range(cs):
            if dz or dc:
                f = lax.rem(c + dc, cs) * zs + lax.rem(z + dz, zs)
                net.send(src.at[:, pl.ds(f * width, width)], out.at[c, z], (0, dc, dz, 0))


def gather_block(net, width, block, out):
    x, y = net.me["x"], net.me["y"]
    xs, cs, ys = (net.sizes[a] for a in "xcy")

    def slot(px, py, i, j):
        return out.at[px, i, j, :, pl.ds(py * width, width)]

    next_x, next_y = [], []
    for j in range(net.sizes["z"]):
        for i in range(cs):
            src = block.at[i, j]
            net.keep(src, slot(x, y, i, j))
            for dx in range(1, xs):
                copy = net.send(src, slot(x, y, i, j), (dx, 0, 0, 0))
                if i % 2 == 0:
                    next_y.append((copy, slot(back(x, dx, xs), y, i, j)))
            copy = net.send(src, slot(x, y, i, j), OTHER_Y)
            if i % 2 == 1:
                next_x.append((copy, slot(x, back(y, 1, ys), i, j)))
    yield
    for copy, ref in next_y:
        copy.landed()
        net.send(ref, ref, OTHER_Y)
        yield
    for copy, ref in next_x:
        copy.landed()
        for dx in range(1, xs):
            net.send(ref, ref, (dx, 0, 0, 0))
        yield


def gather_mlp(net, width, src, out):
    x, c, z, y = (net.me[a] for a in AXES)
    xs, cs, zs, ys = (net.sizes[a] for a in AXES)

    def slot(px, py, i, j):
        return out.at[px, i, j, :, pl.ds(py * width, width)]

    got = []
    for dz in far_first(zs):
        for dc in range(cs):
            if dz or dc:
                f = lax.rem(c + dc, cs) * zs + lax.rem(z + dz, zs)
                copy = net.send(
                    src.at[:, pl.ds(f * width, width)], slot(x, y, c, z), (0, dc, dz, 0)
                )
                got.append((copy, back(c, dc, cs), back(z, dz, zs)))
    own = src.at[:, pl.ds((c * zs + z) * width, width)]
    net.keep(own, slot(x, y, c, z))
    next_x, next_y = [], []

    def onward(block, i, j, x_first):
        for dx in range(1, xs):
            copy = net.send(block, slot(x, y, i, j), (dx, 0, 0, 0))
            if x_first:
                next_y.append((copy, slot(back(x, dx, xs), y, i, j)))
        copy = net.send(block, slot(x, y, i, j), OTHER_Y)
        if not x_first:
            next_x.append((copy, slot(x, back(y, 1, ys), i, j)))

    yield
    onward(own, c, z, True)
    yield
    for count, (copy, i, j) in enumerate(got):
        copy.landed()
        onward(slot(x, y, i, j), i, j, count % 2 == 1)
        yield
    for copy, ref in next_y:
        copy.landed()
        net.send(ref, ref, OTHER_Y)
        yield
    for copy, ref in next_x:
        copy.landed()
        for dx in range(1, xs):
            net.send(ref, ref, (dx, 0, 0, 0))
        yield


def attention_forward(width, shape, net, *refs):
    normed, cosine, sine, bias, tokens, gain, w_query, w_out, pairs, up = refs[:10]
    queries, attended, attended_low, lse, middle, all_rows, all_up = refs[10:17]
    query_in, out_in, near, table, part_out, part_in, normed_out, flipped = refs[17:]
    blocks, heads, rows = shape
    x, c, z, y = (net.me[a] for a in AXES)
    n, ys = net.sizes["n"], net.sizes["y"]
    half = rows // ys
    mlp = gather_mlp(net, width, up, all_up)
    next(mlp)
    loads = [net.keep(w_query, query_in), net.keep(w_out, out_in)]
    me = (x * net.sizes["c"] + c) * net.sizes["z"] + z
    for j in range(blocks):
        for side in range(2):
            loads.append(net.keep(pairs.at[side, back(me, blocks - 1 - j, n)], near.at[side, j]))
    next(mlp)

    def head(h):
        at = pl.ds(h * HD, HD)
        raw = jnp.dot(normed[...], query_in[:, at], preferred_element_type=F32)
        turned = raw[:, : HD // 2]
        turned = turned * cosine[...] + pltpu.roll(turned, HD // 4, 1) * sine[...]
        queries[:, at] = (
            jnp.concatenate([turned, raw[:, HD // 2 :]], axis=1) * HD ** (-0.5)
        ).astype(BF16)
        query = queries[:, at]
        top = None
        for j in range(blocks):
            scores = lax.dot_general(near[0, j], query, CONTRACT_LAST, preferred_element_type=F32)
            scores = scores + bias[j].astype(F32)
            table[h % 2, j] = scores
            best = jnp.max(scores, axis=0, keepdims=True)
            top = best if top is None else jnp.maximum(top, best)
        total = jnp.zeros_like(top)
        result = jnp.zeros((HD, rows), F32)
        for j in range(blocks):
            grown = jnp.exp(table[h % 2, j] - top)
            total = total + jnp.sum(grown, axis=0, keepdims=True)
            result = result + jnp.dot(
                flipped[j], grown.astype(BF16), preferred_element_type=F32
            )
        lse[h] = top + jnp.log(total)
        result = (result / total).T
        attended[:, at] = result
        attended_low[:, at] = result.astype(BF16)

    some = 256

    def project(i, carry):
        at = pl.ds(pl.multiple_of(i * some, some), some)
        both = lax.dot_general(
            attended_low[...], out_in[at], CONTRACT_LAST, preferred_element_type=F32
        )
        first, second = both[:half], both[half:]
        part_out[:, at] = jnp.where(y == 0, second, first).astype(BF16)
        middle[:, at] = tokens[:, at].astype(F32) + jnp.where(y == 0, first, second)
        return carry

    for load in loads:
        load.landed()
    if net.sems is not None:
        for j in range(blocks):
            flipped[j] = near[1, j].T
        for h in range(heads):
            head(h)
        lax.fori_loop(0, D // some, project, 0)
    swap = net.send(part_out, part_in, OTHER_Y)
    for _ in range(3):
        next(mlp)
    swap.landed()

    def norm(at):
        values = middle[at] + part_in[at].astype(F32)
        middle[at] = values
        inverse = lax.rsqrt(jnp.mean(values * values, axis=-1, keepdims=True) + EPSILON)
        normed_out[at] = (values * inverse * gain[...]).astype(BF16)

    net.add(half, norm)
    together(net, gather_rows(net, normed_out, all_rows), mlp)


def mlp_forward(width, net, rows, block, normed, gate, up, all_rows, all_blocks, *refs):
    outs, (normed_in, gate_in, up_in), results = refs[:3], refs[3:6], refs[6:9]

    def products():
        first = net.keep(normed, normed_in)
        some, tiles = 512, 2
        if net.sems is not None:
            tiles = gate.shape[1] // some
        ats = [pl.ds(i * some, some) for i in range(tiles)]
        loads = [
            (net.keep(gate.at[:, at], gate_in.at[:, at]), net.keep(up.at[:, at], up_in.at[:, at]))
            for at in ats
        ]
        yield
        first.landed()
        for at, pair in zip(ats, loads):
            for load in pair:
                load.landed()
            if net.sems is not None:
                results[0][:, at] = jnp.dot(
                    normed_in[...], gate_in[:, at], preferred_element_type=F32
                )
            yield
            if net.sems is not None:
                results[1][:, at] = jnp.dot(
                    normed_in[...], up_in[:, at], preferred_element_type=F32
                )
            yield
            if net.sems is not None:
                gate_pre, up_pre = results[0][:, at], results[1][:, at]
                factor = math.sqrt(2.0 / math.pi)
                square = gate_pre * gate_pre
                bent = jnp.tanh(factor * gate_pre * (1.0 + 0.044715 * square))
                share = 0.5 + 0.5 * bent
                active = gate_pre * share
                slope = share + 0.5 * gate_pre * (1.0 - bent * bent) * factor * (
                    1.0 + 3.0 * 0.044715 * square
                )
                results[0][:, at] = active
                results[1][:, at] = up_pre * slope
                results[2][:, at] = (active * up_pre).astype(BF16)
            for result, out in zip(results, outs):
                net.keep(result.at[:, at], out.at[:, at])
            yield

    together(
        net,
        products(),
        (gather_rows(net, rows, all_rows), 2),
        gather_block(net, width, block, all_blocks),
    )


def together(net, *plans):
    plans = [plan if isinstance(plan, tuple) else (plan, 1) for plan in plans]
    while plans:
        for entry in list(plans):
            for _ in range(entry[1]):
                if next(entry[0], plans) is plans:
                    plans.remove(entry)
                    break


def far_first(size):
    return sorted(range(size), key=lambda d: -min(d, size - d))


def ends_first(size):
    return sorted(range(size), key=lambda t: min(t, size - 1 - t))


def add_low(net, target, other, rows):
    def step(at):
        target[at] = (target[at].astype(F32) + other[at].astype(F32)).astype(BF16)

    net.add(rows, step)


def sum_along_line(net, own, rising, falling, rows):
    z, size = net.me["z"], net.sizes["z"]
    ups = [(t, True) for t in range(size - 1, 0, -1)]
    downs = [(t, False) for t in range(size - 1)]
    copies = {}
    for t, up in ups + downs:
        copies[t, up] = net.send(
            own.at[t],
            (rising if up else falling).at[t],
            (0, 0, 1 if up else size - 1, 0),
            sends=(z < t) if up else (z > t),
            comes=((z > 0) & (z <= t)) if up else ((z < size - 1) & (z >= t)),
            now=False,
        )

    def take(t, up):
        copies[t, up].copy.wait_recv()
        add_low(net, own.at[t], (rising if up else falling).at[t], rows)

    def move(t, up):
        inner = ((z > 0) & (z < t)) if up else ((z < size - 1) & (z > t))

        def onward():
            take(t, up)
            copies[t, up].copy.start()

        pl.when(inner)(onward)

    def from_ends(count, skip):
        if net.sems is not None:
            for step in list(zip(ups, downs))[skip : skip + count]:
                for end, key in zip((0, size - 1), step):
                    pl.when(z == end)(copies[key].copy.start)

    from_ends(1, 0)
    yield
    from_ends(size, 1)
    for first, second in zip(ups + downs, downs + ups):
        if net.sems is not None:
            pl.when(z < size // 2)(lambda: move(*first))
            pl.when(z >= size // 2)(lambda: move(*second))
        yield
    for t, up in ups + downs:
        if net.sems is not None:
            last = (z == t) & ((z > 0) if up else (z < size - 1))
            pl.when(last)(lambda: take(t, up))
            copies[t, up].arrived = True
        yield


def sum_products(net, produce, out, part, own, got, rising, falling):
    z, zs = net.me["z"], net.sizes["z"]
    rows = 0 if net.sems is None else out.shape[0]
    line = sum_along_line(net, own, rising, falling, rows)
    order = ends_first(zs)
    for some in (order[:2], order[2:]):
        ready = {}
        for t in some:
            produce(t)
            ready[t] = net.send(part.at[t], got.at[t], SIBLING)
        for t in some:
            ready[t].landed()
            add_low(net, own.at[t], got.at[t], rows)
        if some[0] == order[0]:
            next(line)
    yield from line

    def result(at):
        out[at] = own[z, at].astype(F32)

    net.add(rows, result)


def sum_rows(net, part, out, own, got, rising, falling):
    c, z = net.me["c"], net.me["z"]
    zs = net.sizes["z"]
    rows = 0 if net.sems is None else out.shape[0]
    ready = {}
    for t in ends_first(zs):
        ready[t] = (
            net.send(part.at[lax.rem(c + 1, net.sizes["c"]), t], got.at[t], SIBLING),
            net.keep(part.at[c, t], own.at[t]),
        )
    yield
    for t in ends_first(zs):
        for copy in ready[t]:
            copy.landed()
        add_low(net, own.at[t], got.at[t], rows)
    yield from sum_along_line(net, own, rising, falling, rows)

    def result(at):
        out[at] = own[z, at].astype(F32)

    net.add(rows, result)


def sum_weights(net, *refs):
    x, c, z, y = (net.me[a] for a in AXES)
    xs, cs, zs = (net.sizes[a] for a in "xcz")
    sources, swapped, gains, grad_up = refs[0:3], refs[3:6], refs[6], refs[7]
    outs, swapped_out, gains_out, other_pair = refs[8:11], refs[11:14], refs[14], refs[15]
    up_out = refs[16]
    own, got, from_x, from_z = (refs[17 + 3 * i : 20 + 3 * i] for i in range(4))
    rows = 0 if net.sems is None else outs[0].shape[0]
    order = far_first(zs)
    ready = {}
    for dx in [*range(1, xs), 0]:
        i = lax.rem(x + dx, xs)
        for dz in order:
            j = lax.rem(z + dz, zs)
            for k in range(3):
                ready[dx, dz, k] = (
                    net.send(
                        sources[k].at[i, lax.rem(c + 1, cs), j], got[k].at[i, j], SIBLING
                    ),
                    net.keep(sources[k].at[i, c, j], own[k].at[i, j]),
                )
    for src, dst in zip(swapped, swapped_out):
        net.send(src, dst, OTHER_Y)
    gains_to_owners(net, gains, gains_out)
    scatter_columns(net, grad_up, up_out)
    over = {}
    for dx in range(1, xs):
        i = lax.rem(x + dx, xs)
        for dz in order:
            j = lax.rem(z + dz, zs)
            for k in range(3):
                for copy in ready[dx, dz, k]:
                    copy.landed()

                def pair(at, mine=own[k], other=got[k], i=i, j=j):
                    mine[i, j, at] = (
                        mine[i, j, at].astype(F32) + other[i, j, at].astype(F32)
                    ).astype(BF16)

                net.add(rows, pair)
                over[dx, dz, k] = net.send(
                    own[k].at[i, j], from_x[k].at[dx - 1, j], (dx, 0, 0, 0)
                )
    sent = {}
    for dz in order:
        j = lax.rem(z + dz, zs)
        for k in range(3):
            for copy in ready[0, dz, k]:
                copy.landed()
            for dx in range(1, xs):
                over[dx, dz, k].landed()

            def chips(at, mine=own[k], other=got[k], far=from_x[k], j=j):
                total = mine[x, j, at].astype(F32) + other[x, j, at].astype(F32)
                for dx in range(1, xs):
                    total = total + far[dx - 1, j, at].astype(F32)
                return total

            if dz:

                def keep_low(at, mine=own[k], chips=chips, j=j):
                    mine[x, j, at] = chips(at).astype(BF16)

                net.add(rows, keep_low)
                sent[dz, k] = net.send(own[k].at[x, j], from_z[k].at[dz - 1], (0, 0, dz, 0))
            else:

                def keep_wide(at, out=outs[k], chips=chips):
                    out[at] = chips(at)

                net.add(rows, keep_wide)
    for k in (2, 0, 1):
        for dz in order[:-1]:
            sent[dz, k].landed()

            def more(at, out=outs[k], far=from_z[k], dz=dz):
                out[at] += far[dz - 1, at].astype(F32)

            net.add(rows, more)
        if k == 2:
            net.send(outs[2], other_pair, OTHER_Y)


def swap_y(net, *refs):
    count = len(refs) // 2
    for src, dst in zip(refs[:count], refs[count:]):
        net.send(src, dst, OTHER_Y)


def scatter_columns(net, src, dst):
    c, z = net.me["c"], net.me["z"]
    cs, zs = net.sizes["c"], net.sizes["z"]
    width = 0 if net.sems is None else src.shape[-1]
    slot = dst.at[:, pl.ds((c * zs + z) * width, width)]
    net.keep(src.at[c, z], slot)
    for dz in range(zs):
        for dc in range(cs):
            if dz or dc:
                piece = src.at[lax.rem(c + dc, cs), lax.rem(z + dz, zs)]
                net.send(piece, slot, (0, dc, dz, 0))


def swap_rows_scatter(net, rows, grad, rows_out, grad_out):
    swap_y(net, rows, rows_out)
    scatter_columns(net, grad, grad_out)


def attention_back(
    net, shape, queries, bias, lse, attended, cosine, sine, loads, out, query_out, branch, w_out, grads, parts, got,
    own, sums, pairs, query_sum
):
    y, n = net.me["y"], net.sizes["n"]
    blocks, heads, rows = shape
    for load in loads:
        load.landed()
    delta = []
    if net.sems is not None:
        for h in range(heads):
            at = pl.ds(h * HD, HD)
            grad = jnp.dot(branch[...], w_out[:, at], preferred_element_type=F32).astype(BF16)
            grads[:, at] = grad
            delta.append(
                jnp.sum((grad.astype(F32) * attended[:, at]).T, axis=0, keepdims=True)
            )

    def block(j, carry):
        keys, values, hidden = pairs[0, j], pairs[1, j], bias[j].astype(F32)
        flipped = keys.T
        for h in range(heads):
            at = pl.ds(h * HD, HD)
            query, grad = queries[:, at], grads[:, at]
            scores = lax.dot_general(keys, query, CONTRACT_LAST, preferred_element_type=F32)
            probs = jnp.exp(scores + hidden - lse[h])
            prob_grad = lax.dot_general(values, grad, CONTRACT_LAST, preferred_element_type=F32)
            score_grad = (probs * (prob_grad - delta[h])).astype(BF16)
            value_sum = jnp.dot(probs.astype(BF16), grad, preferred_element_type=F32)
            key_sum = jnp.dot(score_grad, query, preferred_element_type=F32)
            if h:
                sums[0] += key_sum
                sums[1] += value_sum
            else:
                sums[0] = key_sum
                sums[1] = value_sum
            query_sum[at] += jnp.dot(flipped, score_grad, preferred_element_type=F32)
        parts[0, j] = sums[0].astype(BF16)
        parts[1, j] = sums[1].astype(BF16)
        return carry

    def deliver(some):
        for j in some:
            over[j].landed()

            def both(at, j=j):
                own[j, at] = (parts[y, j, at].astype(F32) + got[j, at].astype(F32)).astype(BF16)

            net.add(rows, both)
            offset = blocks - 1 - j
            if offset:
                net.send(own.at[j], out.at[offset], ((n - offset) % n, 0))
            else:
                net.keep(own.at[j], out.at[0])

    if net.sems is not None:
        query_sum[...] = jnp.zeros_like(query_sum)
    over, before = {}, ()
    for first in range(0, blocks, 3):
        some = range(first, min(first + 3, blocks))
        if net.sems is not None:
            lax.fori_loop(some.start, some.stop, block, 0)
        for j in some:
            over[j] = net.send(parts.at[back(y, 1, net.sizes["y"]), j], got.at[j], OTHER_Y)
        yield
        deliver(before)
        yield
        before = some
    if net.sems is not None:
        for h in range(heads):
            at = pl.ds(h * HD, HD)
            raw = query_sum[at].T
            turned = raw[:, : HD // 2]
            turned = turned * cosine[...] - pltpu.roll(turned, HD // 4, 1) * sine[...]
            query_out[:, at] = (
                jnp.concatenate([turned, raw[:, HD // 2 :]], axis=1) * HD ** (-0.5)
            ).astype(BF16)
    deliver(before)


def multiply(net, shape, transposed, loads, out, left_in, right_in, result, busy):
    sides, tall, width = shape
    for load in loads:
        load.landed()
    some, group = 256, 2
    for first in range(0, tall // some, group):
        last = min(first + group, tall // some)
        for copy in busy.get(first, ()):
            copy.landed()

        def tile(i, carry):
            at = pl.ds(pl.multiple_of(i * some, some), some)
            if transposed:
                result[:, at] = lax.dot_general(
                    left_in[...], right_in[at], CONTRACT_LAST, preferred_element_type=F32
                ).astype(BF16)
            else:
                product = lax.dot_general(
                    left_in[:, at], right_in[...], CONTRACT_FIRST, preferred_element_type=F32
                ).astype(BF16)
                for side in range(sides):
                    result[side, at] = product[:, side * width : (side + 1) * width]
            return carry

        if net.sems is not None:
            lax.fori_loop(first, last, tile, 0)
        at = pl.ds(first * some, (last - first) * some)
        if transposed:
            net.keep(result.at[:, at], out.at[:, at])
        else:
            busy[first] = [net.keep(result.at[i, at], out.at[i, at]) for i in range(sides)]
        yield


def sum_second(shape, net, *refs):
    arrays, (out, out_up, out_feed), scratch = refs[:7], refs[7:10], refs[10:]
    sums, inside, result, feed = scratch[:5], scratch[5:12], scratch[12], scratch[13]
    gate_grad, up_grad, gate, up, normed, hidden, down = inside
    loads = [net.keep(src, dst) for src, dst in zip(arrays, inside)]
    part, own = sums[:2]
    half = 0 if net.sems is None else out.shape[0]
    c, zs = net.me["c"], net.sizes["z"]

    def produce(t):
        for load in loads[:4]:
            load.landed()

        def rows_of(ref):
            return jnp.concatenate(
                [ref[pl.ds((i * zs + t) * half, half)] for i in range(net.sizes["c"])]
            )

        def tile(i, carry):
            at = pl.ds(pl.multiple_of(i * 256, 256), 256)
            both = lax.dot_general(
                rows_of(gate_grad), gate[at], CONTRACT_LAST, preferred_element_type=F32
            ) + lax.dot_general(
                rows_of(up_grad), up[at], CONTRACT_LAST, preferred_element_type=F32
            )
            first, second = both[:half].astype(BF16), both[half:].astype(BF16)
            own[t, :, at] = jnp.where(c == 0, first, second)
            part[t, :, at] = jnp.where(c == 0, second, first)
            return carry

        if net.sems is not None:
            lax.fori_loop(0, D // 256, tile, 0)

    def others():
        yield from multiply(net, shape, False, loads, out_up, normed, up_grad, result, {})
        yield from multiply(net, shape, True, (), out_feed, hidden, down, feed, {})

    line = sum_products(net, produce, out, *sums)
    next(line)
    together(net, (others(), 3), line)


def attention_back_sum_feed(shape, dims, net, *refs):
    inside, (all_pairs, branch, other, w_out, low, normed, feed, grad_gate) = refs[:6], refs[6:14]
    pairs_out, query_out, feed_out, grad_out, grad_query, gate_out = refs[14:20]
    scratch = refs[20:]
    branch_in, out_in, grads, parts, got, own, sums, pairs, query_sum = scratch[:9]
    low_in, normed_in, result = scratch[13:]
    me = (net.me["x"] * net.sizes["c"] + net.me["c"]) * net.sizes["z"] + net.me["z"]
    half, y = 0 if net.sems is None else branch.shape[0], net.me["y"]
    loads = [net.keep(w_out, out_in)]
    for src, i in ((branch, y), (other, back(y, 1, net.sizes["y"]))):
        at = pl.ds(pl.multiple_of(i * half, half or 1), half)
        loads.append(net.keep(src, branch_in.at[at]))
    loads += [
        net.keep(all_pairs.at[i, back(me, shape[0] - 1 - j, net.sizes["n"])], pairs.at[i, j])
        for j in range(shape[0])
        for i in range(2)
    ]
    later = [net.keep(low, low_in), net.keep(normed, normed_in)]
    scatter_columns(net, grad_gate, gate_out)

    def attention():
        yield
        yield from attention_back(
            net, shape, *inside, loads, pairs_out, query_out, *scratch[:9]
        )
        busy = {}
        yield from multiply(net, dims, False, later, grad_out, branch_in, low_in, result, busy)
        yield from multiply(net, dims, False, (), grad_query, normed_in, query_out, result, busy)

    line = sum_rows(net, feed, feed_out, *scratch[9:13])
    next(line)
    together(net, attention(), line)


def gains_to_owners(net, gains, gains_out):
    x, c, z, y = (net.me[a] for a in AXES)
    n = net.sizes["n"]
    me = (x * net.sizes["c"] + c) * net.sizes["z"] + z
    for offset in range(n):
        for dy in range(net.sizes["y"]):
            slot, piece = gains_out.at[y, me], gains.at[lax.rem(me + offset, n)]
            if offset == 0 and dy == 0:
                net.keep(piece, slot)
            else:
                net.send(piece, slot, (offset, dy))


def rms_forward(values, gain_row):
    inverse = lax.rsqrt(jnp.mean(values * values, axis=-1, keepdims=True) + EPSILON)
    return (values * inverse * gain_row, inverse)


def rms_backward(values, inverse, gain_row, incoming):
    scaled = incoming * gain_row
    gain_grad = jnp.sum(incoming * values * inverse, axis=0)
    value_grad = inverse * scaled - values * inverse * inverse * inverse * jnp.mean(
        scaled * values, axis=-1, keepdims=True
    )
    return (value_grad, gain_grad)


def rope_tables(positions):
    quarter = HD // 4
    freqs = jnp.exp(-math.log(10000.0) * jnp.arange(quarter, dtype=jnp.float32) * 2.0 / (HD // 2))
    angles = positions.astype(jnp.float32)[:, None] * freqs[None, :]
    return (jnp.cos(angles), jnp.sin(angles))


def rotate(values, cosine_table, sine_table):
    quarter = cosine_table.shape[1]
    lead_part = values[..., :quarter]
    pair_part = values[..., quarter : 2 * quarter]
    tail_part = values[..., 2 * quarter :]
    cos_wide = cosine_table[:, None, :]
    sin_wide = sine_table[:, None, :]
    return jnp.concatenate(
        [
            lead_part * cos_wide - pair_part * sin_wide,
            pair_part * cos_wide + lead_part * sin_wide,
            tail_part,
        ],
        axis=-1,
    )


def segment_of(index, doc_ends):
    return jnp.sum((doc_ends[None, :] <= index[:, None]).astype(jnp.int32), axis=1)


def adam_update(weight, moment_old, square_old, gradient, rate_step, decay_rate):
    moment_new = BETA_ONE * moment_old + (1.0 - BETA_ONE) * gradient
    square_new = BETA_TWO * square_old + (1.0 - BETA_TWO) * gradient * gradient
    corrected = moment_new / (1.0 - BETA_ONE**STEP)
    corrected_square = square_new / (1.0 - BETA_TWO**STEP)
    weight_new = weight - rate_step * (
        corrected / (jnp.sqrt(corrected_square) + ADAM_EPS) + decay_rate * weight
    )
    return (moment_new, square_new, weight_new)


def body(
    sizes,
    tokens,
    cotangent,
    doc_lengths,
    w_query,
    w_keyvalue,
    w_out,
    w_gate,
    w_up,
    w_down,
    norm_gains,
    first_query,
    first_keyvalue,
    first_out,
    first_gate,
    first_up,
    first_down,
    first_gains,
    second_query,
    second_keyvalue,
    second_out,
    second_gate,
    second_up,
    second_down,
    second_gains,
):
    masters = (w_query, w_keyvalue, w_out, w_gate, w_up, w_down, norm_gains)
    firsts = (first_query, first_keyvalue, first_out, first_gate, first_up, first_down, first_gains)
    seconds = (
        second_query,
        second_keyvalue,
        second_out,
        second_gate,
        second_up,
        second_down,
        second_gains,
    )
    x, c, z, y = (lax.axis_index(a) for a in AXES)
    X, C, Z, Y, N = (sizes[a] for a in (*AXES, "n"))
    F = C * Z
    rows_w = w_query.shape[0]
    columns = w_query.shape[1]
    rows = tokens.shape[0]
    half = rows // Y
    head_count = columns // HD
    mlp_columns = w_gate.shape[1]
    width = -(-mlp_columns // (F * 128)) * 128
    device = (x * C + c) * Z + z

    def pick(values, index):
        return lax.dynamic_index_in_dim(values, index, 0, keepdims=False)

    def after(value, *others):
        return lax.optimization_barrier((value, *others))[0]

    low_gains = jnp.pad(norm_gains.astype(BF16).astype(F32), ((0, 6), (0, 0)))
    pair_weight = lax.dynamic_slice_in_dim(w_keyvalue, y * HD, HD, 1).astype(BF16)
    square, oblong = (rows_w, columns), (rows_w, mlp_columns)
    padded = (rows_w, F * width)
    g_pair, g_gains, low_query, low_out, low_gate, low_up, low_down = exchange(
        functools.partial(gather_small, 5),
        [pair_weight, low_gains, w_query, w_out, w_gate, w_up, w_down],
        [((X, C, Z, rows_w, HD), BF16), ((X, C, Z, 8, rows_w), F32)]
        + [(square, BF16)] * 2
        + [(padded, BF16)] * 3,
        sizes,
        2,
        20,
        scratch=[(square, F32)] * 2
        + [(oblong, F32)] * 3
        + [(square, BF16)] * 2
        + [(padded, BF16)] * 3,
    )
    g_pair = g_pair.reshape(D, HD)
    gain_values = g_gains.reshape(N, 8, rows_w)[:, :2].transpose(1, 0, 2).reshape(2, D)
    start_row = device * rows
    query_index = start_row + jnp.arange(rows, dtype=jnp.int32)
    doc_ends = jnp.cumsum(doc_lengths.reshape(-1))
    query_segment = segment_of(query_index, doc_ends)
    cosine_table, sine_table = rope_tables(query_index % SEQ_LEN)
    reach = (WINDOW - 1) // rows + 1
    scale = HD ** (-0.5)
    residual_in = tokens.astype(F32)
    normed_first, inverse_first = rms_forward(residual_in, gain_values[0])
    normed_first = normed_first.astype(BF16)
    pair_raw = jnp.dot(normed_first, g_pair, preferred_element_type=F32)
    own_pair = jnp.where(
        y == 0, rotate(pair_raw[:, None], cosine_table, sine_table)[:, 0], pair_raw
    ).astype(BF16)

    own_pair = with_layout_constraint(own_pair, Layout((0, 1)))
    all_pairs = lax.all_gather(own_pair, ("y", "x", "c", "z"), axis=0, tiled=True)
    g_query, g_out, g_gate, down_block = exchange(
        functools.partial(gather_weights, width),
        [after(low_query, own_pair), low_out, low_gate, low_down],
        [((X, C, Z, rows_w, columns), BF16)] * 2
        + [((X, C, Z, rows_w, Y * width), BF16), ((C, Z, rows_w, width), BF16)],
        sizes,
        1,
        130,
    )
    g_query, g_out = g_query.reshape(D, columns), g_out.reshape(D, columns)
    g_gate = g_gate.reshape(D, Y * width)
    cotangent_half = pick(cotangent.reshape(Y, half, D), y)
    all_pairs = all_pairs.reshape(Y, N, rows, HD)
    key_index = start_row - reach * rows + jnp.arange((reach + 1) * rows, dtype=jnp.int32)
    key_segment = segment_of(key_index, doc_ends)
    allowed = (
        (query_segment[:, None] == key_segment[None, :])
        & (key_index[None, :] <= query_index[:, None])
        & (query_index[:, None] - key_index[None, :] < WINDOW)
        & (key_index[None, :] >= 0)
    )
    bias = jnp.where(allowed.T, 0.0, -jnp.inf).astype(BF16).reshape(reach + 1, rows, rows)
    cosine_wide = jnp.concatenate([cosine_table, cosine_table], axis=1)
    sine_wide = jnp.concatenate([-sine_table, sine_table], axis=1)
    tokens_half = pick(tokens.reshape(Y, half, D), y)
    query_rot, attended, attended_low, log_total, middle, normed_all, g_up = exchange(
        functools.partial(attention_forward, width, (reach + 1, head_count, rows)),
        [
            normed_first,
            cosine_wide,
            sine_wide,
            bias,
            tokens_half,
            gain_values[1:],
            g_query,
            g_out,
            all_pairs,
            low_up,
        ],
        [
            ((rows, columns), BF16),
            ((rows, columns), F32),
            ((rows, columns), BF16),
            ((head_count, 1, rows), F32),
            ((half, D), F32),
            ((C, Z, half, D), BF16),
            ((X, C, Z, rows_w, Y * width), BF16),
        ],
        sizes,
        3,
        90,
        scratch=[
            ((D, columns), BF16),
            ((D, columns), BF16),
            ((2, reach + 1, rows, HD), BF16),
            ((2, reach + 1, rows, rows), F32),
            ((half, D), BF16),
            ((half, D), BF16),
            ((half, D), BF16),
            ((reach + 1, HD, rows), BF16),
        ],
        in_vmem=range(5),
        arrays_in_vmem=range(6),
    )
    inverse_second = lax.rsqrt(jnp.mean(middle * middle, axis=-1, keepdims=True) + EPSILON)
    normed_all = normed_all.reshape(F * half, D)
    g_up = g_up.reshape(D, Y * width)
    wide, tall = (F * half, Y * width), (D, Y * width)
    down_grad, g_down, active, up_slope, hidden = exchange(
        functools.partial(mlp_forward, width),
        [cotangent_half.astype(BF16), down_block, normed_all, g_gate, g_up],
        [((C, Z, half, D), BF16), ((X, C, Z, rows_w, Y * width), BF16)]
        + [(wide, F32), (wide, F32), (wide, BF16)],
        sizes,
        4,
        50,
        scratch=[
            ((F * half, D), BF16),
            (tall, BF16),
            (tall, BF16),
            (wide, F32),
            (wide, F32),
            (wide, BF16),
        ],
    )
    down_grad = down_grad.reshape(F * half, D)
    g_down = g_down.reshape(D, Y * width)
    hidden_grad = jnp.dot(down_grad, g_down, preferred_element_type=F32)
    gate_grad = (hidden_grad * up_slope).astype(BF16)
    up_grad = (hidden_grad * active).astype(BF16)

    def weight_grad(left, right):
        sides = [
            lax.dot_general(
                left,
                right[:, i * width : (i + 1) * width],
                CONTRACT_FIRST,
                preferred_element_type=F32,
            ).astype(BF16)
            for i in range(Y)
        ]
        return jnp.stack(sides).reshape(Y * X, C, Z, rows_w, width)

    whole_down = weight_grad(down_grad, hidden)

    def over_y_x(whole_grad):
        return lax.psum_scatter(
            whole_grad, ("y", "x"), scatter_dimension=0, tiled=True
        ).reshape(F, rows_w, width)

    whole_gate = weight_grad(normed_all, gate_grad)
    part_down, part_gate = over_y_x(whole_down), over_y_x(whole_gate)
    second_grad, whole_up, feed_part = exchange(
        functools.partial(sum_second, (Y, D, width)),
        [after(gate_grad, whole_down, whole_gate), up_grad, g_gate, g_up, normed_all, hidden, g_down],
        [((half, D), F32), ((Y, D, width), BF16), ((F * half, D), BF16)],
        sizes,
        5,
        65,
        scratch=[((Z, half, D), BF16)] * 5
        + [(wide, BF16)] * 2
        + [(tall, BF16)] * 2
        + [((F * half, D), BF16), (wide, BF16), (tall, BF16)]
        + [((Y, D, width), BF16), ((F * half, D), BF16)],
        in_vmem=(0,),
    )
    part_up = over_y_x(whole_up.reshape(Y * X, C, Z, rows_w, width))

    def whole(own, other):
        return jnp.where(
            y == 0, jnp.concatenate([own, other]), jnp.concatenate([other, own])
        )

    middle_norm_grad, gain_two = rms_backward(middle, inverse_second, gain_values[1], second_grad)
    middle_grad = cotangent_half + middle_norm_grad
    branch_half = middle_grad.astype(BF16)
    branch_in, new_down = exchange(
        swap_rows_scatter,
        [branch_half, part_down.reshape(C, Z, rows_w, width)],
        [((half, D), BF16), ((rows_w, F * width), BF16)],
        sizes,
        7,
        35,
    )
    pair_parts, query_grad, feed_out, grad_out, grad_query, new_gate = exchange(
        functools.partial(
            attention_back_sum_feed, (reach + 1, head_count, rows), (1, D, columns)
        ),
        [
            query_rot,
            bias,
            log_total,
            attended,
            cosine_wide,
            sine_wide,
            all_pairs,
            branch_half,
            branch_in,
            g_out,
            attended_low,
            normed_first,
            feed_part.reshape(C, Z, half, D),
            part_gate.reshape(C, Z, rows_w, width),
        ],
        [
            ((reach + 1, rows, HD), BF16),
            ((rows, columns), BF16),
            ((half, D), F32),
            ((1, D, columns), BF16),
            ((1, D, columns), BF16),
            ((rows_w, F * width), BF16),
        ],
        sizes,
        8,
        95,
        scratch=[
            ((rows, D), BF16),
            ((D, columns), BF16),
            ((rows, columns), BF16),
            ((2, reach + 1, rows, HD), BF16),
            ((reach + 1, rows, HD), BF16),
            ((reach + 1, rows, HD), BF16),
            ((2, rows, HD), F32),
            ((2, reach + 1, rows, HD), BF16),
            ((columns, rows), F32),
        ]
        + [((Z, half, D), BF16)] * 4
        + [((rows, columns), BF16), ((rows, D), BF16), ((1, D, columns), BF16)],
        in_vmem=(1, 2),
        arrays_in_vmem=range(6),
    )
    mixed_half = middle + feed_out
    pair_total = jnp.sum(pair_parts.astype(F32), axis=0)
    pair_total = jnp.where(
        y == 0, rotate(pair_total[:, None], cosine_table, -sine_table)[:, 0], pair_total
    ).astype(BF16)
    first_part = (
        lax.dot_general(query_grad, g_query, CONTRACT_LAST, preferred_element_type=F32)
        + lax.dot_general(pair_total, g_pair, CONTRACT_LAST, preferred_element_type=F32)
    )
    gain_one = jnp.sum(first_part * residual_in * inverse_first, axis=0)
    first_part = first_part.astype(BF16)
    grad_gains = jnp.pad(
        jnp.stack([gain_one, gain_two]).reshape(2, N, rows_w).transpose(1, 0, 2),
        ((0, 0), (0, 6), (0, 0)),
    )
    grad_pair = lax.dot_general(
        normed_first, pair_total, CONTRACT_FIRST, preferred_element_type=F32
    ).astype(BF16)
    attention_grads = [
        g.reshape(X, C, Z, rows_w, -1) for g in (grad_query, grad_out, grad_pair)
    ]
    widths = (columns, columns, HD)
    (
        reduced_query,
        reduced_out,
        reduced_half,
        first_in,
        middle_in,
        mixed_in,
        gain_parts,
        half_in,
        new_up,
    ) = exchange(
        sum_weights,
        [
            *attention_grads,
            first_part,
            middle_grad,
            mixed_half,
            grad_gains,
            part_up.reshape(C, Z, rows_w, width),
        ],
        [((rows_w, w), F32) for w in widths]
        + [((rows, D), BF16), ((half, D), F32), ((half, D), F32), ((Y, N, 8, rows_w), F32)]
        + [((rows_w, HD), F32), ((rows_w, F * width), BF16)],
        sizes,
        9,
        110,
        scratch=[((X, Z, rows_w, w), BF16) for w in widths] * 2
        + [((X - 1, Z, rows_w, w), BF16) for w in widths]
        + [((Z - 1, rows_w, w), BF16) for w in widths],
        in_vmem=(0, 1, 2),
    )
    first_grad = first_part.astype(F32) + first_in.astype(F32)
    input_norm_grad, _ = rms_backward(residual_in, inverse_first, gain_values[0], first_grad)
    token_grad = whole(middle_grad, middle_in) + input_norm_grad
    mixed = whole(mixed_half, mixed_in)
    reduced_gains = jnp.sum(gain_parts, axis=(0, 1))[:2]
    reduced_mlp = [g[:, :mlp_columns].astype(F32) for g in (new_gate, new_up, new_down)]
    reduced_pair = jnp.where(
        y == 0,
        jnp.concatenate([reduced_half, half_in], axis=1),
        jnp.concatenate([half_in, reduced_half], axis=1),
    )
    reduced = (reduced_query, reduced_pair, reduced_out, *reduced_mlp, reduced_gains)
    dense_rate = 2.0 * D ** (-0.5)
    out_rate = 2.0 * max(1, H * HD // 64) ** (-0.5)
    rates = (dense_rate, dense_rate, out_rate, dense_rate, dense_rate, dense_rate, 0.4)
    decays = (DECAY, DECAY, DECAY, DECAY, DECAY, DECAY, 0.0)
    new_firsts = []
    new_seconds = []
    updated = []
    for weight, moment_old, square_old, gradient, rate_step, decay_rate in zip(
        masters, firsts, seconds, reduced, rates, decays
    ):
        moment_new, square_new, weight_new = adam_update(
            weight, moment_old, square_old, gradient, rate_step, decay_rate
        )
        new_firsts.append(moment_new)
        new_seconds.append(square_new)
        updated.append(weight_new)
    return (mixed, token_grad, *new_firsts, *new_seconds, *updated)


def solution(mesh):
    shape = dict(mesh.shape)
    sizes = {"x": shape["dp"] // 2, "c": 2, "z": shape["group"], "y": shape["tensor"]}
    sizes["n"] = sizes["x"] * sizes["c"] * sizes["z"]
    grid = Mesh(mesh.devices.reshape([sizes[a] for a in AXES]), AXES)
    blocks = ("x", "c", "z")
    by_rows, by_both, gains = P(blocks, None), P(blocks, "y"), P(None, blocks)
    weights = (by_both, by_rows, by_both, by_both, by_both, by_both, gains)
    return jax.shard_map(
        functools.partial(body, sizes),
        mesh=grid,
        in_specs=(by_rows, by_rows, P(), *weights * 3),
        out_specs=(by_rows, by_rows, *weights * 3),
        check_vma=False,
    )
```
